32 devices in a mesh: groups: 2 (over x), ctx: 8 (over z, y), chan: 2 (over core).
Axes of the slice: x: 2, y: 2, z: 4, core: 2. Of those that a mesh axis runs over, the one named last changes fastest.
Arguments:
- tokens: int32 [4, 512], P('groups', 'ctx'), parts along dimension 0, may hold values from 0 to 511
- embed_table: bfloat16 [512, 4096], replicated, may hold values from -8 to 8
- norm_gain: float32 [4096], replicated, may hold values from 0.1 to 1.9
- input_proj: bfloat16 [4096, 3, 2048], P('ctx', None, 'chan'), may hold values from -0.09375 to 0.09375
- short_filter: float32 [3, 128, 3], P(None, 'chan'), may hold values from -3.5 to 3.5
- pole_rate: float32 [128, 16], P('chan'), may hold values from 0.0005859375 to 0.2
- residue: float32 [128, 16], P('chan'), may hold values from -1.5 to 1.5
- skip_gain: float32 [2048], P('chan'), may hold values from -3 to 3
- output_proj: bfloat16 [2048, 4096], P('chan', 'ctx'), may hold values from -0.125 to 0.125
Outputs:
- block_out: bfloat16 [4, 512, 4096], P('groups', 'ctx', 'chan'), parts along dimension 0
The draws below stay inside these ranges and needn't reach their ends.
There are 2 independent parts, one for each index of `groups`. The reference program is written for one: setup_inputs(seed, part) draws one part's arguments, and reference() takes and returns one part's arrays. A program takes and returns all parts, laid end to end along the dimension named above; an argument that names none is the same for every part. Nothing has to cross between parts.
All inputs are finite; a program needn't handle non-finite values.
Results may differ from the reference program's by a relative error of at most 0.0078.
Values may be sent and summed in bfloat16 or wider, within the bound.
No kernel may reach another device: no remote copies, remote signals or barrier semaphores. Data moves between devices by JAX's collectives and lax.ppermute only.
A program may use at most 128 MiB of HBM per device.

```python
import math
import jax
import jax.numpy as jnp
from jax import lax

D = 4096
VOCAB = 512
HC = 2048
GS = 16
POLES = 16
KS = 3
GEN = 2
LEN = 512


def draw_embed_table(key, part):
    first_key, second_key, third_key = jax.random.split(key, 3)
    row_scale = 10.0 ** jax.random.uniform(first_key, (VOCAB, 1), jnp.float32)
    col_scale = 10.0 ** jax.random.uniform(second_key, (1, D), jnp.float32)
    values = jnp.clip(jax.random.normal(third_key, (VOCAB, D), jnp.float32), -4.0, 4.0)
    return (0.02 * values * row_scale * col_scale).astype(jnp.bfloat16)


def draw_pole_rate(key, part):
    first_key, second_key, third_key, fourth_key = jax.random.split(key, 4)
    shape = (HC // GS, POLES)
    slow_rate = jnp.exp(jax.random.uniform(first_key, shape, jnp.float32, math.log(0.3), math.log(2.0))) / LEN
    middle_rate = jnp.exp(jax.random.uniform(fourth_key, shape, jnp.float32, math.log(2.0) - math.log(LEN), math.log(0.02)))
    fast_rate = jnp.exp(jax.random.uniform(second_key, shape, jnp.float32, math.log(0.02), math.log(0.2)))
    slow_share = 0.5
    middle_share = 0.25
    picked = jax.random.uniform(third_key, shape, jnp.float32)
    rate = jnp.where(picked < slow_share, slow_rate, jnp.where(picked < slow_share + middle_share, middle_rate, fast_rate))
    return rate.astype(jnp.float32)


def with_ends(result, key, smallest, high):
    extent = result.shape
    spot = [jax.random.randint(jax.random.fold_in(key, axis), (), 0, extent[axis]) for axis in range(len(extent))]
    result = result.at[tuple(spot)].set(smallest)
    longest = extent.index(max(extent))
    spot[longest] = (spot[longest] + 1) % extent[longest]
    return result.at[tuple(spot)].set(high)


def block_levels(own_key, extent, shards, low, top_value):
    loudness, own = 1.0, jax.random.fold_in(own_key, 6)
    for axis_at, shards_of in shards:
        draws = jnp.exp(jax.random.uniform(jax.random.fold_in(own, axis_at), (shards_of,), jnp.float32, low / len(shards), top_value / len(shards)))
        loudness = loudness * jnp.repeat(draws, extent[axis_at] // shards_of).reshape([-1 if axis == axis_at else 1 for axis in range(len(extent))])
    return loudness


def centred(stream_key, extent, scale, reach, shards=(), dtype=jnp.bfloat16):
    array = jax.random.normal(stream_key, extent, jnp.float32) * scale
    if len(shards) > 0:
        array = block_levels(stream_key, extent, shards, -0.22, 0.18) * array
    return jnp.clip(array, min=-reach, max=reach).astype(dtype)


def setup_inputs(seed: int = 0, part: int = 0) -> dict:
    key_list = jax.random.split(jax.random.key(seed), 10)
    part_splits = jax.random.split(jax.random.fold_in(key_list[9], part), 10)
    return {
        "tokens": with_ends(jax.random.randint(part_splits[0], (GEN, LEN), 0, VOCAB), jax.random.fold_in(part_splits[0], 1), 0, VOCAB - 1).astype(jnp.int32),
        "embed_table": draw_embed_table(jax.random.fold_in(key_list[9], 71), part),
        "norm_gain": jnp.clip(1.0 + 0.18 * jax.random.normal(key_list[2], (D,), jnp.float32), 0.1, 1.9),
        "input_proj": centred(key_list[3], (D, 3, HC), D ** -0.5, 0.09375, ((0, 8), (2, 2))),
        "short_filter": centred(key_list[4], (3, HC // GS, KS), 0.6, 3.5, ((1, 2),), jnp.float32),
        "pole_rate": draw_pole_rate(jax.random.fold_in(key_list[9], 71), part),
        "residue": centred(key_list[6], (HC // GS, POLES), 0.25, 1.5, ((0, 2),), jnp.float32),
        "skip_gain": centred(key_list[7], (HC,), 0.5, 3.0, ((0, 2),), jnp.float32),
        "output_proj": centred(key_list[8], (HC, D), HC ** -0.5, 0.125, ((0, 2), (1, 8))),
    }


epsilon = 1e-06

def reference(tokens, embed_table, norm_gain, input_proj, short_filter, pole_rate, residue, skip_gain, output_proj):
    embedded = jnp.take(embed_table, tokens, axis=0)
    widened = embedded.astype(jnp.float32)
    inv_rms = lax.rsqrt(lax.optimization_barrier(jnp.mean(widened * widened, axis=-1, keepdims=True)) + epsilon)
    normed = (widened * inv_rms * norm_gain).astype(jnp.bfloat16)
    flat_rows = normed.reshape(GEN * LEN, D)
    summed = jnp.dot(flat_rows, input_proj.reshape(D, 3 * HC), preferred_element_type=jnp.float32)
    projected = summed.astype(jnp.bfloat16).reshape(GEN, LEN, 3, HC)
    widened_proj = projected.astype(jnp.float32)
    taps_full = jnp.repeat(short_filter, GS, axis=1)
    filtered = jnp.zeros((GEN, LEN, 3, HC), jnp.float32)
    for lag in range(KS):
        shifted = jnp.pad(widened_proj, ((0, 0), (lag, 0), (0, 0), (0, 0)))[:, :LEN]
        filtered = filtered + taps_full[:, :, lag] * shifted
    query_part = filtered[:, :, 0]
    product = filtered[:, :, 1] * filtered[:, :, 2]
    pole_decay = jnp.exp(-pole_rate)
    pole_amp = residue * jnp.sqrt(-jnp.expm1(-2.0 * pole_rate))
    decay_full = jnp.repeat(pole_decay, GS, axis=0)
    amp_full = jnp.repeat(pole_amp, GS, axis=0)

    def advance(carried, column):
        carried = decay_full * carried + column[:, :, None]
        return (carried, lax.optimization_barrier(jnp.sum(carried * amp_full, axis=-1)))
    start_state = jnp.zeros((GEN, HC, POLES), jnp.float32)
    final_state, history = lax.scan(advance, start_state, jnp.moveaxis(product, 1, 0))
    long_conv = jnp.moveaxis(history, 0, 1)
    gated = (query_part * (long_conv + skip_gain * product)).astype(jnp.bfloat16)
    mixed = jnp.dot(gated.reshape(GEN * LEN, HC), output_proj, preferred_element_type=jnp.float32)
    block_out = (widened.reshape(GEN * LEN, D) + mixed).astype(jnp.bfloat16)
    return block_out.reshape(GEN, LEN, D)
```

```python
import functools

import jax
import jax.numpy as jnp
from jax import lax
from jax.experimental import pallas as pl
from jax.experimental.pallas import tpu as pltpu
from jax.sharding import PartitionSpec as P

epsilon = 1e-06
highest = lax.Precision.HIGHEST
f32 = jnp.float32
bf16 = jnp.bfloat16
CHUNK = 128
LANES = 128
VMEM_LIMIT = 48 * 1024 * 1024


def passed_along(shard, axis, by):
    count = lax.axis_size(axis)
    pairs = [(i, i + by) for i in range(count) if 0 <= i + by < count]
    return lax.ppermute(shard, axis, pairs)


def entering(shard, axis, combine, identity):
    count, mine = (lax.axis_size(axis), lax.axis_index(axis))
    everything = jax.tree.map(lambda part: lax.all_gather(part, axis), shard)
    start = jax.tree.map(
        lambda part, zero: jnp.broadcast_to(jnp.asarray(zero, part.dtype), part.shape),
        shard,
        identity,
    )

    def hop(k, before):
        reached = k < mine
        new = combine(before, jax.tree.map(lambda part: part[k], everything))
        return jax.tree.map(lambda a, b: jnp.where(reached, a, b), new, before)

    return lax.fori_loop(0, count, hop, start)


def local_block(operands):
    rising, falling, inputs = operands
    length = rising.shape[2]
    toeplitz = jnp.einsum("gnt,gns->gts", rising, falling, precision=highest)
    causal = jnp.arange(length)[:, None] >= jnp.arange(length)[None, :]
    toeplitz = jnp.where(causal[None], toeplitz, 0.0)
    return jnp.einsum("gms,gts->gmt", inputs, toeplitz, precision=highest)


def lookup_rows(token_block, embed_table):
    vocab_count = embed_table.shape[0]
    onehot = (token_block[:, None] == jnp.arange(vocab_count, dtype=jnp.int32)[None, :]).astype(
        jnp.bfloat16
    )
    return jnp.dot(onehot, embed_table, preferred_element_type=jnp.float32)


def general_body(
    tokens,
    embed_table,
    norm_gain,
    input_proj,
    short_filter,
    pole_rate,
    residue,
    skip_gain,
    output_proj,
):
    genome_count, row_count = tokens.shape
    part_rows, branch_count, channels = input_proj.shape
    groups = pole_rate.shape[0]
    group_size = channels // groups
    tap_count = short_filter.shape[2]
    flat_count = genome_count * row_count
    flat_tokens = tokens.reshape(flat_count)
    widened = lookup_rows(flat_tokens, embed_table)
    inv_rms = lax.rsqrt(jnp.mean(widened * widened, axis=-1, keepdims=True) + epsilon)
    normed = (widened * inv_rms * norm_gain).astype(jnp.bfloat16)
    proj_cols = branch_count * channels
    flat_weight = input_proj.reshape(part_rows, proj_cols)
    spread = lax.all_to_all(normed, "ctx", split_axis=1, concat_axis=0, tiled=True)
    summed = lax.psum_scatter(
        jnp.dot(spread, flat_weight, preferred_element_type=jnp.float32),
        "ctx",
        scatter_dimension=0,
        tiled=True,
    )
    projected = summed.astype(jnp.bfloat16).reshape(genome_count, row_count, branch_count, channels)
    rim = passed_along(projected[:, row_count - (tap_count - 1) :], "ctx", 1)
    extended = jnp.concatenate([rim, projected], axis=1).astype(jnp.float32)
    taps_full = jnp.broadcast_to(
        short_filter[:, :, None, :], (branch_count, groups, group_size, tap_count)
    ).reshape(branch_count, channels, tap_count)
    filtered = jnp.zeros((genome_count, row_count, branch_count, channels), jnp.float32)
    for lag in range(tap_count):
        first_row = tap_count - 1 - lag
        filtered = filtered + taps_full[:, :, lag] * extended[:, first_row : first_row + row_count]
    query_part = filtered[:, :, 0]
    product = filtered[:, :, 1] * filtered[:, :, 2]
    mixes = genome_count * group_size
    grouped = (
        product.reshape(genome_count, row_count, groups, group_size)
        .transpose(2, 0, 3, 1)
        .reshape(groups, mixes, row_count)
    )
    positions = jnp.arange(row_count, dtype=jnp.float32)
    middle = float(row_count // 2)
    powers = jnp.exp(-pole_rate[:, :, None] * positions)
    next_powers = jnp.exp(-pole_rate[:, :, None] * (positions + 1.0))
    pole_amp = residue * jnp.sqrt(-jnp.expm1(-2.0 * pole_rate))
    rising = pole_amp[:, :, None] * jnp.exp(-pole_rate[:, :, None] * (positions - middle))
    falling = jnp.exp(-pole_rate[:, :, None] * (middle - positions))
    block_size = 8
    blocks = groups // block_size
    poles = pole_rate.shape[1]
    local_part = lax.map(
        local_block,
        (
            rising.reshape(blocks, block_size, poles, row_count),
            falling.reshape(blocks, block_size, poles, row_count),
            grouped.reshape(blocks, block_size, mixes, row_count),
        ),
    )
    local_part = local_part.reshape(groups, mixes, row_count)
    end_state = jnp.einsum("gms,gns->gmn", grouped, powers[:, :, ::-1], precision=highest)
    block_decay = jnp.exp(-pole_rate * row_count)

    def combine(earlier, later):
        return (earlier[0] * later[0], later[0][:, None, :] * earlier[1] + later[1])

    identity = (jnp.ones_like(block_decay), jnp.zeros_like(end_state))
    incoming = entering((block_decay, end_state), "ctx", combine, identity)[1]
    weighted = incoming * pole_amp[:, None, :]
    correction = jnp.einsum("gmn,gnt->gmt", weighted, next_powers, precision=highest)
    long_conv = (
        (local_part + correction)
        .reshape(groups, genome_count, group_size, row_count)
        .transpose(1, 3, 0, 2)
        .reshape(genome_count, row_count, channels)
    )
    gated = (
        (query_part * (long_conv + skip_gain * product))
        .astype(jnp.bfloat16)
        .reshape(flat_count, channels)
    )
    partial_value = jnp.dot(
        gated,
        lax.all_gather(output_proj, "ctx", axis=1, tiled=True),
        preferred_element_type=jnp.float32,
    )
    own_share = lax.psum_scatter(partial_value, "chan", scatter_dimension=1, tiled=True)
    half_width = own_share.shape[1]
    residual_part = lax.dynamic_slice_in_dim(
        widened, lax.axis_index("chan") * half_width, half_width, 1
    )
    block_out = (residual_part + own_share).astype(jnp.bfloat16)
    return block_out.reshape(genome_count, row_count, half_width)


def swapped(value, axis, mask):
    count = lax.axis_size(axis)
    return lax.ppermute(value, axis, [(i, i ^ mask) for i in range(count)])


def swapped_both(value, ctx_mask):
    count, cores = lax.axis_size("ctx"), lax.axis_size("chan")
    pairs = [
        (i * cores + c, (i ^ ctx_mask) * cores + (c ^ 1)) for i in range(count) for c in range(cores)
    ]
    return lax.ppermute(value, ("ctx", "chan"), pairs)


def split(value):
    high = value.astype(bf16)
    return high, (value - high.astype(f32)).astype(bf16)


def dot3(a_high, a_low, b):
    b_high, b_low = split(b)
    total = jnp.dot(a_high, b_high, preferred_element_type=f32)
    total += jnp.dot(a_low, b_high, preferred_element_type=f32)
    return total + jnp.dot(a_high, b_low, preferred_element_type=f32)


def lane_half(shape):
    return lax.broadcasted_iota(jnp.int32, shape, len(shape) - 1) < LANES // 2


def half_turn(value):
    return pltpu.roll(value, LANES // 2, value.ndim - 1)


def filter_kernel(rate_ref, rate_col_ref, amp_ref, high_ref, low_ref, ends_high_ref, ends_low_ref, fade_ref):
    square = (CHUNK, LANES)
    rate, amp = rate_ref[...], amp_ref[...]
    row = lax.broadcasted_iota(jnp.int32, square, 0)
    col = lax.broadcasted_iota(jnp.int32, square, 1)
    place = row.astype(f32)
    middle = float(CHUNK // 2)
    rising = amp * jnp.exp(-rate * (place - middle))
    falling = jnp.exp(-rate * (middle - place))
    poles = 16
    count = LANES // poles
    for g in range(count):
        own = jnp.where(col // poles == g, falling, 0.0)
        block = lax.dot_general(
            rising, own, (((1,), (1,)), ((), ())), precision=highest, preferred_element_type=f32
        )
        block = jnp.where(row >= col, block, 0.0)
        high, low = split(block)
        high_ref[:, g * CHUNK : (g + 1) * CHUNK] = high
        low_ref[:, g * CHUNK : (g + 1) * CHUNK] = low
    high, low = split(amp * jnp.exp(-rate * (place + 1.0)))
    high_ref[:, count * CHUNK :] = high
    low_ref[:, count * CHUNK :] = low
    rate_col = rate_col_ref[...]
    high, low = split(jnp.exp(-rate_col * (float(CHUNK - 1) - col.astype(f32))))
    ends_high_ref[...] = high
    ends_low_ref[...] = low
    fade_ref[...] = jnp.exp(-rate_col * float(CHUNK)) + jnp.zeros(square, f32)


def partial_kernel(place_ref, normed_ref, *refs):
    weight_refs, (keep_ref, send_ref) = refs[:-2], refs[-2:]
    quad, half = place_ref[0], place_ref[1]
    depth = weight_refs[0].shape[1]
    rows = normed_ref.shape[0]
    for j in range(weight_refs[0].shape[0]):
        total = jnp.zeros((rows, LANES), f32)
        for m, weight_ref in enumerate(weight_refs):
            first = pl.multiple_of((quad ^ m) * depth, depth)
            total += jnp.dot(
                normed_ref[:, pl.ds(first, depth)], weight_ref[j], preferred_element_type=f32
            )
        total = jnp.where(half == 0, total, half_turn(total))
        top, bottom = total[: rows // 2], total[rows // 2 :]
        left = lane_half(top.shape)
        keep_ref[j] = jnp.where(left, top, half_turn(bottom))
        send_ref[j] = jnp.where(left, half_turn(top), bottom).astype(bf16)


def conv_kernel(
    place_ref, token_ref, own_ref, other_ref, taps_ref, skip_ref, high_ref, low_ref, ends_high_ref, ends_low_ref, fade_ref, out_ref, *, genomes
):
    group = place_ref[2]
    branches, half_vocab, _ = own_ref.shape
    positions = token_ref.shape[0]
    length = positions // genomes
    vocab = lax.broadcasted_iota(jnp.int32, (positions, 2 * half_vocab), 1)
    picked = (token_ref[...] == vocab).astype(f32).astype(bf16)
    row = lax.broadcasted_iota(jnp.int32, (positions, LANES), 0) % length
    filtered = []
    for j in range(branches):
        mine, theirs = own_ref[j].astype(f32), other_ref[j].astype(f32)
        first = jnp.where(group == 0, mine, theirs)
        second = jnp.where(group == 0, theirs, mine)
        left = lane_half(first.shape)
        top = jnp.where(left, first, half_turn(second))
        bottom = jnp.where(left, half_turn(first), second)
        table = jnp.concatenate([top, bottom], axis=0).astype(bf16)
        now = jnp.dot(picked, table, preferred_element_type=f32)
        total = taps_ref[3 * j : 3 * j + 1] * now
        for lag in (1, 2):
            late = jnp.where(row >= lag, pltpu.roll(now, lag, 0), 0.0)
            total += taps_ref[3 * j + lag : 3 * j + lag + 1] * late
        filtered.append(total)
    query = filtered[0]
    product = filtered[1] * filtered[2]
    size = 16
    count = LANES // size
    width = genomes * LANES
    lane = lax.broadcasted_iota(jnp.int32, (CHUNK, width), 1) % LANES
    pole_row = lax.broadcasted_iota(jnp.int32, (LANES, width), 0)
    same = pole_row // size == (lax.broadcasted_iota(jnp.int32, (LANES, width), 1) % LANES) // size
    fade = jnp.concatenate([fade_ref[...]] * genomes, axis=1)
    state = jnp.zeros((LANES, width), f32)
    chunks = length // CHUNK
    for c in range(chunks):
        spans = [slice(b * length + c * CHUNK, b * length + (c + 1) * CHUNK) for b in range(genomes)]
        block = jnp.concatenate([product[span] for span in spans], axis=1)
        stacked = jnp.concatenate(
            [jnp.where(lane // size == g, block, 0.0) for g in range(count)] + [state], axis=0
        )
        conv = dot3(high_ref[...], low_ref[...], stacked)
        for b, span in enumerate(spans):
            value = conv[:, b * LANES : (b + 1) * LANES] + skip_ref[...] * product[span]
            out_ref[span, :] = (query[span] * value).astype(bf16)
        if c < chunks - 1:
            ends = dot3(ends_high_ref[...], ends_low_ref[...], block)
            state = fade * state + jnp.where(same, ends, 0.0)


def output_kernel(place_ref, token_ref, rows_ref, far_rows_ref, *refs):
    piece_refs, (near_own, near_far, core_own, core_far, out_ref) = refs[:4], refs[4:]
    quad, half, core = place_ref[0], place_ref[1], place_ref[3]
    count = token_ref.shape[0]
    vocab = lax.broadcasted_iota(jnp.int32, (count, rows_ref.shape[0]), 1)
    picked = (token_ref[...] == vocab).astype(f32).astype(bf16)
    block = 2 * LANES
    joined = []
    for piece_ref in piece_refs:
        pair = []
        for other_core in (0, 1):
            near = piece_ref[other_core].astype(f32)
            far = piece_ref[2 + other_core].astype(f32)
            first = jnp.where(half == 0, near, far)
            second = jnp.where(half == 0, far, near)
            left = lane_half(first.shape)
            pair.append(
                jnp.concatenate(
                    [
                        jnp.where(left, first, half_turn(second)),
                        jnp.where(left, half_turn(first), second),
                    ],
                    axis=1,
                ).astype(bf16)
            )
        joined.append(pair)
    for far, (table_ref, weights) in enumerate(
        ((rows_ref, (near_own, core_own)), (far_rows_ref, (near_far, core_far)))
    ):
        total = jnp.dot(picked, table_ref[...], preferred_element_type=f32)
        mixed = jnp.zeros(total.shape, f32)
        for m in range(4):
            first = pl.multiple_of((quad ^ m) * block, block)
            for other_core in (0, 1):
                mixed += jnp.dot(
                    joined[m][other_core],
                    weights[other_core][pl.ds(first, block), :],
                    preferred_element_type=f32,
                )
        out_ref[half ^ far ^ core] = (total + mixed).astype(bf16)


def place_kernel(place_ref, *refs):
    piece_refs, out_ref = refs[:4], refs[4]
    quad, core = place_ref[0], place_ref[3]
    width = piece_refs[0].shape[2]
    for m, piece_ref in enumerate(piece_refs):
        first = pl.multiple_of((quad ^ m) * width, width)
        for g in (0, 1):
            out_ref[core ^ g, :, pl.ds(first, width)] = piece_ref[g]


def called(kernel, out_shape, scalars, *operands, flops=0, moved=0):
    smem = pl.BlockSpec(memory_space=pltpu.SMEM)
    vmem = pl.BlockSpec(memory_space=pltpu.VMEM)
    many = isinstance(out_shape, (list, tuple))
    return pl.pallas_call(
        kernel,
        out_shape=out_shape,
        in_specs=[smem] * len(scalars) + [vmem] * len(operands),
        out_specs=[vmem] * len(out_shape) if many else vmem,
        compiler_params=pltpu.CompilerParams(vmem_limit_bytes=VMEM_LIMIT),
        cost_estimate=pl.CostEstimate(flops=flops, bytes_accessed=moved, transcendentals=0),
    )(*scalars, *operands)


def shaped(*shape, dtype=f32):
    return jax.ShapeDtypeStruct(shape, dtype)


def quad_body(
    tokens,
    embed_table,
    norm_gain,
    input_proj,
    short_filter,
    pole_rate,
    residue,
    skip_gain,
    output_proj,
):
    genomes, rows = tokens.shape
    depth, branches, channels = input_proj.shape
    vocab, features = embed_table.shape
    tap_count = short_filter.shape[2]
    poles = pole_rate.shape[1]
    members = lax.axis_size("ctx") // 2
    ctx, core, group = (lax.axis_index(name) for name in ("ctx", "chan", "groups"))
    quad, half = ctx % members, ctx // members
    place = jnp.stack([quad, half, group, core]).astype(jnp.int32)
    block = channels // members

    weights = input_proj.transpose(1, 0, 2)

    def columns(member):
        return lax.dynamic_slice_in_dim(weights, member * block + group * LANES, LANES, 2)

    gathered = [columns(quad)] + [swapped(columns(quad ^ m), "ctx", m) for m in range(1, members)]

    near = jnp.concatenate([tokens, swapped(tokens, "ctx", members)], axis=0)
    all_tokens = [near] + [swapped(near, "ctx", m) for m in range(1, members)]
    stacked = jnp.stack(all_tokens).reshape(members, 2, genomes, rows)
    order = jnp.arange(members) ^ quad
    stacked = stacked[order][:, jnp.arange(2) ^ half]
    group_tokens = stacked.transpose(2, 1, 0, 3).reshape(genomes, 2 * members * rows)
    length = group_tokens.shape[1]

    widened = embed_table.astype(f32)
    inv_rms = lax.rsqrt(jnp.mean(widened * widened, axis=-1, keepdims=True) + epsilon)
    part = features // 2
    own_half = lax.dynamic_slice_in_dim(embed_table, half * part, part, 1).astype(f32)
    own_gain = lax.dynamic_slice_in_dim(norm_gain, half * part, part, 0)
    normed = (own_half * inv_rms * own_gain).astype(bf16)

    def own_rows(array, axis):
        per = array.shape[axis] // (members * 4)
        first = quad * 4 * per + half * per
        return jnp.concatenate(
            [lax.dynamic_slice_in_dim(array, first + i * 2 * per, per, axis) for i in (0, 1)], axis
        )

    own_rate, own_residue = own_rows(pole_rate, 0), own_rows(residue, 0)
    own_amp = own_residue * jnp.sqrt(-jnp.expm1(-2.0 * own_rate))
    own_skip = own_rows(skip_gain, 0).reshape(1, LANES)
    own_taps = jnp.repeat(own_rows(short_filter, 1).transpose(0, 2, 1), LANES // own_rate.shape[0], axis=2)
    own_taps = own_taps.reshape(branches * tap_count, LANES)
    filters = called(
        filter_kernel,
        [
            shaped(CHUNK, 9 * CHUNK, dtype=bf16),
            shaped(CHUNK, 9 * CHUNK, dtype=bf16),
            shaped(LANES, CHUNK, dtype=bf16),
            shaped(LANES, CHUNK, dtype=bf16),
            shaped(LANES, LANES),
        ],
        (),
        own_rate.reshape(1, LANES),
        own_rate.reshape(LANES, 1),
        own_amp.reshape(1, LANES),
    )

    keep, send = called(
        partial_kernel,
        [shaped(branches, vocab // 2, LANES), shaped(branches, vocab // 2, LANES, dtype=bf16)],
        (place,),
        normed,
        *gathered,
        flops=2 * vocab * part * branches * LANES,
        moved=4 << 20,
    )
    summed = (keep + swapped(send, "ctx", members).astype(f32)).astype(bf16)
    other = swapped(summed, "groups", 1)

    gated = called(
        functools.partial(conv_kernel, genomes=genomes),
        shaped(genomes * length, LANES, dtype=bf16),
        (place,),
        group_tokens.reshape(genomes * length, 1),
        summed,
        other,
        own_taps,
        own_skip,
        *filters,
    ).reshape(genomes, 2, length // 2, LANES)

    def span(genome, part_index):
        return lax.dynamic_slice(
            gated, (genome, part_index, 0, 0), (1, 1, length // 2, LANES)
        ).reshape(length // 2, LANES)

    piece = jnp.stack(
        [
            span(core, half),
            swapped(span(core ^ 1, half), "chan", 1),
            swapped(span(core, half ^ 1), "ctx", members),
            swapped_both(span(core ^ 1, half ^ 1), members),
        ]
    )
    pieces = [piece] + [swapped(piece, "ctx", m) for m in range(1, members)]

    half_rows = output_proj.shape[0] // 2
    fetched = swapped(
        lax.dynamic_slice_in_dim(output_proj, group * half_rows, half_rows, 0), "ctx", members
    )
    shared = swapped(fetched, "groups", 1)
    far_proj = jnp.where(
        group == 0,
        jnp.concatenate([fetched, shared], axis=0),
        jnp.concatenate([shared, fetched], axis=0),
    )
    core_own = swapped(output_proj, "chan", 1)
    core_far = swapped(far_proj, "chan", 1)

    width = output_proj.shape[1]
    own_tokens = lax.dynamic_slice(
        group_tokens, (core, half * (length // 2)), (1, length // 2)
    ).reshape(length // 2, 1)
    results = called(
        output_kernel,
        shaped(2, length // 2, width, dtype=bf16),
        (place,),
        own_tokens,
        lax.dynamic_slice_in_dim(embed_table, ctx * width, width, 1),
        lax.dynamic_slice_in_dim(embed_table, (ctx ^ members) * width, width, 1),
        *pieces,
        output_proj,
        far_proj,
        core_own,
        core_far,
    )
    both = jnp.stack([results[0], swapped(results[1], "chan", 1)])

    def rows_of(member):
        return lax.dynamic_slice_in_dim(both, member * rows, rows, 1)

    arrived = [rows_of(quad)] + [swapped(rows_of(quad ^ m), "ctx", m) for m in range(1, members)]
    return called(
        place_kernel, shaped(genomes, rows, members * width, dtype=bf16), (place,), *arrived
    )


def solution(mesh):
    sizes = tuple(mesh.shape[name] for name in ("groups", "ctx", "chan"))
    return jax.shard_map(
        quad_body if sizes == (2, 8, 2) else general_body,
        mesh=mesh,
        in_specs=(
            P("groups", "ctx"),
            P(),
            P(),
            P("ctx", None, "chan"),
            P(None, "chan", None),
            P("chan", None),
            P("chan", None),
            P("chan"),
            P("chan", "ctx"),
        ),
        out_specs=P("groups", "ctx", "chan"),
        check_vma=False,
    )
```

```python
import functools

import jax
import jax.numpy as jnp
from jax import lax
from jax.experimental import pallas as pl
from jax.experimental.pallas import tpu as pltpu
from jax.sharding import PartitionSpec as P

epsilon = 1e-06
highest = lax.Precision.HIGHEST
f32 = jnp.float32
bf16 = jnp.bfloat16
CHUNK = 128
LANES = 128
MIB = 1024 * 1024
SPARE = 16


def passed_along(shard, axis, by):
    count = lax.axis_size(axis)
    pairs = [(i, i + by) for i in range(count) if 0 <= i + by < count]
    return lax.ppermute(shard, axis, pairs)


def entering(shard, axis, combine, identity):
    count, mine = (lax.axis_size(axis), lax.axis_index(axis))
    everything = jax.tree.map(lambda part: lax.all_gather(part, axis), shard)
    start = jax.tree.map(
        lambda part, zero: jnp.broadcast_to(jnp.asarray(zero, part.dtype), part.shape),
        shard,
        identity,
    )

    def hop(k, before):
        reached = k < mine
        new = combine(before, jax.tree.map(lambda part: part[k], everything))
        return jax.tree.map(lambda a, b: jnp.where(reached, a, b), new, before)

    return lax.fori_loop(0, count, hop, start)


def local_block(operands):
    rising, falling, inputs = operands
    length = rising.shape[2]
    toeplitz = jnp.einsum("gnt,gns->gts", rising, falling, precision=highest)
    causal = jnp.arange(length)[:, None] >= jnp.arange(length)[None, :]
    toeplitz = jnp.where(causal[None], toeplitz, 0.0)
    return jnp.einsum("gms,gts->gmt", inputs, toeplitz, precision=highest)


def lookup_rows(token_block, embed_table):
    vocab_count = embed_table.shape[0]
    onehot = (token_block[:, None] == jnp.arange(vocab_count, dtype=jnp.int32)[None, :]).astype(
        jnp.bfloat16
    )
    return jnp.dot(onehot, embed_table, preferred_element_type=jnp.float32)


def general_body(
    tokens,
    embed_table,
    norm_gain,
    input_proj,
    short_filter,
    pole_rate,
    residue,
    skip_gain,
    output_proj,
):
    genome_count, row_count = tokens.shape
    part_rows, branch_count, channels = input_proj.shape
    groups = pole_rate.shape[0]
    group_size = channels // groups
    tap_count = short_filter.shape[2]
    flat_count = genome_count * row_count
    flat_tokens = tokens.reshape(flat_count)
    widened = lookup_rows(flat_tokens, embed_table)
    inv_rms = lax.rsqrt(jnp.mean(widened * widened, axis=-1, keepdims=True) + epsilon)
    normed = (widened * inv_rms * norm_gain).astype(jnp.bfloat16)
    proj_cols = branch_count * channels
    flat_weight = input_proj.reshape(part_rows, proj_cols)
    spread = lax.all_to_all(normed, "ctx", split_axis=1, concat_axis=0, tiled=True)
    summed = lax.psum_scatter(
        jnp.dot(spread, flat_weight, preferred_element_type=jnp.float32),
        "ctx",
        scatter_dimension=0,
        tiled=True,
    )
    projected = summed.astype(jnp.bfloat16).reshape(genome_count, row_count, branch_count, channels)
    rim = passed_along(projected[:, row_count - (tap_count - 1) :], "ctx", 1)
    extended = jnp.concatenate([rim, projected], axis=1).astype(jnp.float32)
    taps_full = jnp.broadcast_to(
        short_filter[:, :, None, :], (branch_count, groups, group_size, tap_count)
    ).reshape(branch_count, channels, tap_count)
    filtered = jnp.zeros((genome_count, row_count, branch_count, channels), jnp.float32)
    for lag in range(tap_count):
        first_row = tap_count - 1 - lag
        filtered = filtered + taps_full[:, :, lag] * extended[:, first_row : first_row + row_count]
    query_part = filtered[:, :, 0]
    product = filtered[:, :, 1] * filtered[:, :, 2]
    mixes = genome_count * group_size
    grouped = (
        product.reshape(genome_count, row_count, groups, group_size)
        .transpose(2, 0, 3, 1)
        .reshape(groups, mixes, row_count)
    )
    positions = jnp.arange(row_count, dtype=jnp.float32)
    middle = float(row_count // 2)
    powers = jnp.exp(-pole_rate[:, :, None] * positions)
    next_powers = jnp.exp(-pole_rate[:, :, None] * (positions + 1.0))
    pole_amp = residue * jnp.sqrt(-jnp.expm1(-2.0 * pole_rate))
    rising = pole_amp[:, :, None] * jnp.exp(-pole_rate[:, :, None] * (positions - middle))
    falling = jnp.exp(-pole_rate[:, :, None] * (middle - positions))
    block_size = 8
    blocks = groups // block_size
    poles = pole_rate.shape[1]
    local_part = lax.map(
        local_block,
        (
            rising.reshape(blocks, block_size, poles, row_count),
            falling.reshape(blocks, block_size, poles, row_count),
            grouped.reshape(blocks, block_size, mixes, row_count),
        ),
    )
    local_part = local_part.reshape(groups, mixes, row_count)
    end_state = jnp.einsum("gms,gns->gmn", grouped, powers[:, :, ::-1], precision=highest)
    block_decay = jnp.exp(-pole_rate * row_count)

    def combine(earlier, later):
        return (earlier[0] * later[0], later[0][:, None, :] * earlier[1] + later[1])

    identity = (jnp.ones_like(block_decay), jnp.zeros_like(end_state))
    incoming = entering((block_decay, end_state), "ctx", combine, identity)[1]
    weighted = incoming * pole_amp[:, None, :]
    correction = jnp.einsum("gmn,gnt->gmt", weighted, next_powers, precision=highest)
    long_conv = (
        (local_part + correction)
        .reshape(groups, genome_count, group_size, row_count)
        .transpose(1, 3, 0, 2)
        .reshape(genome_count, row_count, channels)
    )
    gated = (
        (query_part * (long_conv + skip_gain * product))
        .astype(jnp.bfloat16)
        .reshape(flat_count, channels)
    )
    partial_value = jnp.dot(
        gated,
        lax.all_gather(output_proj, "ctx", axis=1, tiled=True),
        preferred_element_type=jnp.float32,
    )
    own_share = lax.psum_scatter(partial_value, "chan", scatter_dimension=1, tiled=True)
    half_width = own_share.shape[1]
    residual_part = lax.dynamic_slice_in_dim(
        widened, lax.axis_index("chan") * half_width, half_width, 1
    )
    block_out = (residual_part + own_share).astype(jnp.bfloat16)
    return block_out.reshape(genome_count, row_count, half_width)


def swapped(value, axis, mask):
    count = lax.axis_size(axis)
    return lax.ppermute(value, axis, [(i, i ^ mask) for i in range(count)])


def swapped_both(value, ctx_mask):
    count, cores = lax.axis_size("ctx"), lax.axis_size("chan")
    pairs = [
        (i * cores + c, (i ^ ctx_mask) * cores + (c ^ 1)) for i in range(count) for c in range(cores)
    ]
    return lax.ppermute(value, ("ctx", "chan"), pairs)


def split(value):
    high = value.astype(bf16)
    return high, (value - high.astype(f32)).astype(bf16)


def dot3(a_high, a_low, b):
    b_high, b_low = split(b)
    total = jnp.dot(a_high, b_high, preferred_element_type=f32)
    total += jnp.dot(a_low, b_high, preferred_element_type=f32)
    return total + jnp.dot(a_high, b_low, preferred_element_type=f32)


def lane_half(shape):
    return lax.broadcasted_iota(jnp.int32, shape, len(shape) - 1) < LANES // 2


def half_turn(value):
    return pltpu.roll(value, LANES // 2, value.ndim - 1)


def norm_kernel(place_ref, table_ref, gain_ref, part_ref, packed_ref, out_ref):
    del place_ref, packed_ref
    widened = table_ref[...].astype(f32)
    mean = jnp.sum(widened * widened, axis=1, keepdims=True) / widened.shape[1]
    own = part_ref[...].astype(f32)
    out_ref[...] = (own * lax.rsqrt(mean + epsilon) * gain_ref[...]).astype(bf16)


def pack_kernel(place_ref, token_ref, weight_ref, *refs):
    out_refs, sems = refs[:-1], refs[-1]
    quad, group = place_ref[0], place_ref[2]
    branches, depth, channels = weight_ref.shape
    members = len(out_refs)
    block = channels // members
    copies = []
    for m in (1, 2, 3, 0):
        first = pl.multiple_of((quad ^ m) * block + group * LANES, LANES)
        for j in range(branches):
            copies.append(
                pltpu.make_async_copy(
                    weight_ref.at[j, :, pl.ds(first, LANES)],
                    out_refs[m].at[pl.ds(j * depth, depth), :],
                    sems.at[m, j],
                )
            )
            copies[-1].start()
    rows = token_ref.shape[1]
    row = lax.broadcasted_iota(jnp.int32, (SPARE, rows), 0)
    token = jnp.where(row % 4 < 2, token_ref[0:1, :], token_ref[1:2, :])
    token = jnp.where(row % 2 == 0, token >> 8, token & 255)
    token = jnp.where(row // 4 == quad, token, 0).astype(f32).astype(bf16)
    for out_ref in out_refs:
        out_ref[branches * depth :, :] = jnp.zeros((SPARE, LANES), bf16)
        out_ref[branches * depth :, :rows] = token
    for copy in copies:
        copy.wait()


def pick(half, near_ref, far_ref, picked_ref, genomes, rows):
    vocab = picked_ref.shape[1]
    length = picked_ref.shape[0] // genomes
    first = near_ref.shape[0] - SPARE
    diagonal = lax.broadcasted_iota(jnp.int32, (rows, rows), 0) == lax.broadcasted_iota(
        jnp.int32, (rows, rows), 1
    )
    entries = lax.broadcasted_iota(jnp.int32, (rows, vocab), 1).astype(f32)
    for other, ref in enumerate((near_ref, far_ref)):
        parts = ref[first:, :rows].astype(f32)
        for member in range(length // (2 * rows)):
            for b in range(genomes):
                at = 4 * member + 2 * b
                line = parts[at : at + 1] * 256.0 + parts[at + 1 : at + 2]
                column = jnp.sum(jnp.where(diagonal, line, 0.0), axis=1, keepdims=True)
                place = b * length + (half ^ other) * (length // 2) + member * rows
                picked_ref[pl.ds(pl.multiple_of(place, rows), rows), :] = (
                    (column == entries).astype(f32).astype(bf16)
                )


def prepare_kernel(place_ref, rate_ref, amp_ref, taps_ref, skip_ref, matrices_ref, rows_ref):
    quad, half = place_ref[0], place_ref[1]

    group_count = rate_ref.shape[1]
    poles = rate_ref.shape[0]
    count = LANES // poles

    def group_at(lane):
        place = lane // poles
        return quad * (2 * count) + (place // (count // 2)) * count + half * (count // 2) + place % (count // 2)

    lane = lax.broadcasted_iota(jnp.int32, (group_count, LANES), 1)
    chosen = (lax.broadcasted_iota(jnp.int32, (group_count, LANES), 0) == group_at(lane)).astype(f32)
    turned_lane = lax.broadcasted_iota(jnp.int32, (LANES, group_count), 0)
    turned = (lax.broadcasted_iota(jnp.int32, (LANES, group_count), 1) == group_at(turned_lane)).astype(f32)

    def along_lanes(ref):
        spread = jnp.dot(ref[...], chosen, precision=highest, preferred_element_type=f32)
        keep = lax.broadcasted_iota(jnp.int32, spread.shape, 0) == lax.broadcasted_iota(
            jnp.int32, spread.shape, 1
        ) % poles
        return jnp.sum(jnp.where(keep, spread, 0.0), axis=0, keepdims=True)

    rate, amp = along_lanes(rate_ref), along_lanes(amp_ref)
    spread = lax.dot_general(
        turned, rate_ref[...], (((1,), (1,)), ((), ())), precision=highest, preferred_element_type=f32
    )
    keep = lax.broadcasted_iota(jnp.int32, spread.shape, 1) == lax.broadcasted_iota(
        jnp.int32, spread.shape, 0
    ) % poles
    rate_col = jnp.sum(jnp.where(keep, spread, 0.0), axis=1, keepdims=True)

    square = (CHUNK, LANES)
    row = lax.broadcasted_iota(jnp.int32, square, 0)
    col = lax.broadcasted_iota(jnp.int32, square, 1)
    at = row.astype(f32)
    middle = float(CHUNK // 2)
    rising = amp * jnp.exp(-rate * (at - middle))
    falling = jnp.exp(-rate * (middle - at))
    width = (count + 1) * CHUNK
    for g in range(count):
        own = jnp.where(col // poles == g, falling, 0.0)
        block = lax.dot_general(
            rising, own, (((1,), (1,)), ((), ())), precision=highest, preferred_element_type=f32
        )
        high, low = split(jnp.where(row >= col, block, 0.0))
        matrices_ref[:, g * CHUNK : (g + 1) * CHUNK] = high
        matrices_ref[:, width + g * CHUNK : width + (g + 1) * CHUNK] = low
    high, low = split(amp * jnp.exp(-rate * (at + 1.0)))
    matrices_ref[:, count * CHUNK : width] = high
    matrices_ref[:, width + count * CHUNK : 2 * width] = low
    high, low = split(jnp.exp(-rate_col * (float(CHUNK - 1) - col.astype(f32))))
    matrices_ref[:, 2 * width : 2 * width + CHUNK] = high
    matrices_ref[:, 2 * width + CHUNK :] = low

    rows_ref[:LANES] = jnp.exp(-rate_col * float(CHUNK)) + jnp.zeros(square, f32)
    branches = taps_ref.shape[0]
    for j in range(branches):
        taps = jnp.dot(taps_ref[j], chosen, precision=highest, preferred_element_type=f32)
        rows_ref[LANES + 8 * j : LANES + 8 * j + taps.shape[0]] = taps
    upper = skip_ref[pl.ds(2 * quad, 1), :]
    lower = skip_ref[pl.ds(2 * quad + 1, 1), :]
    upper = jnp.where(half == 0, upper, half_turn(upper))
    lower = jnp.where(half == 1, lower, half_turn(lower))
    end = LANES + 8 * branches
    rows_ref[end : end + 1] = jnp.where(lane_half(upper.shape), upper, lower)


def partial_kernel(place_ref, normed_ref, *refs):
    weight_refs, (keep_ref, send_ref) = refs[:-2], refs[-2:]
    quad, half = place_ref[0], place_ref[1]
    rows, features = normed_ref.shape
    depth = features // len(weight_refs)
    count = weight_refs[0].shape[0] // depth
    total = jnp.zeros((rows, count * LANES), f32)
    tokens = jnp.zeros((SPARE, LANES), f32)
    for m, weight_ref in enumerate(weight_refs):
        first = pl.multiple_of((quad ^ m) * depth, depth)
        columns = jnp.concatenate(
            [weight_ref[j * depth : (j + 1) * depth, :] for j in range(count)], axis=1
        )
        total += jnp.dot(
            normed_ref[:, pl.ds(first, depth)], columns, preferred_element_type=f32
        )
        tokens += weight_ref[count * depth :, :].astype(f32)
    part = rows // 2
    for j in range(count):
        mine = total[:, j * LANES : (j + 1) * LANES]
        mine = jnp.where(half == 0, mine, half_turn(mine))
        top, bottom = mine[:part], mine[part:]
        left = lane_half(top.shape)
        keep_ref[j * part : (j + 1) * part, :] = jnp.where(left, top, half_turn(bottom))
        send_ref[j * part : (j + 1) * part, :] = jnp.where(left, half_turn(top), bottom).astype(bf16)
    send_ref[count * part :, :] = tokens.astype(bf16)


def filtered_branch(group, picked, row, mine, theirs, rows_ref, branch):
    mine, theirs = mine.astype(f32), theirs.astype(f32)
    first = jnp.where(group == 0, mine, theirs)
    second = jnp.where(group == 0, theirs, mine)
    left = lane_half(first.shape)
    top = jnp.where(left, first, half_turn(second))
    bottom = jnp.where(left, half_turn(first), second)
    table = jnp.concatenate([top, bottom], axis=0).astype(bf16)
    now = jnp.dot(picked, table, preferred_element_type=f32)
    first_tap = LANES + 8 * branch
    total = rows_ref[first_tap : first_tap + 1] * now
    for lag in range(1, 3):
        late = jnp.where(row >= lag, pltpu.roll(now, lag, 0), 0.0)
        total += rows_ref[first_tap + lag : first_tap + lag + 1] * late
    return total


def conv_kernel(
    place_ref, near_ref, far_ref, own_ref, other_ref, matrices_ref, rows_ref, *refs, genomes, rows
):
    piece_refs, (mine_ref, picked_ref, held_ref) = refs[:4], refs[4:]
    half, group, core = place_ref[1], place_ref[2], place_ref[3]
    pick(half, near_ref, far_ref, picked_ref, genomes, rows)
    positions = picked_ref.shape[0]
    length = positions // genomes
    row = lax.broadcasted_iota(jnp.int32, (positions, LANES), 0) % length
    picked = picked_ref[...]
    query, key, value = (
        filtered_branch(group, picked, row, own_ref[j], other_ref[j], rows_ref, j) for j in range(3)
    )
    product = key * value
    size = 16
    count = LANES // size
    width = genomes * LANES
    lane = lax.broadcasted_iota(jnp.int32, (CHUNK, width), 1) % LANES
    pole_row = lax.broadcasted_iota(jnp.int32, (LANES, width), 0)
    same = pole_row // size == (lax.broadcasted_iota(jnp.int32, (LANES, width), 1) % LANES) // size
    fade = jnp.concatenate([rows_ref[:LANES]] * genomes, axis=1)
    end = LANES + 8 * own_ref.shape[0]
    skip = rows_ref[end : end + 1]
    across = (count + 1) * CHUNK
    high, low = matrices_ref[:, :across], matrices_ref[:, across : 2 * across]
    ends_high = matrices_ref[:, 2 * across : 2 * across + CHUNK]
    ends_low = matrices_ref[:, 2 * across + CHUNK :]
    state = jnp.zeros((LANES, width), f32)
    chunks = length // CHUNK
    for c in range(chunks):
        spans = [slice(b * length + c * CHUNK, b * length + (c + 1) * CHUNK) for b in range(genomes)]
        block = jnp.concatenate([product[span] for span in spans], axis=1)
        stacked = jnp.concatenate(
            [jnp.where(lane // size == g, block, 0.0) for g in range(count)] + [state], axis=0
        )
        conv = dot3(high, low, stacked)
        for b, span in enumerate(spans):
            value = conv[:, b * LANES : (b + 1) * LANES] + skip * product[span]
            held_ref[span, :] = (query[span] * value).astype(bf16)
        if c < chunks - 1:
            ends = dot3(ends_high, ends_low, block)
            state = fade * state + jnp.where(same, ends, 0.0)
    part = length // 2
    for r, piece_ref in enumerate(piece_refs):
        place = 2 * (core ^ (r % 2)) + (half ^ (r // 2))
        piece_ref[...] = held_ref[pl.ds(pl.multiple_of(place * part, part), part), :]
    mine_ref[...] = picked_ref[pl.ds(pl.multiple_of((2 * core + half) * part, part), part), :]


def offer_kernel(place_ref, rows_ref, packed_ref, out_ref):
    del place_ref, packed_ref
    out_ref[...] = rows_ref[...]


def residual(picked_ref, table_ref, first, width):
    return jnp.dot(
        picked_ref[...],
        table_ref[:, pl.ds(pl.multiple_of(first, width), width)],
        preferred_element_type=f32,
    )


def near_kernel(place_ref, picked_ref, table_ref, *refs):
    piece_refs, (own_ref, core_ref, out_ref, joined_ref) = refs[:4], refs[4:]
    quad, half = place_ref[0], place_ref[1]
    block = 2 * LANES
    for m, piece_ref in enumerate(piece_refs):
        for other_core in (0, 1):
            near = piece_ref[other_core].astype(f32)
            far = piece_ref[2 + other_core].astype(f32)
            first = jnp.where(half == 0, near, far)
            second = jnp.where(half == 0, far, near)
            left = lane_half(first.shape)
            pair = [
                jnp.where(left, first, half_turn(second)),
                jnp.where(left, half_turn(first), second),
            ]
            joined_ref[2 * (quad ^ m) + other_core] = jnp.concatenate(pair, axis=1).astype(bf16)
    width = own_ref.shape[1]
    total = jnp.zeros(out_ref.shape, f32)
    for member in range(4):
        rows = slice(member * block, (member + 1) * block)
        for other_core, ref in enumerate((own_ref, core_ref)):
            total += jnp.dot(
                joined_ref[2 * member + other_core], ref[rows, :], preferred_element_type=f32
            )
    total += residual(picked_ref, table_ref, (4 * half + quad) * width, width)
    out_ref[...] = total.astype(bf16)


def far_kernel(place_ref, picked_ref, table_ref, near_ref, joined_ref, *refs):
    far_refs, out_ref = (refs[:2], refs[2:4]), refs[4]
    quad, half, group, core = (place_ref[i] for i in range(4))
    block = 2 * LANES
    width = near_ref.shape[1]
    total = jnp.zeros(near_ref.shape, f32)
    for member in range(4):
        rows = slice((member % 2) * block, (member % 2 + 1) * block)
        for other_core in (0, 1):
            source = 2 * (2 * (group ^ (member // 2)) + member % 2) + other_core
            total += jnp.dot(
                joined_ref[source],
                far_refs[member // 2][other_core][rows, :],
                preferred_element_type=f32,
            )
    total += residual(picked_ref, table_ref, (4 * (half ^ 1) + (quad ^ 2)) * width, width)
    out_ref[half ^ core] = near_ref[...]
    out_ref[half ^ 1 ^ core] = total.astype(bf16)


def place_kernel(place_ref, *refs):
    piece_refs, out_ref = refs[:4], refs[4]
    quad, half, core = place_ref[0], place_ref[1], place_ref[3]
    width = piece_refs[0].shape[2]
    for m, piece_ref in enumerate(piece_refs):
        first = pl.multiple_of((quad ^ m ^ (2 * (half ^ core))) * width, width)
        for g in (0, 1):
            out_ref[core ^ g, :, pl.ds(first, width)] = piece_ref[g]


def called(kernel, out_shape, scalars, *operands, scratch=(), mib=16, earlier=()):
    smem = pl.BlockSpec(memory_space=pltpu.SMEM)
    vmem = pl.BlockSpec(memory_space=pltpu.VMEM)
    anywhere = pl.BlockSpec(memory_space=pl.ANY)
    many = isinstance(out_shape, (list, tuple))
    inputs, waits = len(scalars) + len(operands), len(earlier)

    def body(*refs):
        kernel(*refs[:inputs], *refs[inputs + waits :])

    return pl.pallas_call(
        body,
        out_shape=out_shape,
        in_specs=[smem] * len(scalars) + [vmem] * len(operands) + [anywhere] * waits,
        out_specs=[vmem] * len(out_shape) if many else vmem,
        scratch_shapes=scratch,
        compiler_params=pltpu.CompilerParams(vmem_limit_bytes=mib * MIB),
    )(*scalars, *operands, *earlier)


def shaped(*shape, dtype=f32):
    return jax.ShapeDtypeStruct(shape, dtype)


def pass_kernel(*refs):
    del refs


def after(value, earlier):
    return pl.pallas_call(
        pass_kernel,
        out_shape=shaped(*value.shape, dtype=value.dtype),
        in_specs=[pl.BlockSpec(memory_space=pl.ANY)] * 2,
        out_specs=pl.BlockSpec(memory_space=pl.ANY),
        input_output_aliases={0: 0},
        compiler_params=pltpu.CompilerParams(vmem_limit_bytes=MIB),
    )(value, earlier)


def quad_body(
    tokens,
    embed_table,
    norm_gain,
    input_proj,
    short_filter,
    pole_rate,
    residue,
    skip_gain,
    output_proj,
):
    genomes, rows = tokens.shape
    depth, branches, channels = input_proj.shape
    vocab, features = embed_table.shape
    members = lax.axis_size("ctx") // 2
    ctx, core, group = (lax.axis_index(name) for name in ("ctx", "chan", "groups"))
    quad, half = ctx % members, ctx // members
    place = jnp.stack([quad, half, group, core]).astype(jnp.int32)
    block = channels // members

    weights = input_proj.transpose(1, 0, 2)
    anywhere = pl.BlockSpec(memory_space=pl.ANY)
    packed = pl.pallas_call(
        pack_kernel,
        out_shape=[shaped(branches * depth + SPARE, LANES, dtype=bf16)] * members,
        in_specs=[
            pl.BlockSpec(memory_space=pltpu.SMEM),
            pl.BlockSpec(memory_space=pltpu.VMEM),
            anywhere,
        ],
        out_specs=[pl.BlockSpec(memory_space=pltpu.VMEM)] * members,
        scratch_shapes=[pltpu.SemaphoreType.DMA((members, branches))],
        compiler_params=pltpu.CompilerParams(vmem_limit_bytes=62 * MIB),
    )(place, tokens, weights)
    gathered = [packed[0]] + [swapped(packed[m], "ctx", m) for m in range(1, members)]
    length = 2 * members * rows

    half_rows = output_proj.shape[0] // 2
    width = output_proj.shape[1]
    offered = pl.pallas_call(
        offer_kernel,
        out_shape=shaped(half_rows, width, dtype=bf16),
        grid_spec=pltpu.PrefetchScalarGridSpec(
            num_scalar_prefetch=1,
            grid=(1,),
            in_specs=[pl.BlockSpec((half_rows, width), lambda i, place: (place[2], 0)), anywhere],
            out_specs=pl.BlockSpec((half_rows, width), lambda i, place: (0, 0)),
        ),
        compiler_params=pltpu.CompilerParams(vmem_limit_bytes=4 * MIB),
    )(place, output_proj, packed[0])
    count = 2 * members
    inner = [(i, count - 2 - i + 2 * (i % 2)) for i in range(members // 2, members + members // 2)]
    outer = [
        (i, count - 2 - i + 2 * (i % 2))
        for i in range(count)
        if not members // 2 <= i < members + members // 2
    ]

    part = features // 2
    step = 128
    normed = pl.pallas_call(
        norm_kernel,
        out_shape=shaped(vocab, part, dtype=bf16),
        grid_spec=pltpu.PrefetchScalarGridSpec(
            num_scalar_prefetch=1,
            grid=(vocab // step,),
            in_specs=[
                pl.BlockSpec((step, features), lambda i, place: (i, 0)),
                pl.BlockSpec((1, part), lambda i, place: (0, place[1])),
                pl.BlockSpec((step, part), lambda i, place: (i, place[1])),
                anywhere,
            ],
            out_specs=pl.BlockSpec((step, part), lambda i, place: (i, 0)),
        ),
        compiler_params=pltpu.CompilerParams(vmem_limit_bytes=16 * MIB),
    )(place, embed_table, norm_gain.reshape(1, features), embed_table, gathered[1])

    inner_fetched = lax.ppermute(offered, "ctx", inner)
    amp = residue * jnp.sqrt(-jnp.expm1(-2.0 * pole_rate))
    across = (LANES // pole_rate.shape[1] + 1) * CHUNK
    matrices, lines = called(
        prepare_kernel,
        [
            shaped(CHUNK, 2 * across + 2 * CHUNK, dtype=bf16),
            shaped(LANES + 8 * (branches + 1), LANES),
        ],
        (place,),
        pole_rate.T,
        amp.T,
        short_filter.transpose(0, 2, 1),
        skip_gain.reshape(-1, LANES),
        earlier=(gathered[1],),
    )

    table_rows = branches * (vocab // 2)
    keep, send = called(
        partial_kernel,
        [shaped(table_rows, LANES), shaped(table_rows + SPARE, LANES, dtype=bf16)],
        (place,),
        normed,
        *gathered,
        earlier=(matrices, inner_fetched),
    )
    arrived = swapped(send, "ctx", members)
    own = (keep + arrived[:table_rows].astype(f32)).astype(bf16)
    own = own.reshape(branches, vocab // 2, LANES)
    other = swapped(own, "groups", 1)
    span = length // 2
    *pieces, picked = called(
        functools.partial(conv_kernel, genomes=genomes, rows=rows),
        [shaped(span, LANES, dtype=bf16)] * 4 + [shaped(span, vocab, dtype=bf16)],
        (place,),
        send,
        arrived,
        own,
        other,
        matrices,
        lines,
        scratch=[pltpu.VMEM((genomes * length, vocab), bf16), pltpu.VMEM((genomes * length, LANES), bf16)],
    )
    core_piece = swapped(pieces[1], "chan", 1)
    piece = jnp.stack(
        [
            pieces[0],
            core_piece,
            swapped(pieces[2], "ctx", members),
            swapped_both(pieces[3], members),
        ]
    )
    gated = [piece] + [swapped(piece, "ctx", m) for m in range(1, members)]

    outer_fetched = lax.ppermute(after(offered, own), "ctx", outer)
    fetched = jnp.where((ctx >= members // 2) & (ctx < members + members // 2), inner_fetched, outer_fetched)
    fetched = after(fetched, piece)
    shared = swapped(fetched, "groups", 1)
    for ready in gated[1:]:
        shared = after(shared, ready)
    near, joined = called(
        near_kernel,
        [shaped(span, width, dtype=bf16), shaped(4 * 2, span, 2 * LANES, dtype=bf16)],
        (place,),
        picked,
        embed_table,
        *gated,
        output_proj,
        swapped(output_proj, "chan", 1),
        mib=24,
    )
    results = called(
        far_kernel,
        shaped(2, span, width, dtype=bf16),
        (place,),
        picked,
        embed_table,
        near,
        joined,
        fetched,
        swapped(fetched, "chan", 1),
        shared,
        swapped(shared, "chan", 1),
        mib=24,
    )
    both = jnp.stack([results[0], swapped(results[1], "chan", 1)])

    def rows_of(member):
        return lax.dynamic_slice_in_dim(both, member * rows, rows, 1)

    arrived = [rows_of(quad)] + [swapped(rows_of(quad ^ m), "ctx", m) for m in range(1, members)]
    return called(
        place_kernel, shaped(genomes, rows, members * width, dtype=bf16), (place,), *arrived
    )


def solution(mesh):
    sizes = tuple(mesh.shape[name] for name in ("groups", "ctx", "chan"))
    return jax.shard_map(
        quad_body if sizes == (2, 8, 2) else general_body,
        mesh=mesh,
        in_specs=(
            P("groups", "ctx"),
            P(),
            P(),
            P("ctx", None, "chan"),
            P(None, "chan", None),
            P("chan", None),
            P("chan", None),
            P("chan"),
            P("chan", "ctx"),
        ),
        out_specs=P("groups", "ctx", "chan"),
        check_vma=False,
    )
```

```python
import functools

import jax
import jax.numpy as jnp
from jax import lax
from jax.experimental import pallas as pl
from jax.experimental.pallas import tpu as pltpu
from jax.sharding import PartitionSpec as P

epsilon = 1e-06
highest = lax.Precision.HIGHEST
f32 = jnp.float32
bf16 = jnp.bfloat16
CHUNK = 128
LANES = 128
MIB = 1024 * 1024
SPARE = 16


def passed_along(shard, axis, by):
    count = lax.axis_size(axis)
    pairs = [(i, i + by) for i in range(count) if 0 <= i + by < count]
    return lax.ppermute(shard, axis, pairs)


def entering(shard, axis, combine, identity):
    count, mine = (lax.axis_size(axis), lax.axis_index(axis))
    everything = jax.tree.map(lambda part: lax.all_gather(part, axis), shard)
    start = jax.tree.map(
        lambda part, zero: jnp.broadcast_to(jnp.asarray(zero, part.dtype), part.shape),
        shard,
        identity,
    )

    def hop(k, before):
        reached = k < mine
        new = combine(before, jax.tree.map(lambda part: part[k], everything))
        return jax.tree.map(lambda a, b: jnp.where(reached, a, b), new, before)

    return lax.fori_loop(0, count, hop, start)


def local_block(operands):
    rising, falling, inputs = operands
    length = rising.shape[2]
    toeplitz = jnp.einsum("gnt,gns->gts", rising, falling, precision=highest)
    causal = jnp.arange(length)[:, None] >= jnp.arange(length)[None, :]
    toeplitz = jnp.where(causal[None], toeplitz, 0.0)
    return jnp.einsum("gms,gts->gmt", inputs, toeplitz, precision=highest)


def lookup_rows(token_block, embed_table):
    vocab_count = embed_table.shape[0]
    onehot = (token_block[:, None] == jnp.arange(vocab_count, dtype=jnp.int32)[None, :]).astype(
        jnp.bfloat16
    )
    return jnp.dot(onehot, embed_table, preferred_element_type=jnp.float32)


def general_body(
    tokens,
    embed_table,
    norm_gain,
    input_proj,
    short_filter,
    pole_rate,
    residue,
    skip_gain,
    output_proj,
):
    genome_count, row_count = tokens.shape
    part_rows, branch_count, channels = input_proj.shape
    groups = pole_rate.shape[0]
    group_size = channels // groups
    tap_count = short_filter.shape[2]
    flat_count = genome_count * row_count
    flat_tokens = tokens.reshape(flat_count)
    widened = lookup_rows(flat_tokens, embed_table)
    inv_rms = lax.rsqrt(jnp.mean(widened * widened, axis=-1, keepdims=True) + epsilon)
    normed = (widened * inv_rms * norm_gain).astype(jnp.bfloat16)
    proj_cols = branch_count * channels
    flat_weight = input_proj.reshape(part_rows, proj_cols)
    spread = lax.all_to_all(normed, "ctx", split_axis=1, concat_axis=0, tiled=True)
    summed = lax.psum_scatter(
        jnp.dot(spread, flat_weight, preferred_element_type=jnp.float32),
        "ctx",
        scatter_dimension=0,
        tiled=True,
    )
    projected = summed.astype(jnp.bfloat16).reshape(genome_count, row_count, branch_count, channels)
    rim = passed_along(projected[:, row_count - (tap_count - 1) :], "ctx", 1)
    extended = jnp.concatenate([rim, projected], axis=1).astype(jnp.float32)
    taps_full = jnp.broadcast_to(
        short_filter[:, :, None, :], (branch_count, groups, group_size, tap_count)
    ).reshape(branch_count, channels, tap_count)
    filtered = jnp.zeros((genome_count, row_count, branch_count, channels), jnp.float32)
    for lag in range(tap_count):
        first_row = tap_count - 1 - lag
        filtered = filtered + taps_full[:, :, lag] * extended[:, first_row : first_row + row_count]
    query_part = filtered[:, :, 0]
    product = filtered[:, :, 1] * filtered[:, :, 2]
    mixes = genome_count * group_size
    grouped = (
        product.reshape(genome_count, row_count, groups, group_size)
        .transpose(2, 0, 3, 1)
        .reshape(groups, mixes, row_count)
    )
    positions = jnp.arange(row_count, dtype=jnp.float32)
    middle = float(row_count // 2)
    powers = jnp.exp(-pole_rate[:, :, None] * positions)
    next_powers = jnp.exp(-pole_rate[:, :, None] * (positions + 1.0))
    pole_amp = residue * jnp.sqrt(-jnp.expm1(-2.0 * pole_rate))
    rising = pole_amp[:, :, None] * jnp.exp(-pole_rate[:, :, None] * (positions - middle))
    falling = jnp.exp(-pole_rate[:, :, None] * (middle - positions))
    block_size = 8
    blocks = groups // block_size
    poles = pole_rate.shape[1]
    local_part = lax.map(
        local_block,
        (
            rising.reshape(blocks, block_size, poles, row_count),
            falling.reshape(blocks, block_size, poles, row_count),
            grouped.reshape(blocks, block_size, mixes, row_count),
        ),
    )
    local_part = local_part.reshape(groups, mixes, row_count)
    end_state = jnp.einsum("gms,gns->gmn", grouped, powers[:, :, ::-1], precision=highest)
    block_decay = jnp.exp(-pole_rate * row_count)

    def combine(earlier, later):
        return (earlier[0] * later[0], later[0][:, None, :] * earlier[1] + later[1])

    identity = (jnp.ones_like(block_decay), jnp.zeros_like(end_state))
    incoming = entering((block_decay, end_state), "ctx", combine, identity)[1]
    weighted = incoming * pole_amp[:, None, :]
    correction = jnp.einsum("gmn,gnt->gmt", weighted, next_powers, precision=highest)
    long_conv = (
        (local_part + correction)
        .reshape(groups, genome_count, group_size, row_count)
        .transpose(1, 3, 0, 2)
        .reshape(genome_count, row_count, channels)
    )
    gated = (
        (query_part * (long_conv + skip_gain * product))
        .astype(jnp.bfloat16)
        .reshape(flat_count, channels)
    )
    partial_value = jnp.dot(
        gated,
        lax.all_gather(output_proj, "ctx", axis=1, tiled=True),
        preferred_element_type=jnp.float32,
    )
    own_share = lax.psum_scatter(partial_value, "chan", scatter_dimension=1, tiled=True)
    half_width = own_share.shape[1]
    residual_part = lax.dynamic_slice_in_dim(
        widened, lax.axis_index("chan") * half_width, half_width, 1
    )
    block_out = (residual_part + own_share).astype(jnp.bfloat16)
    return block_out.reshape(genome_count, row_count, half_width)


def swapped(value, axis, mask):
    count = lax.axis_size(axis)
    return lax.ppermute(value, axis, [(i, i ^ mask) for i in range(count)])


def swapped_both(value, ctx_mask):
    count, cores = lax.axis_size("ctx"), lax.axis_size("chan")
    pairs = [
        (i * cores + c, (i ^ ctx_mask) * cores + (c ^ 1)) for i in range(count) for c in range(cores)
    ]
    return lax.ppermute(value, ("ctx", "chan"), pairs)


def split(value):
    high = value.astype(bf16)
    return high, (value - high.astype(f32)).astype(bf16)


def dot3(a_high, a_low, b):
    b_high, b_low = split(b)
    total = jnp.dot(a_high, b_high, preferred_element_type=f32)
    total += jnp.dot(a_low, b_high, preferred_element_type=f32)
    return total + jnp.dot(a_high, b_low, preferred_element_type=f32)


def lane_half(shape):
    return lax.broadcasted_iota(jnp.int32, shape, len(shape) - 1) < LANES // 2


def half_turn(value):
    return pltpu.roll(value, LANES // 2, value.ndim - 1)


def norm_kernel(place_ref, table_ref, gain_ref, part_ref, packed_ref, out_ref):
    del place_ref, packed_ref
    widened = table_ref[...].astype(f32)
    mean = jnp.sum(widened * widened, axis=1, keepdims=True) / widened.shape[1]
    own = part_ref[...].astype(f32)
    out_ref[...] = (own * lax.rsqrt(mean + epsilon) * gain_ref[...]).astype(bf16)


def pack_kernel(token_ref, weight_ref, *refs):
    out_refs, sems = refs[:-1], refs[-1]
    branches, depth, channels = weight_ref.shape
    members = len(out_refs)
    quad, group = lax.axis_index("ctx") % members, lax.axis_index("groups")
    block = channels // members
    copies = []
    for m in (1, 2, 3, 0):
        first = pl.multiple_of((quad ^ m) * block + group * LANES, LANES)
        for j in range(branches):
            copies.append(
                pltpu.make_async_copy(
                    weight_ref.at[j, :, pl.ds(first, LANES)],
                    out_refs[m].at[pl.ds(j * depth, depth), :],
                    sems.at[m, j],
                )
            )
            copies[-1].start()
    rows = token_ref.shape[1]
    row = lax.broadcasted_iota(jnp.int32, (SPARE, rows), 0)
    token = jnp.where(row % 4 < 2, token_ref[0:1, :], token_ref[1:2, :])
    token = jnp.where(row % 2 == 0, token >> 8, token & 255)
    token = jnp.where(row // 4 == quad, token, 0).astype(f32).astype(bf16)
    for out_ref in out_refs:
        out_ref[branches * depth :, :] = jnp.zeros((SPARE, LANES), bf16)
        out_ref[branches * depth :, :rows] = token
    for copy in copies:
        copy.wait()


def pick(half, near_ref, far_ref, picked_ref, genomes, rows):
    vocab = picked_ref.shape[1]
    length = picked_ref.shape[0] // genomes
    first = near_ref.shape[0] - SPARE
    diagonal = lax.broadcasted_iota(jnp.int32, (rows, rows), 0) == lax.broadcasted_iota(
        jnp.int32, (rows, rows), 1
    )
    entries = lax.broadcasted_iota(jnp.int32, (rows, vocab), 1).astype(f32)
    for other, ref in enumerate((near_ref, far_ref)):
        parts = ref[first:, :rows].astype(f32)
        for member in range(length // (2 * rows)):
            for b in range(genomes):
                at = 4 * member + 2 * b
                line = parts[at : at + 1] * 256.0 + parts[at + 1 : at + 2]
                column = jnp.sum(jnp.where(diagonal, line, 0.0), axis=1, keepdims=True)
                place = b * length + (half ^ other) * (length // 2) + member * rows
                picked_ref[pl.ds(pl.multiple_of(place, rows), rows), :] = (
                    (column == entries).astype(f32).astype(bf16)
                )


def prepare_kernel(place_ref, rate_ref, amp_ref, taps_ref, skip_ref, matrices_ref, rows_ref):
    quad, half = place_ref[0], place_ref[1]

    group_count = rate_ref.shape[1]
    poles = rate_ref.shape[0]
    count = LANES // poles

    def group_at(lane):
        place = lane // poles
        return quad * (2 * count) + (place // (count // 2)) * count + half * (count // 2) + place % (count // 2)

    lane = lax.broadcasted_iota(jnp.int32, (group_count, LANES), 1)
    chosen = (lax.broadcasted_iota(jnp.int32, (group_count, LANES), 0) == group_at(lane)).astype(f32)
    turned_lane = lax.broadcasted_iota(jnp.int32, (LANES, group_count), 0)
    turned = (lax.broadcasted_iota(jnp.int32, (LANES, group_count), 1) == group_at(turned_lane)).astype(f32)

    def along_lanes(ref):
        spread = jnp.dot(ref[...], chosen, precision=highest, preferred_element_type=f32)
        keep = lax.broadcasted_iota(jnp.int32, spread.shape, 0) == lax.broadcasted_iota(
            jnp.int32, spread.shape, 1
        ) % poles
        return jnp.sum(jnp.where(keep, spread, 0.0), axis=0, keepdims=True)

    rate, amp = along_lanes(rate_ref), along_lanes(amp_ref)
    spread = lax.dot_general(
        turned, rate_ref[...], (((1,), (1,)), ((), ())), precision=highest, preferred_element_type=f32
    )
    keep = lax.broadcasted_iota(jnp.int32, spread.shape, 1) == lax.broadcasted_iota(
        jnp.int32, spread.shape, 0
    ) % poles
    rate_col = jnp.sum(jnp.where(keep, spread, 0.0), axis=1, keepdims=True)

    square = (CHUNK, LANES)
    row = lax.broadcasted_iota(jnp.int32, square, 0)
    col = lax.broadcasted_iota(jnp.int32, square, 1)
    at = row.astype(f32)
    middle = float(CHUNK // 2)
    rising = amp * jnp.exp(-rate * (at - middle))
    falling = jnp.exp(-rate * (middle - at))
    width = (count + 1) * CHUNK
    for g in range(count):
        own = jnp.where(col // poles == g, falling, 0.0)
        block = lax.dot_general(
            rising, own, (((1,), (1,)), ((), ())), precision=highest, preferred_element_type=f32
        )
        high, low = split(jnp.where(row >= col, block, 0.0))
        matrices_ref[:, g * CHUNK : (g + 1) * CHUNK] = high
        matrices_ref[:, width + g * CHUNK : width + (g + 1) * CHUNK] = low
    high, low = split(amp * jnp.exp(-rate * (at + 1.0)))
    matrices_ref[:, count * CHUNK : width] = high
    matrices_ref[:, width + count * CHUNK : 2 * width] = low
    high, low = split(jnp.exp(-rate_col * (float(CHUNK - 1) - col.astype(f32))))
    matrices_ref[:, 2 * width : 2 * width + CHUNK] = high
    matrices_ref[:, 2 * width + CHUNK :] = low

    rows_ref[:LANES] = jnp.exp(-rate_col * float(CHUNK)) + jnp.zeros(square, f32)
    branches = taps_ref.shape[0]
    for j in range(branches):
        taps = jnp.dot(taps_ref[j], chosen, precision=highest, preferred_element_type=f32)
        rows_ref[LANES + 8 * j : LANES + 8 * j + taps.shape[0]] = taps
    upper = skip_ref[pl.ds(2 * quad, 1), :]
    lower = skip_ref[pl.ds(2 * quad + 1, 1), :]
    upper = jnp.where(half == 0, upper, half_turn(upper))
    lower = jnp.where(half == 1, lower, half_turn(lower))
    end = LANES + 8 * branches
    rows_ref[end : end + 1] = jnp.where(lane_half(upper.shape), upper, lower)


def partial_kernel(place_ref, normed_ref, *refs):
    weight_refs, (keep_ref, send_ref) = refs[:-2], refs[-2:]
    quad, half = place_ref[0], place_ref[1]
    rows, features = normed_ref.shape
    depth = features // len(weight_refs)
    count = weight_refs[0].shape[0] // depth
    total = jnp.zeros((rows, count * LANES), f32)
    tokens = jnp.zeros((SPARE, LANES), f32)
    for m, weight_ref in enumerate(weight_refs):
        first = pl.multiple_of((quad ^ m) * depth, depth)
        columns = jnp.concatenate(
            [weight_ref[j * depth : (j + 1) * depth, :] for j in range(count)], axis=1
        )
        total += jnp.dot(
            normed_ref[:, pl.ds(first, depth)], columns, preferred_element_type=f32
        )
        tokens += weight_ref[count * depth :, :].astype(f32)
    part = rows // 2
    for j in range(count):
        mine = total[:, j * LANES : (j + 1) * LANES]
        mine = jnp.where(half == 0, mine, half_turn(mine))
        top, bottom = mine[:part], mine[part:]
        left = lane_half(top.shape)
        keep_ref[j * part : (j + 1) * part, :] = jnp.where(left, top, half_turn(bottom))
        send_ref[j * part : (j + 1) * part, :] = jnp.where(left, half_turn(top), bottom).astype(bf16)
    send_ref[count * part :, :] = tokens.astype(bf16)


def filtered_branch(group, picked, row, mine, theirs, rows_ref, branch):
    mine, theirs = mine.astype(f32), theirs.astype(f32)
    first = jnp.where(group == 0, mine, theirs)
    second = jnp.where(group == 0, theirs, mine)
    left = lane_half(first.shape)
    top = jnp.where(left, first, half_turn(second))
    bottom = jnp.where(left, half_turn(first), second)
    table = jnp.concatenate([top, bottom], axis=0).astype(bf16)
    now = jnp.dot(picked, table, preferred_element_type=f32)
    first_tap = LANES + 8 * branch
    total = rows_ref[first_tap : first_tap + 1] * now
    for lag in range(1, 3):
        late = jnp.where(row >= lag, pltpu.roll(now, lag, 0), 0.0)
        total += rows_ref[first_tap + lag : first_tap + lag + 1] * late
    return total


def conv_kernel(
    place_ref, near_ref, far_ref, own_ref, other_ref, matrices_ref, rows_ref, *refs, genomes, rows
):
    piece_refs, (mine_ref, picked_ref, held_ref) = refs[:4], refs[4:]
    half, group, core = place_ref[1], place_ref[2], place_ref[3]
    pick(half, near_ref, far_ref, picked_ref, genomes, rows)
    positions = picked_ref.shape[0]
    length = positions // genomes
    row = lax.broadcasted_iota(jnp.int32, (positions, LANES), 0) % length
    picked = picked_ref[...]
    query, key, value = (
        filtered_branch(group, picked, row, own_ref[j], other_ref[j], rows_ref, j) for j in range(3)
    )
    product = key * value
    size = 16
    count = LANES // size
    width = genomes * LANES
    lane = lax.broadcasted_iota(jnp.int32, (CHUNK, width), 1) % LANES
    pole_row = lax.broadcasted_iota(jnp.int32, (LANES, width), 0)
    same = pole_row // size == (lax.broadcasted_iota(jnp.int32, (LANES, width), 1) % LANES) // size
    fade = jnp.concatenate([rows_ref[:LANES]] * genomes, axis=1)
    end = LANES + 8 * own_ref.shape[0]
    skip = rows_ref[end : end + 1]
    across = (count + 1) * CHUNK
    high, low = matrices_ref[:, :across], matrices_ref[:, across : 2 * across]
    ends_high = matrices_ref[:, 2 * across : 2 * across + CHUNK]
    ends_low = matrices_ref[:, 2 * across + CHUNK :]
    state = jnp.zeros((LANES, width), f32)
    chunks = length // CHUNK
    for c in range(chunks):
        spans = [slice(b * length + c * CHUNK, b * length + (c + 1) * CHUNK) for b in range(genomes)]
        block = jnp.concatenate([product[span] for span in spans], axis=1)
        stacked = jnp.concatenate(
            [jnp.where(lane // size == g, block, 0.0) for g in range(count)] + [state], axis=0
        )
        conv = dot3(high, low, stacked)
        for b, span in enumerate(spans):
            value = conv[:, b * LANES : (b + 1) * LANES] + skip * product[span]
            held_ref[span, :] = (query[span] * value).astype(bf16)
        if c < chunks - 1:
            ends = dot3(ends_high, ends_low, block)
            state = fade * state + jnp.where(same, ends, 0.0)
    part = length // 2
    for r, piece_ref in enumerate(piece_refs):
        place = 2 * (core ^ (r % 2)) + (half ^ (r // 2))
        piece_ref[...] = held_ref[pl.ds(pl.multiple_of(place * part, part), part), :]
    mine_ref[...] = picked_ref[pl.ds(pl.multiple_of((2 * core + half) * part, part), part), :]


def offer_kernel(place_ref, rows_ref, packed_ref, first_ref, second_ref):
    del place_ref, packed_ref
    count = first_ref.shape[0]
    first_ref[...] = rows_ref[:count]
    second_ref[...] = rows_ref[count:]


def residual(picked_ref, table_ref, first, width):
    return jnp.dot(
        picked_ref[...],
        table_ref[:, pl.ds(pl.multiple_of(first, width), width)],
        preferred_element_type=f32,
    )


def near_kernel(place_ref, picked_ref, table_ref, *refs):
    piece_refs, (own_ref, core_ref, out_ref, joined_ref) = refs[:4], refs[4:]
    quad, half = place_ref[0], place_ref[1]
    block = 2 * LANES
    for m, piece_ref in enumerate(piece_refs):
        for other_core in (0, 1):
            near = piece_ref[other_core].astype(f32)
            far = piece_ref[2 + other_core].astype(f32)
            first = jnp.where(half == 0, near, far)
            second = jnp.where(half == 0, far, near)
            left = lane_half(first.shape)
            pair = [
                jnp.where(left, first, half_turn(second)),
                jnp.where(left, half_turn(first), second),
            ]
            joined_ref[2 * (quad ^ m) + other_core] = jnp.concatenate(pair, axis=1).astype(bf16)
    width = own_ref.shape[1]
    total = jnp.zeros(out_ref.shape, f32)
    for member in range(4):
        rows = slice(member * block, (member + 1) * block)
        for other_core, ref in enumerate((own_ref, core_ref)):
            total += jnp.dot(
                joined_ref[2 * member + other_core], ref[rows, :], preferred_element_type=f32
            )
    total += residual(picked_ref, table_ref, (4 * half + quad) * width, width)
    out_ref[...] = total.astype(bf16)


def far_kernel(place_ref, picked_ref, table_ref, near_ref, joined_ref, *refs):
    far_refs, out_ref = (refs[:2], refs[2:4]), refs[4]
    quad, half, group, core = (place_ref[i] for i in range(4))
    block = 2 * LANES
    width = near_ref.shape[1]
    total = jnp.zeros(near_ref.shape, f32)
    for member in range(4):
        rows = slice((member % 2) * block, (member % 2 + 1) * block)
        for other_core in (0, 1):
            source = 2 * (2 * (group ^ (member // 2)) + member % 2) + other_core
            total += jnp.dot(
                joined_ref[source],
                far_refs[member // 2][other_core][rows, :],
                preferred_element_type=f32,
            )
    total += residual(picked_ref, table_ref, (4 * (half ^ 1) + (quad ^ 2)) * width, width)
    out_ref[half ^ core] = near_ref[...]
    out_ref[half ^ 1 ^ core] = total.astype(bf16)


def place_kernel(place_ref, *refs):
    piece_refs, out_ref = refs[:4], refs[4]
    quad, half, core = place_ref[0], place_ref[1], place_ref[3]
    width = piece_refs[0].shape[2]
    for m, piece_ref in enumerate(piece_refs):
        first = pl.multiple_of((quad ^ m ^ (2 * (half ^ core))) * width, width)
        for g in (0, 1):
            out_ref[core ^ g, :, pl.ds(first, width)] = piece_ref[g]


def called(kernel, out_shape, scalars, *operands, scratch=(), mib=16, earlier=()):
    smem = pl.BlockSpec(memory_space=pltpu.SMEM)
    vmem = pl.BlockSpec(memory_space=pltpu.VMEM)
    anywhere = pl.BlockSpec(memory_space=pl.ANY)
    many = isinstance(out_shape, (list, tuple))
    inputs, waits = len(scalars) + len(operands), len(earlier)

    def body(*refs):
        kernel(*refs[:inputs], *refs[inputs + waits :])

    return pl.pallas_call(
        body,
        out_shape=out_shape,
        in_specs=[smem] * len(scalars) + [vmem] * len(operands) + [anywhere] * waits,
        out_specs=[vmem] * len(out_shape) if many else vmem,
        scratch_shapes=scratch,
        compiler_params=pltpu.CompilerParams(vmem_limit_bytes=mib * MIB),
    )(*scalars, *operands, *earlier)


def shaped(*shape, dtype=f32):
    return jax.ShapeDtypeStruct(shape, dtype)


def pass_kernel(*refs):
    del refs


def after(value, earlier):
    return pl.pallas_call(
        pass_kernel,
        out_shape=shaped(*value.shape, dtype=value.dtype),
        in_specs=[pl.BlockSpec(memory_space=pl.ANY)] * 2,
        out_specs=pl.BlockSpec(memory_space=pl.ANY),
        input_output_aliases={0: 0},
        compiler_params=pltpu.CompilerParams(vmem_limit_bytes=MIB),
    )(value, earlier)


def quad_body(
    tokens,
    embed_table,
    norm_gain,
    input_proj,
    short_filter,
    pole_rate,
    residue,
    skip_gain,
    output_proj,
):
    genomes, rows = tokens.shape
    depth, branches, channels = input_proj.shape
    vocab, features = embed_table.shape
    members = lax.axis_size("ctx") // 2
    ctx, core, group = (lax.axis_index(name) for name in ("ctx", "chan", "groups"))
    quad, half = ctx % members, ctx // members
    place = jnp.stack([quad, half, group, core]).astype(jnp.int32)
    block = channels // members

    weights = input_proj.transpose(1, 0, 2)
    anywhere = pl.BlockSpec(memory_space=pl.ANY)
    packed = pl.pallas_call(
        pack_kernel,
        out_shape=[shaped(branches * depth + SPARE, LANES, dtype=bf16)] * members,
        in_specs=[pl.BlockSpec(memory_space=pltpu.VMEM), anywhere],
        out_specs=[pl.BlockSpec(memory_space=pltpu.VMEM)] * members,
        scratch_shapes=[pltpu.SemaphoreType.DMA((members, branches))],
        compiler_params=pltpu.CompilerParams(vmem_limit_bytes=61 * MIB),
    )(tokens, weights)
    gathered = [packed[0]] + [swapped(packed[m], "ctx", m) for m in range(1, members)]
    length = 2 * members * rows

    half_rows = output_proj.shape[0] // 2
    width = output_proj.shape[1]
    offered = pl.pallas_call(
        offer_kernel,
        out_shape=[shaped(half_rows // 2, width, dtype=bf16)] * 2,
        grid_spec=pltpu.PrefetchScalarGridSpec(
            num_scalar_prefetch=1,
            grid=(1,),
            in_specs=[pl.BlockSpec((half_rows, width), lambda i, place: (place[2], 0)), anywhere],
            out_specs=[pl.BlockSpec((half_rows // 2, width), lambda i, place: (0, 0))] * 2,
        ),
        compiler_params=pltpu.CompilerParams(vmem_limit_bytes=4 * MIB),
    )(place, output_proj, packed[1])
    count = 2 * members
    inner = [(i, count - 2 - i + 2 * (i % 2)) for i in range(members // 2, members + members // 2)]
    outer = [
        (i, count - 2 - i + 2 * (i % 2))
        for i in range(count)
        if not members // 2 <= i < members + members // 2
    ]

    part = features // 2
    step = 128
    normed = pl.pallas_call(
        norm_kernel,
        out_shape=shaped(vocab, part, dtype=bf16),
        grid_spec=pltpu.PrefetchScalarGridSpec(
            num_scalar_prefetch=1,
            grid=(vocab // step,),
            in_specs=[
                pl.BlockSpec((step, features), lambda i, place: (i, 0)),
                pl.BlockSpec((1, part), lambda i, place: (0, place[1])),
                pl.BlockSpec((step, part), lambda i, place: (i, place[1])),
                anywhere,
            ],
            out_specs=pl.BlockSpec((step, part), lambda i, place: (i, 0)),
        ),
        compiler_params=pltpu.CompilerParams(vmem_limit_bytes=16 * MIB),
    )(place, embed_table, norm_gain.reshape(1, features), embed_table, gathered[1])

    inner_fetched = [lax.ppermute(rows_part, "ctx", inner) for rows_part in offered]
    amp = residue * jnp.sqrt(-jnp.expm1(-2.0 * pole_rate))
    across = (LANES // pole_rate.shape[1] + 1) * CHUNK
    matrices, lines = called(
        prepare_kernel,
        [
            shaped(CHUNK, 2 * across + 2 * CHUNK, dtype=bf16),
            shaped(LANES + 8 * (branches + 1), LANES),
        ],
        (place,),
        pole_rate.T,
        amp.T,
        short_filter.transpose(0, 2, 1),
        skip_gain.reshape(-1, LANES),
        earlier=(gathered[1],),
    )

    table_rows = branches * (vocab // 2)
    keep, send = called(
        partial_kernel,
        [shaped(table_rows, LANES), shaped(table_rows + SPARE, LANES, dtype=bf16)],
        (place,),
        normed,
        *gathered,
        earlier=(matrices, *inner_fetched),
    )
    arrived = swapped(send, "ctx", members)
    own = (keep + arrived[:table_rows].astype(f32)).astype(bf16)
    own = own.reshape(branches, vocab // 2, LANES)
    other = swapped(own, "groups", 1)
    span = length // 2
    *pieces, picked = called(
        functools.partial(conv_kernel, genomes=genomes, rows=rows),
        [shaped(span, LANES, dtype=bf16)] * 4 + [shaped(span, vocab, dtype=bf16)],
        (place,),
        send,
        arrived,
        own,
        other,
        matrices,
        lines,
        scratch=[pltpu.VMEM((genomes * length, vocab), bf16), pltpu.VMEM((genomes * length, LANES), bf16)],
    )
    core_piece = swapped(pieces[1], "chan", 1)
    piece = jnp.stack(
        [
            pieces[0],
            core_piece,
            swapped(pieces[2], "ctx", members),
            swapped_both(pieces[3], members),
        ]
    )
    gated = [piece] + [swapped(piece, "ctx", m) for m in range(1, members)]

    outer_fetched = [lax.ppermute(after(rows_part, own), "ctx", outer) for rows_part in offered]
    fetched = jnp.where(
        (ctx >= members // 2) & (ctx < members + members // 2),
        jnp.concatenate(inner_fetched),
        jnp.concatenate(outer_fetched),
    )
    fetched = after(fetched, piece)
    shared = swapped(fetched, "groups", 1)
    for ready in gated[1:]:
        shared = after(shared, ready)
    near, joined = called(
        near_kernel,
        [shaped(span, width, dtype=bf16), shaped(4 * 2, span, 2 * LANES, dtype=bf16)],
        (place,),
        picked,
        embed_table,
        *gated,
        output_proj,
        swapped(output_proj, "chan", 1),
        mib=24,
    )
    results = called(
        far_kernel,
        shaped(2, span, width, dtype=bf16),
        (place,),
        picked,
        embed_table,
        near,
        joined,
        fetched,
        swapped(fetched, "chan", 1),
        shared,
        swapped(shared, "chan", 1),
        mib=24,
    )
    both = jnp.stack([results[0], swapped(results[1], "chan", 1)])

    def rows_of(member):
        return lax.dynamic_slice_in_dim(both, member * rows, rows, 1)

    arrived = [rows_of(quad)] + [swapped(rows_of(quad ^ m), "ctx", m) for m in range(1, members)]
    return called(
        place_kernel, shaped(genomes, rows, members * width, dtype=bf16), (place,), *arrived
    )


def solution(mesh):
    sizes = tuple(mesh.shape[name] for name in ("groups", "ctx", "chan"))
    return jax.shard_map(
        quad_body if sizes == (2, 8, 2) else general_body,
        mesh=mesh,
        in_specs=(
            P("groups", "ctx"),
            P(),
            P(),
            P("ctx", None, "chan"),
            P(None, "chan", None),
            P("chan", None),
            P("chan", None),
            P("chan"),
            P("chan", "ctx"),
        ),
        out_specs=P("groups", "ctx", "chan"),
        check_vma=False,
    )
```

```python
import functools

import jax
import jax.numpy as jnp
from jax import lax
from jax.experimental import pallas as pl
from jax.experimental.pallas import tpu as pltpu
from jax.sharding import PartitionSpec as P

epsilon = 1e-06
highest = lax.Precision.HIGHEST
f32 = jnp.float32
bf16 = jnp.bfloat16
CHUNK = 128
LANES = 128
MIB = 1024 * 1024
SPARE = 16


def passed_along(shard, axis, by):
    count = lax.axis_size(axis)
    pairs = [(i, i + by) for i in range(count) if 0 <= i + by < count]
    return lax.ppermute(shard, axis, pairs)


def entering(shard, axis, combine, identity):
    count, mine = (lax.axis_size(axis), lax.axis_index(axis))
    everything = jax.tree.map(lambda part: lax.all_gather(part, axis), shard)
    start = jax.tree.map(
        lambda part, zero: jnp.broadcast_to(jnp.asarray(zero, part.dtype), part.shape),
        shard,
        identity,
    )

    def hop(k, before):
        reached = k < mine
        new = combine(before, jax.tree.map(lambda part: part[k], everything))
        return jax.tree.map(lambda a, b: jnp.where(reached, a, b), new, before)

    return lax.fori_loop(0, count, hop, start)


def local_block(operands):
    rising, falling, inputs = operands
    length = rising.shape[2]
    toeplitz = jnp.einsum("gnt,gns->gts", rising, falling, precision=highest)
    causal = jnp.arange(length)[:, None] >= jnp.arange(length)[None, :]
    toeplitz = jnp.where(causal[None], toeplitz, 0.0)
    return jnp.einsum("gms,gts->gmt", inputs, toeplitz, precision=highest)


def lookup_rows(token_block, embed_table):
    vocab_count = embed_table.shape[0]
    onehot = (token_block[:, None] == jnp.arange(vocab_count, dtype=jnp.int32)[None, :]).astype(
        jnp.bfloat16
    )
    return jnp.dot(onehot, embed_table, preferred_element_type=jnp.float32)


def general_body(
    tokens,
    embed_table,
    norm_gain,
    input_proj,
    short_filter,
    pole_rate,
    residue,
    skip_gain,
    output_proj,
):
    genome_count, row_count = tokens.shape
    part_rows, branch_count, channels = input_proj.shape
    groups = pole_rate.shape[0]
    group_size = channels // groups
    tap_count = short_filter.shape[2]
    flat_count = genome_count * row_count
    flat_tokens = tokens.reshape(flat_count)
    widened = lookup_rows(flat_tokens, embed_table)
    inv_rms = lax.rsqrt(jnp.mean(widened * widened, axis=-1, keepdims=True) + epsilon)
    normed = (widened * inv_rms * norm_gain).astype(jnp.bfloat16)
    proj_cols = branch_count * channels
    flat_weight = input_proj.reshape(part_rows, proj_cols)
    spread = lax.all_to_all(normed, "ctx", split_axis=1, concat_axis=0, tiled=True)
    summed = lax.psum_scatter(
        jnp.dot(spread, flat_weight, preferred_element_type=jnp.float32),
        "ctx",
        scatter_dimension=0,
        tiled=True,
    )
    projected = summed.astype(jnp.bfloat16).reshape(genome_count, row_count, branch_count, channels)
    rim = passed_along(projected[:, row_count - (tap_count - 1) :], "ctx", 1)
    extended = jnp.concatenate([rim, projected], axis=1).astype(jnp.float32)
    taps_full = jnp.broadcast_to(
        short_filter[:, :, None, :], (branch_count, groups, group_size, tap_count)
    ).reshape(branch_count, channels, tap_count)
    filtered = jnp.zeros((genome_count, row_count, branch_count, channels), jnp.float32)
    for lag in range(tap_count):
        first_row = tap_count - 1 - lag
        filtered = filtered + taps_full[:, :, lag] * extended[:, first_row : first_row + row_count]
    query_part = filtered[:, :, 0]
    product = filtered[:, :, 1] * filtered[:, :, 2]
    mixes = genome_count * group_size
    grouped = (
        product.reshape(genome_count, row_count, groups, group_size)
        .transpose(2, 0, 3, 1)
        .reshape(groups, mixes, row_count)
    )
    positions = jnp.arange(row_count, dtype=jnp.float32)
    middle = float(row_count // 2)
    powers = jnp.exp(-pole_rate[:, :, None] * positions)
    next_powers = jnp.exp(-pole_rate[:, :, None] * (positions + 1.0))
    pole_amp = residue * jnp.sqrt(-jnp.expm1(-2.0 * pole_rate))
    rising = pole_amp[:, :, None] * jnp.exp(-pole_rate[:, :, None] * (positions - middle))
    falling = jnp.exp(-pole_rate[:, :, None] * (middle - positions))
    block_size = 8
    blocks = groups // block_size
    poles = pole_rate.shape[1]
    local_part = lax.map(
        local_block,
        (
            rising.reshape(blocks, block_size, poles, row_count),
            falling.reshape(blocks, block_size, poles, row_count),
            grouped.reshape(blocks, block_size, mixes, row_count),
        ),
    )
    local_part = local_part.reshape(groups, mixes, row_count)
    end_state = jnp.einsum("gms,gns->gmn", grouped, powers[:, :, ::-1], precision=highest)
    block_decay = jnp.exp(-pole_rate * row_count)

    def combine(earlier, later):
        return (earlier[0] * later[0], later[0][:, None, :] * earlier[1] + later[1])

    identity = (jnp.ones_like(block_decay), jnp.zeros_like(end_state))
    incoming = entering((block_decay, end_state), "ctx", combine, identity)[1]
    weighted = incoming * pole_amp[:, None, :]
    correction = jnp.einsum("gmn,gnt->gmt", weighted, next_powers, precision=highest)
    long_conv = (
        (local_part + correction)
        .reshape(groups, genome_count, group_size, row_count)
        .transpose(1, 3, 0, 2)
        .reshape(genome_count, row_count, channels)
    )
    gated = (
        (query_part * (long_conv + skip_gain * product))
        .astype(jnp.bfloat16)
        .reshape(flat_count, channels)
    )
    partial_value = jnp.dot(
        gated,
        lax.all_gather(output_proj, "ctx", axis=1, tiled=True),
        preferred_element_type=jnp.float32,
    )
    own_share = lax.psum_scatter(partial_value, "chan", scatter_dimension=1, tiled=True)
    half_width = own_share.shape[1]
    residual_part = lax.dynamic_slice_in_dim(
        widened, lax.axis_index("chan") * half_width, half_width, 1
    )
    block_out = (residual_part + own_share).astype(jnp.bfloat16)
    return block_out.reshape(genome_count, row_count, half_width)


def swapped(value, axis, mask):
    count = lax.axis_size(axis)
    return lax.ppermute(value, axis, [(i, i ^ mask) for i in range(count)])


def swapped_both(value, ctx_mask):
    count, cores = lax.axis_size("ctx"), lax.axis_size("chan")
    pairs = [
        (i * cores + c, (i ^ ctx_mask) * cores + (c ^ 1)) for i in range(count) for c in range(cores)
    ]
    return lax.ppermute(value, ("ctx", "chan"), pairs)


def split(value):
    high = value.astype(bf16)
    return high, (value - high.astype(f32)).astype(bf16)


def dot3(a_high, a_low, b):
    b_high, b_low = split(b)
    total = jnp.dot(a_high, b_high, preferred_element_type=f32)
    total += jnp.dot(a_low, b_high, preferred_element_type=f32)
    return total + jnp.dot(a_high, b_low, preferred_element_type=f32)


def lane_half(shape):
    return lax.broadcasted_iota(jnp.int32, shape, len(shape) - 1) < LANES // 2


def half_turn(value):
    return pltpu.roll(value, LANES // 2, value.ndim - 1)


def norm_kernel(place_ref, table_ref, gain_ref, part_ref, pair_ref, query_ref, out_ref):
    del place_ref, pair_ref, query_ref
    widened = table_ref[...].astype(f32)
    mean = jnp.sum(widened * widened, axis=1, keepdims=True) / widened.shape[1]
    own = part_ref[...].astype(f32)
    out_ref[...] = (own * lax.rsqrt(mean + epsilon) * gain_ref[...]).astype(bf16)


def pack_kernel(token_ref, weight_ref, *refs):
    out_refs, sems = refs[:-1], refs[-1]
    branches, depth, channels = weight_ref.shape
    members = len(out_refs)
    quad, group = lax.axis_index("ctx") % members, lax.axis_index("groups")
    block = channels // members
    copies = []
    for m in (1, 2, 3, 0):
        first = pl.multiple_of((quad ^ m) * block + group * LANES, LANES)
        for j in range(branches):
            copies.append(
                pltpu.make_async_copy(
                    weight_ref.at[j, :, pl.ds(first, LANES)],
                    out_refs[m].at[pl.ds((j + 2) % 3 * depth, depth), :],
                    sems.at[m, j],
                )
            )
            copies[-1].start()
    rows = token_ref.shape[1]
    row = lax.broadcasted_iota(jnp.int32, (SPARE, rows), 0)
    token = jnp.where(row % 4 < 2, token_ref[0:1, :], token_ref[1:2, :])
    token = jnp.where(row % 2 == 0, token >> 8, token & 255)
    token = jnp.where(row // 4 == quad, token, 0).astype(f32).astype(bf16)
    for out_ref in out_refs:
        out_ref[branches * depth :, :] = jnp.zeros((SPARE, LANES), bf16)
        out_ref[branches * depth :, :rows] = token
    for copy in copies:
        copy.wait()


def pick(half, near_ref, far_ref, picked_ref, genomes, rows):
    vocab = picked_ref.shape[1]
    length = picked_ref.shape[0] // genomes
    first = near_ref.shape[0] - SPARE
    diagonal = lax.broadcasted_iota(jnp.int32, (rows, rows), 0) == lax.broadcasted_iota(
        jnp.int32, (rows, rows), 1
    )
    entries = lax.broadcasted_iota(jnp.int32, (rows, vocab), 1).astype(f32)
    for other, ref in enumerate((near_ref, far_ref)):
        parts = ref[first:, :rows].astype(f32)
        for member in range(length // (2 * rows)):
            for b in range(genomes):
                at = 4 * member + 2 * b
                line = parts[at : at + 1] * 256.0 + parts[at + 1 : at + 2]
                column = jnp.sum(jnp.where(diagonal, line, 0.0), axis=1, keepdims=True)
                place = b * length + (half ^ other) * (length // 2) + member * rows
                picked_ref[pl.ds(pl.multiple_of(place, rows), rows), :] = (
                    (column == entries).astype(f32).astype(bf16)
                )


def prepare_kernel(place_ref, rate_ref, amp_ref, taps_ref, skip_ref, matrices_ref, rows_ref):
    quad, half = place_ref[0], place_ref[1]

    group_count = rate_ref.shape[1]
    poles = rate_ref.shape[0]
    count = LANES // poles

    def group_at(lane):
        place = lane // poles
        return quad * (2 * count) + (place // (count // 2)) * count + half * (count // 2) + place % (count // 2)

    lane = lax.broadcasted_iota(jnp.int32, (group_count, LANES), 1)
    chosen = (lax.broadcasted_iota(jnp.int32, (group_count, LANES), 0) == group_at(lane)).astype(f32)
    turned_lane = lax.broadcasted_iota(jnp.int32, (LANES, group_count), 0)
    turned = (lax.broadcasted_iota(jnp.int32, (LANES, group_count), 1) == group_at(turned_lane)).astype(f32)

    def along_lanes(ref):
        spread = jnp.dot(ref[...], chosen, precision=highest, preferred_element_type=f32)
        keep = lax.broadcasted_iota(jnp.int32, spread.shape, 0) == lax.broadcasted_iota(
            jnp.int32, spread.shape, 1
        ) % poles
        return jnp.sum(jnp.where(keep, spread, 0.0), axis=0, keepdims=True)

    rate, amp = along_lanes(rate_ref), along_lanes(amp_ref)
    spread = lax.dot_general(
        turned, rate_ref[...], (((1,), (1,)), ((), ())), precision=highest, preferred_element_type=f32
    )
    keep = lax.broadcasted_iota(jnp.int32, spread.shape, 1) == lax.broadcasted_iota(
        jnp.int32, spread.shape, 0
    ) % poles
    rate_col = jnp.sum(jnp.where(keep, spread, 0.0), axis=1, keepdims=True)

    square = (CHUNK, LANES)
    row = lax.broadcasted_iota(jnp.int32, square, 0)
    col = lax.broadcasted_iota(jnp.int32, square, 1)
    at = row.astype(f32)
    middle = float(CHUNK // 2)
    rising = amp * jnp.exp(-rate * (at - middle))
    falling = jnp.exp(-rate * (middle - at))
    width = (count + 1) * CHUNK
    for g in range(count):
        own = jnp.where(col // poles == g, falling, 0.0)
        block = lax.dot_general(
            rising, own, (((1,), (1,)), ((), ())), precision=highest, preferred_element_type=f32
        )
        high, low = split(jnp.where(row >= col, block, 0.0))
        matrices_ref[:, g * CHUNK : (g + 1) * CHUNK] = high
        matrices_ref[:, width + g * CHUNK : width + (g + 1) * CHUNK] = low
    high, low = split(amp * jnp.exp(-rate * (at + 1.0)))
    matrices_ref[:, count * CHUNK : width] = high
    matrices_ref[:, width + count * CHUNK : 2 * width] = low
    high, low = split(jnp.exp(-rate_col * (float(CHUNK - 1) - col.astype(f32))))
    matrices_ref[:, 2 * width : 2 * width + CHUNK] = high
    matrices_ref[:, 2 * width + CHUNK :] = low

    rows_ref[:LANES] = jnp.exp(-rate_col * float(CHUNK)) + jnp.zeros(square, f32)
    branches = taps_ref.shape[0]
    for j in range(branches):
        taps = jnp.dot(taps_ref[j], chosen, precision=highest, preferred_element_type=f32)
        rows_ref[LANES + 8 * j : LANES + 8 * j + taps.shape[0]] = taps
    upper = skip_ref[pl.ds(2 * quad, 1), :]
    lower = skip_ref[pl.ds(2 * quad + 1, 1), :]
    upper = jnp.where(half == 0, upper, half_turn(upper))
    lower = jnp.where(half == 1, lower, half_turn(lower))
    end = LANES + 8 * branches
    rows_ref[end : end + 1] = jnp.where(lane_half(upper.shape), upper, lower)


def partial_kernel(place_ref, normed_ref, *refs, begin, count):
    weight_refs, (keep_ref, send_ref) = refs[:-2], refs[-2:]
    quad, half = place_ref[0], place_ref[1]
    rows, features = normed_ref.shape
    depth = features // len(weight_refs)
    total = jnp.zeros((rows, count * LANES), f32)
    tokens = jnp.zeros((SPARE, LANES), f32)
    for m, weight_ref in enumerate(weight_refs):
        first = pl.multiple_of((quad ^ m) * depth, depth)
        columns = jnp.concatenate(
            [weight_ref[j * depth : (j + 1) * depth, :] for j in range(begin, begin + count)], axis=1
        )
        total += jnp.dot(
            normed_ref[:, pl.ds(first, depth)], columns, preferred_element_type=f32
        )
        tokens += weight_ref[weight_ref.shape[0] - SPARE :, :].astype(f32)
    part = rows // 2
    for j in range(count):
        mine = total[:, j * LANES : (j + 1) * LANES]
        mine = jnp.where(half == 0, mine, half_turn(mine))
        top, bottom = mine[:part], mine[part:]
        left = lane_half(top.shape)
        keep_ref[j * part : (j + 1) * part, :] = jnp.where(left, top, half_turn(bottom))
        send_ref[j * part : (j + 1) * part, :] = jnp.where(left, half_turn(top), bottom).astype(bf16)
    if send_ref.shape[0] > count * part:
        send_ref[count * part :, :] = tokens.astype(bf16)


def filtered_branch(group, picked, row, mine, theirs, rows_ref, branch):
    mine, theirs = mine.astype(f32), theirs.astype(f32)
    first = jnp.where(group == 0, mine, theirs)
    second = jnp.where(group == 0, theirs, mine)
    left = lane_half(first.shape)
    top = jnp.where(left, first, half_turn(second))
    bottom = jnp.where(left, half_turn(first), second)
    table = jnp.concatenate([top, bottom], axis=0).astype(bf16)
    now = jnp.dot(picked, table, preferred_element_type=f32)
    first_tap = LANES + 8 * branch
    total = rows_ref[first_tap : first_tap + 1] * now
    for lag in range(1, 3):
        late = jnp.where(row >= lag, pltpu.roll(now, lag, 0), 0.0)
        total += rows_ref[first_tap + lag : first_tap + lag + 1] * late
    return total


def conv_kernel(
    place_ref, near_ref, far_ref, own_ref, other_ref, matrices_ref, rows_ref, value_ref, picked_ref, *, genomes, rows
):
    half, group = place_ref[1], place_ref[2]
    pick(half, near_ref, far_ref, picked_ref, genomes, rows)
    positions = picked_ref.shape[0]
    length = positions // genomes
    row = lax.broadcasted_iota(jnp.int32, (positions, LANES), 0) % length
    picked = picked_ref[...]
    key, value = (
        filtered_branch(group, picked, row, own_ref[j - 1], other_ref[j - 1], rows_ref, j)
        for j in (1, 2)
    )
    product = key * value
    size = 16
    count = LANES // size
    width = genomes * LANES
    lane = lax.broadcasted_iota(jnp.int32, (CHUNK, width), 1) % LANES
    pole_row = lax.broadcasted_iota(jnp.int32, (LANES, width), 0)
    same = pole_row // size == (lax.broadcasted_iota(jnp.int32, (LANES, width), 1) % LANES) // size
    fade = jnp.concatenate([rows_ref[:LANES]] * genomes, axis=1)
    skip = rows_ref[rows_ref.shape[0] - 8 : rows_ref.shape[0] - 7]
    across = (count + 1) * CHUNK
    high, low = matrices_ref[:, :across], matrices_ref[:, across : 2 * across]
    ends_high = matrices_ref[:, 2 * across : 2 * across + CHUNK]
    ends_low = matrices_ref[:, 2 * across + CHUNK :]
    state = jnp.zeros((LANES, width), f32)
    chunks = length // CHUNK
    for c in range(chunks):
        spans = [slice(b * length + c * CHUNK, b * length + (c + 1) * CHUNK) for b in range(genomes)]
        block = jnp.concatenate([product[span] for span in spans], axis=1)
        stacked = jnp.concatenate(
            [jnp.where(lane // size == g, block, 0.0) for g in range(count)] + [state], axis=0
        )
        conv = dot3(high, low, stacked)
        for b, span in enumerate(spans):
            value_ref[span, :] = conv[:, b * LANES : (b + 1) * LANES] + skip * product[span]
        if c < chunks - 1:
            ends = dot3(ends_high, ends_low, block)
            state = fade * state + jnp.where(same, ends, 0.0)


def gate_kernel(place_ref, picked_ref, own_ref, other_ref, rows_ref, value_ref, *refs, genomes):
    piece_refs, (mine_ref, held_ref) = refs[:4], refs[4:]
    half, group, core = place_ref[1], place_ref[2], place_ref[3]
    positions = picked_ref.shape[0]
    length = positions // genomes
    row = lax.broadcasted_iota(jnp.int32, (positions, LANES), 0) % length
    query = filtered_branch(group, picked_ref[...], row, own_ref[0], other_ref[0], rows_ref, 0)
    held_ref[...] = (query * value_ref[...]).astype(bf16)
    part = length // 2
    for r, piece_ref in enumerate(piece_refs):
        place = 2 * (core ^ (r % 2)) + (half ^ (r // 2))
        piece_ref[...] = held_ref[pl.ds(pl.multiple_of(place * part, part), part), :]
    mine_ref[...] = picked_ref[pl.ds(pl.multiple_of((2 * core + half) * part, part), part), :]


def offer_kernel(place_ref, rows_ref, packed_ref, first_ref, second_ref):
    del place_ref, packed_ref
    count = first_ref.shape[0]
    first_ref[...] = rows_ref[:count]
    second_ref[...] = rows_ref[count:]


def residual(picked_ref, table_ref, first, width):
    return jnp.dot(
        picked_ref[...],
        table_ref[:, pl.ds(pl.multiple_of(first, width), width)],
        preferred_element_type=f32,
    )


def near_kernel(place_ref, picked_ref, table_ref, *refs):
    piece_refs, (own_ref, core_ref, out_ref, joined_ref) = refs[:4], refs[4:]
    quad, half = place_ref[0], place_ref[1]
    block = 2 * LANES
    for m, piece_ref in enumerate(piece_refs):
        for other_core in (0, 1):
            near = piece_ref[other_core].astype(f32)
            far = piece_ref[2 + other_core].astype(f32)
            first = jnp.where(half == 0, near, far)
            second = jnp.where(half == 0, far, near)
            left = lane_half(first.shape)
            pair = [
                jnp.where(left, first, half_turn(second)),
                jnp.where(left, half_turn(first), second),
            ]
            joined_ref[2 * (quad ^ m) + other_core] = jnp.concatenate(pair, axis=1).astype(bf16)
    width = own_ref.shape[1]
    total = jnp.zeros(out_ref.shape, f32)
    for member in range(4):
        rows = slice(member * block, (member + 1) * block)
        for other_core, ref in enumerate((own_ref, core_ref)):
            total += jnp.dot(
                joined_ref[2 * member + other_core], ref[rows, :], preferred_element_type=f32
            )
    total += residual(picked_ref, table_ref, (4 * half + quad) * width, width)
    out_ref[...] = total.astype(bf16)


def far_kernel(place_ref, picked_ref, table_ref, near_ref, joined_ref, *refs):
    far_refs, out_ref = (refs[:2], refs[2:4]), refs[4]
    quad, half, group, core = (place_ref[i] for i in range(4))
    block = 2 * LANES
    width = near_ref.shape[1]
    total = jnp.zeros(near_ref.shape, f32)
    for member in range(4):
        rows = slice((member % 2) * block, (member % 2 + 1) * block)
        for other_core in (0, 1):
            source = 2 * (2 * (group ^ (member // 2)) + member % 2) + other_core
            total += jnp.dot(
                joined_ref[source],
                far_refs[member // 2][other_core][rows, :],
                preferred_element_type=f32,
            )
    total += residual(picked_ref, table_ref, (4 * (half ^ 1) + (quad ^ 2)) * width, width)
    out_ref[half ^ core] = near_ref[...]
    out_ref[half ^ 1 ^ core] = total.astype(bf16)


def place_kernel(place_ref, *refs):
    piece_refs, out_ref = refs[:4], refs[4]
    quad, half, core = place_ref[0], place_ref[1], place_ref[3]
    width = piece_refs[0].shape[2]
    for m, piece_ref in enumerate(piece_refs):
        first = pl.multiple_of((quad ^ m ^ (2 * (half ^ core))) * width, width)
        for g in (0, 1):
            out_ref[core ^ g, :, pl.ds(first, width)] = piece_ref[g]


def called(kernel, out_shape, scalars, *operands, scratch=(), mib=16, earlier=()):
    smem = pl.BlockSpec(memory_space=pltpu.SMEM)
    vmem = pl.BlockSpec(memory_space=pltpu.VMEM)
    anywhere = pl.BlockSpec(memory_space=pl.ANY)
    many = isinstance(out_shape, (list, tuple))
    inputs, waits = len(scalars) + len(operands), len(earlier)

    def body(*refs):
        kernel(*refs[:inputs], *refs[inputs + waits :])

    return pl.pallas_call(
        body,
        out_shape=out_shape,
        in_specs=[smem] * len(scalars) + [vmem] * len(operands) + [anywhere] * waits,
        out_specs=[vmem] * len(out_shape) if many else vmem,
        scratch_shapes=scratch,
        compiler_params=pltpu.CompilerParams(vmem_limit_bytes=mib * MIB),
    )(*scalars, *operands, *earlier)


def shaped(*shape, dtype=f32):
    return jax.ShapeDtypeStruct(shape, dtype)


def pass_kernel(*refs):
    del refs


def after(value, earlier):
    return pl.pallas_call(
        pass_kernel,
        out_shape=shaped(*value.shape, dtype=value.dtype),
        in_specs=[pl.BlockSpec(memory_space=pl.ANY)] * 2,
        out_specs=pl.BlockSpec(memory_space=pl.ANY),
        input_output_aliases={0: 0},
        compiler_params=pltpu.CompilerParams(vmem_limit_bytes=MIB),
    )(value, earlier)


def quad_body(
    tokens,
    embed_table,
    norm_gain,
    input_proj,
    short_filter,
    pole_rate,
    residue,
    skip_gain,
    output_proj,
):
    genomes, rows = tokens.shape
    depth, branches, channels = input_proj.shape
    vocab, features = embed_table.shape
    members = lax.axis_size("ctx") // 2
    ctx, core, group = (lax.axis_index(name) for name in ("ctx", "chan", "groups"))
    quad, half = ctx % members, ctx // members
    place = jnp.stack([quad, half, group, core]).astype(jnp.int32)
    block = channels // members

    weights = input_proj.transpose(1, 0, 2)
    anywhere = pl.BlockSpec(memory_space=pl.ANY)
    packed = pl.pallas_call(
        pack_kernel,
        out_shape=[shaped(branches * depth + SPARE, LANES, dtype=bf16)] * members,
        in_specs=[pl.BlockSpec(memory_space=pltpu.VMEM), anywhere],
        out_specs=[pl.BlockSpec(memory_space=pltpu.VMEM)] * members,
        scratch_shapes=[pltpu.SemaphoreType.DMA((members, branches))],
        compiler_params=pltpu.CompilerParams(vmem_limit_bytes=61 * MIB),
    )(tokens, weights)
    gathered = [packed[0]] + [swapped(packed[m], "ctx", m) for m in range(1, members)]
    length = 2 * members * rows

    half_rows = output_proj.shape[0] // 2
    width = output_proj.shape[1]
    offered = pl.pallas_call(
        offer_kernel,
        out_shape=[shaped(half_rows // 2, width, dtype=bf16)] * 2,
        grid_spec=pltpu.PrefetchScalarGridSpec(
            num_scalar_prefetch=1,
            grid=(1,),
            in_specs=[pl.BlockSpec((half_rows, width), lambda i, place: (place[2], 0)), anywhere],
            out_specs=[pl.BlockSpec((half_rows // 2, width), lambda i, place: (0, 0))] * 2,
        ),
        compiler_params=pltpu.CompilerParams(vmem_limit_bytes=4 * MIB),
    )(place, output_proj, packed[1])
    count = 2 * members
    inner = [(i, count - 2 - i + 2 * (i % 2)) for i in range(members // 2, members + members // 2)]
    outer = [
        (i, count - 2 - i + 2 * (i % 2))
        for i in range(count)
        if not members // 2 <= i < members + members // 2
    ]

    part = features // 2
    step = 128
    normed = pl.pallas_call(
        norm_kernel,
        out_shape=shaped(vocab, part, dtype=bf16),
        grid_spec=pltpu.PrefetchScalarGridSpec(
            num_scalar_prefetch=1,
            grid=(vocab // step,),
            in_specs=[
                pl.BlockSpec((step, features), lambda i, place: (i, 0)),
                pl.BlockSpec((1, part), lambda i, place: (0, place[1])),
                pl.BlockSpec((step, part), lambda i, place: (i, place[1])),
                anywhere,
                anywhere,
            ],
            out_specs=pl.BlockSpec((step, part), lambda i, place: (i, 0)),
        ),
        compiler_params=pltpu.CompilerParams(vmem_limit_bytes=16 * MIB),
    )(place, embed_table, norm_gain.reshape(1, features), embed_table, gathered[1], packed[1])

    inner_fetched = [lax.ppermute(rows_part, "ctx", inner) for rows_part in offered]
    def partials(begin, count, spare, earlier=()):
        table_rows = count * (vocab // 2)
        return called(
            functools.partial(partial_kernel, begin=begin, count=count),
            [shaped(table_rows, LANES), shaped(table_rows + spare, LANES, dtype=bf16)],
            (place,),
            normed,
            *gathered,
            earlier=earlier,
        )

    def finished(keep, arrived):
        own = (keep + arrived[: keep.shape[0]].astype(f32)).astype(bf16)
        return own.reshape(-1, vocab // 2, LANES)

    pair_keep, pair_send = partials(0, 2, SPARE, tuple(inner_fetched))
    query_keep, query_send = partials(2, 1, 0)
    pair_arrived = swapped(pair_send, "ctx", members)
    query_arrived = swapped(query_send, "ctx", members)
    amp = residue * jnp.sqrt(-jnp.expm1(-2.0 * pole_rate))
    across = (LANES // pole_rate.shape[1] + 1) * CHUNK
    matrices, lines = called(
        prepare_kernel,
        [
            shaped(CHUNK, 2 * across + 2 * CHUNK, dtype=bf16),
            shaped(LANES + 8 * (branches + 1), LANES),
        ],
        (place,),
        pole_rate.T,
        amp.T,
        short_filter.transpose(0, 2, 1),
        skip_gain.reshape(-1, LANES),
        earlier=(pair_send,),
    )

    pair_own = after(finished(pair_keep, pair_arrived), matrices)
    query_own = finished(query_keep, query_arrived)
    pair_other = swapped(pair_own, "groups", 1)
    query_other = swapped(query_own, "groups", 1)

    span = length // 2
    value, picked = called(
        functools.partial(conv_kernel, genomes=genomes, rows=rows),
        [shaped(genomes * length, LANES), shaped(genomes * length, vocab, dtype=bf16)],
        (place,),
        pair_send,
        pair_arrived,
        pair_own,
        pair_other,
        matrices,
        lines,
    )
    *pieces, picked = called(
        functools.partial(gate_kernel, genomes=genomes),
        [shaped(span, LANES, dtype=bf16)] * 4 + [shaped(span, vocab, dtype=bf16)],
        (place,),
        picked,
        query_own,
        query_other,
        lines,
        value,
        scratch=[pltpu.VMEM((genomes * length, LANES), bf16)],
    )
    core_piece = swapped(pieces[1], "chan", 1)
    piece = jnp.stack(
        [
            pieces[0],
            core_piece,
            swapped(pieces[2], "ctx", members),
            swapped_both(pieces[3], members),
        ]
    )
    gated = [piece] + [swapped(piece, "ctx", m) for m in range(1, members)]

    outer_fetched = [lax.ppermute(after(rows_part, pair_own), "ctx", outer) for rows_part in offered]
    fetched = jnp.where(
        (ctx >= members // 2) & (ctx < members + members // 2),
        jnp.concatenate(inner_fetched),
        jnp.concatenate(outer_fetched),
    )
    fetched = after(fetched, piece)
    shared = swapped(fetched, "groups", 1)
    for ready in gated[1:]:
        shared = after(shared, ready)
    near, joined = called(
        near_kernel,
        [shaped(span, width, dtype=bf16), shaped(4 * 2, span, 2 * LANES, dtype=bf16)],
        (place,),
        picked,
        embed_table,
        *gated,
        output_proj,
        swapped(output_proj, "chan", 1),
        mib=24,
    )
    results = called(
        far_kernel,
        shaped(2, span, width, dtype=bf16),
        (place,),
        picked,
        embed_table,
        near,
        joined,
        fetched,
        swapped(fetched, "chan", 1),
        shared,
        swapped(shared, "chan", 1),
        mib=24,
    )
    both = jnp.stack([results[0], swapped(results[1], "chan", 1)])

    def rows_of(member):
        return lax.dynamic_slice_in_dim(both, member * rows, rows, 1)

    arrived = [rows_of(quad)] + [swapped(rows_of(quad ^ m), "ctx", m) for m in range(1, members)]
    return called(
        place_kernel, shaped(genomes, rows, members * width, dtype=bf16), (place,), *arrived
    )


def solution(mesh):
    sizes = tuple(mesh.shape[name] for name in ("groups", "ctx", "chan"))
    return jax.shard_map(
        quad_body if sizes == (2, 8, 2) else general_body,
        mesh=mesh,
        in_specs=(
            P("groups", "ctx"),
            P(),
            P(),
            P("ctx", None, "chan"),
            P(None, "chan", None),
            P("chan", None),
            P("chan", None),
            P("chan"),
            P("chan", "ctx"),
        ),
        out_specs=P("groups", "ctx", "chan"),
        check_vma=False,
    )
```

```python
import functools

import jax
import jax.numpy as jnp
from jax import lax
from jax.experimental import pallas as pl
from jax.experimental.pallas import tpu as pltpu
from jax.sharding import PartitionSpec as P

epsilon = 1e-06
highest = lax.Precision.HIGHEST
f32 = jnp.float32
bf16 = jnp.bfloat16
CHUNK = 128
LANES = 128
MIB = 1024 * 1024
SPARE = 16


def passed_along(shard, axis, by):
    count = lax.axis_size(axis)
    pairs = [(i, i + by) for i in range(count) if 0 <= i + by < count]
    return lax.ppermute(shard, axis, pairs)


def entering(shard, axis, combine, identity):
    count, mine = (lax.axis_size(axis), lax.axis_index(axis))
    everything = jax.tree.map(lambda part: lax.all_gather(part, axis), shard)
    start = jax.tree.map(
        lambda part, zero: jnp.broadcast_to(jnp.asarray(zero, part.dtype), part.shape),
        shard,
        identity,
    )

    def hop(k, before):
        reached = k < mine
        new = combine(before, jax.tree.map(lambda part: part[k], everything))
        return jax.tree.map(lambda a, b: jnp.where(reached, a, b), new, before)

    return lax.fori_loop(0, count, hop, start)


def local_block(operands):
    rising, falling, inputs = operands
    length = rising.shape[2]
    toeplitz = jnp.einsum("gnt,gns->gts", rising, falling, precision=highest)
    causal = jnp.arange(length)[:, None] >= jnp.arange(length)[None, :]
    toeplitz = jnp.where(causal[None], toeplitz, 0.0)
    return jnp.einsum("gms,gts->gmt", inputs, toeplitz, precision=highest)


def lookup_rows(token_block, embed_table):
    vocab_count = embed_table.shape[0]
    onehot = (token_block[:, None] == jnp.arange(vocab_count, dtype=jnp.int32)[None, :]).astype(
        jnp.bfloat16
    )
    return jnp.dot(onehot, embed_table, preferred_element_type=jnp.float32)


def general_body(
    tokens,
    embed_table,
    norm_gain,
    input_proj,
    short_filter,
    pole_rate,
    residue,
    skip_gain,
    output_proj,
):
    genome_count, row_count = tokens.shape
    part_rows, branch_count, channels = input_proj.shape
    groups = pole_rate.shape[0]
    group_size = channels // groups
    tap_count = short_filter.shape[2]
    flat_count = genome_count * row_count
    flat_tokens = tokens.reshape(flat_count)
    widened = lookup_rows(flat_tokens, embed_table)
    inv_rms = lax.rsqrt(jnp.mean(widened * widened, axis=-1, keepdims=True) + epsilon)
    normed = (widened * inv_rms * norm_gain).astype(jnp.bfloat16)
    proj_cols = branch_count * channels
    flat_weight = input_proj.reshape(part_rows, proj_cols)
    spread = lax.all_to_all(normed, "ctx", split_axis=1, concat_axis=0, tiled=True)
    summed = lax.psum_scatter(
        jnp.dot(spread, flat_weight, preferred_element_type=jnp.float32),
        "ctx",
        scatter_dimension=0,
        tiled=True,
    )
    projected = summed.astype(jnp.bfloat16).reshape(genome_count, row_count, branch_count, channels)
    rim = passed_along(projected[:, row_count - (tap_count - 1) :], "ctx", 1)
    extended = jnp.concatenate([rim, projected], axis=1).astype(jnp.float32)
    taps_full = jnp.broadcast_to(
        short_filter[:, :, None, :], (branch_count, groups, group_size, tap_count)
    ).reshape(branch_count, channels, tap_count)
    filtered = jnp.zeros((genome_count, row_count, branch_count, channels), jnp.float32)
    for lag in range(tap_count):
        first_row = tap_count - 1 - lag
        filtered = filtered + taps_full[:, :, lag] * extended[:, first_row : first_row + row_count]
    query_part = filtered[:, :, 0]
    product = filtered[:, :, 1] * filtered[:, :, 2]
    mixes = genome_count * group_size
    grouped = (
        product.reshape(genome_count, row_count, groups, group_size)
        .transpose(2, 0, 3, 1)
        .reshape(groups, mixes, row_count)
    )
    positions = jnp.arange(row_count, dtype=jnp.float32)
    middle = float(row_count // 2)
    powers = jnp.exp(-pole_rate[:, :, None] * positions)
    next_powers = jnp.exp(-pole_rate[:, :, None] * (positions + 1.0))
    pole_amp = residue * jnp.sqrt(-jnp.expm1(-2.0 * pole_rate))
    rising = pole_amp[:, :, None] * jnp.exp(-pole_rate[:, :, None] * (positions - middle))
    falling = jnp.exp(-pole_rate[:, :, None] * (middle - positions))
    block_size = 8
    blocks = groups // block_size
    poles = pole_rate.shape[1]
    local_part = lax.map(
        local_block,
        (
            rising.reshape(blocks, block_size, poles, row_count),
            falling.reshape(blocks, block_size, poles, row_count),
            grouped.reshape(blocks, block_size, mixes, row_count),
        ),
    )
    local_part = local_part.reshape(groups, mixes, row_count)
    end_state = jnp.einsum("gms,gns->gmn", grouped, powers[:, :, ::-1], precision=highest)
    block_decay = jnp.exp(-pole_rate * row_count)

    def combine(earlier, later):
        return (earlier[0] * later[0], later[0][:, None, :] * earlier[1] + later[1])

    identity = (jnp.ones_like(block_decay), jnp.zeros_like(end_state))
    incoming = entering((block_decay, end_state), "ctx", combine, identity)[1]
    weighted = incoming * pole_amp[:, None, :]
    correction = jnp.einsum("gmn,gnt->gmt", weighted, next_powers, precision=highest)
    long_conv = (
        (local_part + correction)
        .reshape(groups, genome_count, group_size, row_count)
        .transpose(1, 3, 0, 2)
        .reshape(genome_count, row_count, channels)
    )
    gated = (
        (query_part * (long_conv + skip_gain * product))
        .astype(jnp.bfloat16)
        .reshape(flat_count, channels)
    )
    partial_value = jnp.dot(
        gated,
        lax.all_gather(output_proj, "ctx", axis=1, tiled=True),
        preferred_element_type=jnp.float32,
    )
    own_share = lax.psum_scatter(partial_value, "chan", scatter_dimension=1, tiled=True)
    half_width = own_share.shape[1]
    residual_part = lax.dynamic_slice_in_dim(
        widened, lax.axis_index("chan") * half_width, half_width, 1
    )
    block_out = (residual_part + own_share).astype(jnp.bfloat16)
    return block_out.reshape(genome_count, row_count, half_width)


def swapped(value, axis, mask):
    count = lax.axis_size(axis)
    return lax.ppermute(value, axis, [(i, i ^ mask) for i in range(count)])


def swapped_both(value, ctx_mask):
    count, cores = lax.axis_size("ctx"), lax.axis_size("chan")
    pairs = [
        (i * cores + c, (i ^ ctx_mask) * cores + (c ^ 1)) for i in range(count) for c in range(cores)
    ]
    return lax.ppermute(value, ("ctx", "chan"), pairs)


def split(value):
    high = value.astype(bf16)
    return high, (value - high.astype(f32)).astype(bf16)


def dot3(a_high, a_low, b):
    b_high, b_low = split(b)
    total = jnp.dot(a_high, b_high, preferred_element_type=f32)
    total += jnp.dot(a_low, b_high, preferred_element_type=f32)
    return total + jnp.dot(a_high, b_low, preferred_element_type=f32)


def lane_half(shape):
    return lax.broadcasted_iota(jnp.int32, shape, len(shape) - 1) < LANES // 2


def half_turn(value):
    return pltpu.roll(value, LANES // 2, value.ndim - 1)


def norm_kernel(place_ref, table_ref, gain_ref, part_ref, pair_ref, query_ref, out_ref):
    del place_ref, pair_ref, query_ref
    widened = table_ref[...].astype(f32)
    mean = jnp.sum(widened * widened, axis=1, keepdims=True) / widened.shape[1]
    own = part_ref[...].astype(f32)
    out_ref[...] = (own * lax.rsqrt(mean + epsilon) * gain_ref[...]).astype(bf16)


def pack_kernel(tokens_ref, weight_ref, *refs):
    out_refs, (held_ref, token_ref, token_sem, in_sems, out_sems) = refs[:-5], refs[-5:]
    branches, depth, channels = weight_ref.shape
    members = len(out_refs)
    quad, group = lax.axis_index("ctx") % members, lax.axis_index("groups")
    block = channels // members
    order = (1, 2, 3, 0)
    fetch = pltpu.make_async_copy(tokens_ref, token_ref, token_sem)
    fetch.start()
    copies = {}
    for m in order:
        first = pl.multiple_of((quad ^ m) * block + group * LANES, LANES)
        for i, j in enumerate((1, 2, 0)):
            copies[m, i] = pltpu.make_async_copy(
                weight_ref.at[j, :, pl.ds(first, LANES)],
                held_ref.at[m, pl.ds(i * depth, depth), :],
                in_sems.at[m, i],
            )
            copies[m, i].start()
    rows = token_ref.shape[1]
    row = lax.broadcasted_iota(jnp.int32, (SPARE, rows), 0)
    fetch.wait()
    token = jnp.where(row % 4 < 2, token_ref[0:1, :], token_ref[1:2, :])
    token = jnp.where(row % 2 == 0, token >> 8, token & 255)
    token = jnp.where(row // 4 == quad, token, 0).astype(f32).astype(bf16)
    for m in order:
        held_ref[m, branches * depth :, :] = jnp.zeros((SPARE, LANES), bf16)
        held_ref[m, branches * depth :, :rows] = token
    results = []
    for m in order:
        for i in range(branches):
            copies[m, i].wait()
        results.append(pltpu.make_async_copy(held_ref.at[m], out_refs[m], out_sems.at[m]))
        results[-1].start()
    for result in results:
        result.wait()


def here():
    members = lax.axis_size("ctx") // 2
    ctx = lax.axis_index("ctx")
    return ctx % members, ctx // members, lax.axis_index("groups"), lax.axis_index("chan")


def pick(half, near_ref, far_ref, picked_ref, genomes, rows):
    vocab = picked_ref.shape[1]
    length = picked_ref.shape[0] // genomes
    first = near_ref.shape[0] - SPARE
    diagonal = lax.broadcasted_iota(jnp.int32, (rows, rows), 0) == lax.broadcasted_iota(
        jnp.int32, (rows, rows), 1
    )
    entries = lax.broadcasted_iota(jnp.int32, (rows, vocab), 1).astype(f32)
    for other, ref in enumerate((near_ref, far_ref)):
        parts = ref[first:, :rows].astype(f32)
        for member in range(length // (2 * rows)):
            for b in range(genomes):
                at = 4 * member + 2 * b
                line = parts[at : at + 1] * 256.0 + parts[at + 1 : at + 2]
                column = jnp.sum(jnp.where(diagonal, line, 0.0), axis=1, keepdims=True)
                place = b * length + (half ^ other) * (length // 2) + member * rows
                picked_ref[pl.ds(pl.multiple_of(place, rows), rows), :] = (
                    (column == entries).astype(f32).astype(bf16)
                )


def prepare_kernel(rate_ref, amp_ref, taps_ref, skip_ref, matrices_ref, rows_ref):
    quad, half, _, _ = here()

    group_count = rate_ref.shape[1]
    poles = rate_ref.shape[0]
    count = LANES // poles

    def group_at(lane):
        place = lane // poles
        return quad * (2 * count) + (place // (count // 2)) * count + half * (count // 2) + place % (count // 2)

    lane = lax.broadcasted_iota(jnp.int32, (group_count, LANES), 1)
    chosen = (lax.broadcasted_iota(jnp.int32, (group_count, LANES), 0) == group_at(lane)).astype(f32)
    turned_lane = lax.broadcasted_iota(jnp.int32, (LANES, group_count), 0)
    turned = (lax.broadcasted_iota(jnp.int32, (LANES, group_count), 1) == group_at(turned_lane)).astype(f32)

    def along_lanes(ref):
        spread = jnp.dot(ref[...], chosen, precision=highest, preferred_element_type=f32)
        keep = lax.broadcasted_iota(jnp.int32, spread.shape, 0) == lax.broadcasted_iota(
            jnp.int32, spread.shape, 1
        ) % poles
        return jnp.sum(jnp.where(keep, spread, 0.0), axis=0, keepdims=True)

    rate, amp = along_lanes(rate_ref), along_lanes(amp_ref)
    spread = lax.dot_general(
        turned, rate_ref[...], (((1,), (1,)), ((), ())), precision=highest, preferred_element_type=f32
    )
    keep = lax.broadcasted_iota(jnp.int32, spread.shape, 1) == lax.broadcasted_iota(
        jnp.int32, spread.shape, 0
    ) % poles
    rate_col = jnp.sum(jnp.where(keep, spread, 0.0), axis=1, keepdims=True)

    square = (CHUNK, LANES)
    row = lax.broadcasted_iota(jnp.int32, square, 0)
    col = lax.broadcasted_iota(jnp.int32, square, 1)
    at = row.astype(f32)
    middle = float(CHUNK // 2)
    rising = amp * jnp.exp(-rate * (at - middle))
    falling = jnp.exp(-rate * (middle - at))
    width = (count + 1) * CHUNK
    for g in range(count):
        own = jnp.where(col // poles == g, falling, 0.0)
        block = lax.dot_general(
            rising, own, (((1,), (1,)), ((), ())), precision=highest, preferred_element_type=f32
        )
        high, low = split(jnp.where(row >= col, block, 0.0))
        matrices_ref[:, g * CHUNK : (g + 1) * CHUNK] = high
        matrices_ref[:, width + g * CHUNK : width + (g + 1) * CHUNK] = low
    high, low = split(amp * jnp.exp(-rate * (at + 1.0)))
    matrices_ref[:, count * CHUNK : width] = high
    matrices_ref[:, width + count * CHUNK : 2 * width] = low
    high, low = split(jnp.exp(-rate_col * (float(CHUNK - 1) - col.astype(f32))))
    matrices_ref[:, 2 * width : 2 * width + CHUNK] = high
    matrices_ref[:, 2 * width + CHUNK :] = low

    rows_ref[:LANES] = jnp.exp(-rate_col * float(CHUNK)) + jnp.zeros(square, f32)
    branches = taps_ref.shape[0]
    for j in range(branches):
        taps = jnp.dot(taps_ref[j], chosen, precision=highest, preferred_element_type=f32)
        rows_ref[LANES + 8 * j : LANES + 8 * j + taps.shape[0]] = taps
    upper = skip_ref[pl.ds(2 * quad, 1), :]
    lower = skip_ref[pl.ds(2 * quad + 1, 1), :]
    upper = jnp.where(half == 0, upper, half_turn(upper))
    lower = jnp.where(half == 1, lower, half_turn(lower))
    end = LANES + 8 * branches
    rows_ref[end : end + 1] = jnp.where(lane_half(upper.shape), upper, lower)


def partial_kernel(normed_ref, *refs, begin, count):
    weight_refs, (keep_ref, send_ref) = refs[:-2], refs[-2:]
    quad, half, _, _ = here()
    rows, features = normed_ref.shape
    depth = features // len(weight_refs)
    total = jnp.zeros((rows, count * LANES), f32)
    tokens = jnp.zeros((SPARE, LANES), f32)
    for m, weight_ref in enumerate(weight_refs):
        first = pl.multiple_of((quad ^ m) * depth, depth)
        columns = jnp.concatenate(
            [weight_ref[j * depth : (j + 1) * depth, :] for j in range(begin, begin + count)], axis=1
        )
        total += jnp.dot(
            normed_ref[:, pl.ds(first, depth)], columns, preferred_element_type=f32
        )
        tokens += weight_ref[weight_ref.shape[0] - SPARE :, :].astype(f32)
    part = rows // 2
    for j in range(count):
        mine = total[:, j * LANES : (j + 1) * LANES]
        mine = jnp.where(half == 0, mine, half_turn(mine))
        top, bottom = mine[:part], mine[part:]
        left = lane_half(top.shape)
        keep_ref[j * part : (j + 1) * part, :] = jnp.where(left, top, half_turn(bottom))
        send_ref[j * part : (j + 1) * part, :] = jnp.where(left, half_turn(top), bottom).astype(bf16)
    if send_ref.shape[0] > count * part:
        send_ref[count * part :, :] = tokens.astype(bf16)


def filtered_branch(group, picked, row, mine, theirs, rows_ref, branch):
    mine, theirs = mine.astype(f32), theirs.astype(f32)
    first = jnp.where(group == 0, mine, theirs)
    second = jnp.where(group == 0, theirs, mine)
    left = lane_half(first.shape)
    top = jnp.where(left, first, half_turn(second))
    bottom = jnp.where(left, half_turn(first), second)
    table = jnp.concatenate([top, bottom], axis=0).astype(bf16)
    now = jnp.dot(picked, table, preferred_element_type=f32)
    first_tap = LANES + 8 * branch
    total = rows_ref[first_tap : first_tap + 1] * now
    for lag in range(1, 3):
        late = jnp.where(row >= lag, pltpu.roll(now, lag, 0), 0.0)
        total += rows_ref[first_tap + lag : first_tap + lag + 1] * late
    return total


def conv_kernel(
    near_ref, far_ref, own_ref, other_ref, matrices_ref, rows_ref, value_ref, picked_ref, *, genomes, rows
):
    _, half, group, _ = here()
    pick(half, near_ref, far_ref, picked_ref, genomes, rows)
    positions = picked_ref.shape[0]
    length = positions // genomes
    row = lax.broadcasted_iota(jnp.int32, (positions, LANES), 0) % length
    picked = picked_ref[...]
    key, value = (
        filtered_branch(group, picked, row, own_ref[j - 1], other_ref[j - 1], rows_ref, j)
        for j in (1, 2)
    )
    product = key * value
    size = 16
    count = LANES // size
    width = genomes * LANES
    lane = lax.broadcasted_iota(jnp.int32, (CHUNK, width), 1) % LANES
    pole_row = lax.broadcasted_iota(jnp.int32, (LANES, width), 0)
    same = pole_row // size == (lax.broadcasted_iota(jnp.int32, (LANES, width), 1) % LANES) // size
    fade = jnp.concatenate([rows_ref[:LANES]] * genomes, axis=1)
    skip = rows_ref[rows_ref.shape[0] - 8 : rows_ref.shape[0] - 7]
    across = (count + 1) * CHUNK
    high, low = matrices_ref[:, :across], matrices_ref[:, across : 2 * across]
    ends_high = matrices_ref[:, 2 * across : 2 * across + CHUNK]
    ends_low = matrices_ref[:, 2 * across + CHUNK :]
    state = jnp.zeros((LANES, width), f32)
    chunks = length // CHUNK
    for c in range(chunks):
        spans = [slice(b * length + c * CHUNK, b * length + (c + 1) * CHUNK) for b in range(genomes)]
        block = jnp.concatenate([product[span] for span in spans], axis=1)
        stacked = jnp.concatenate(
            [jnp.where(lane // size == g, block, 0.0) for g in range(count)] + [state], axis=0
        )
        conv = dot3(high, low, stacked)
        for b, span in enumerate(spans):
            value_ref[span, :] = conv[:, b * LANES : (b + 1) * LANES] + skip * product[span]
        if c < chunks - 1:
            ends = dot3(ends_high, ends_low, block)
            state = fade * state + jnp.where(same, ends, 0.0)


def gate_kernel(picked_ref, own_ref, other_ref, rows_ref, value_ref, *refs, genomes):
    piece_refs, (mine_ref, held_ref) = refs[:4], refs[4:]
    _, half, group, core = here()
    positions = picked_ref.shape[0]
    length = positions // genomes
    row = lax.broadcasted_iota(jnp.int32, (positions, LANES), 0) % length
    query = filtered_branch(group, picked_ref[...], row, own_ref[0], other_ref[0], rows_ref, 0)
    held_ref[...] = (query * value_ref[...]).astype(bf16)
    part = length // 2
    for r, piece_ref in enumerate(piece_refs):
        place = 2 * (core ^ (r % 2)) + (half ^ (r // 2))
        piece_ref[...] = held_ref[pl.ds(pl.multiple_of(place * part, part), part), :]
    mine_ref[...] = picked_ref[pl.ds(pl.multiple_of((2 * core + half) * part, part), part), :]


def offer_kernel(place_ref, rows_ref, packed_ref, first_ref, second_ref):
    del place_ref, packed_ref
    count = first_ref.shape[0]
    first_ref[...] = rows_ref[:count]
    second_ref[...] = rows_ref[count:]


def residual(picked_ref, table_ref, first, width):
    return jnp.dot(
        picked_ref[...],
        table_ref[:, pl.ds(pl.multiple_of(first, width), width)],
        preferred_element_type=f32,
    )


def near_kernel(picked_ref, table_ref, *refs):
    piece_refs, (own_ref, core_ref, out_ref, joined_ref) = refs[:4], refs[4:]
    quad, half, _, _ = here()
    block = 2 * LANES
    for m, piece_ref in enumerate(piece_refs):
        for other_core in (0, 1):
            near = piece_ref[other_core].astype(f32)
            far = piece_ref[2 + other_core].astype(f32)
            first = jnp.where(half == 0, near, far)
            second = jnp.where(half == 0, far, near)
            left = lane_half(first.shape)
            pair = [
                jnp.where(left, first, half_turn(second)),
                jnp.where(left, half_turn(first), second),
            ]
            joined_ref[2 * (quad ^ m) + other_core] = jnp.concatenate(pair, axis=1).astype(bf16)
    width = own_ref.shape[1]
    total = jnp.zeros(out_ref.shape, f32)
    for member in range(4):
        rows = slice(member * block, (member + 1) * block)
        for other_core, ref in enumerate((own_ref, core_ref)):
            total += jnp.dot(
                joined_ref[2 * member + other_core], ref[rows, :], preferred_element_type=f32
            )
    total += residual(picked_ref, table_ref, (4 * half + quad) * width, width)
    out_ref[...] = total.astype(bf16)


def far_kernel(picked_ref, table_ref, near_ref, joined_ref, *refs):
    far_refs, out_ref = (refs[:2], refs[2:4]), refs[4]
    quad, half, group, core = here()
    block = 2 * LANES
    width = near_ref.shape[1]
    total = jnp.zeros(near_ref.shape, f32)
    for member in range(4):
        rows = slice((member % 2) * block, (member % 2 + 1) * block)
        for other_core in (0, 1):
            source = 2 * (2 * (group ^ (member // 2)) + member % 2) + other_core
            total += jnp.dot(
                joined_ref[source],
                far_refs[member // 2][other_core][rows, :],
                preferred_element_type=f32,
            )
    total += residual(picked_ref, table_ref, (4 * (half ^ 1) + (quad ^ 2)) * width, width)
    out_ref[half ^ core] = near_ref[...]
    out_ref[half ^ 1 ^ core] = total.astype(bf16)


def place_kernel(*refs):
    piece_refs, (out_ref, sems) = refs[:4], refs[4:]
    quad, half, _, core = here()
    width = piece_refs[0].shape[2]
    copies = []
    for m, piece_ref in enumerate(piece_refs):
        first = pl.multiple_of((quad ^ m ^ (2 * (half ^ core))) * width, width)
        for g in (0, 1):
            copies.append(
                pltpu.make_async_copy(
                    piece_ref.at[g], out_ref.at[core ^ g, :, pl.ds(first, width)], sems.at[m, g]
                )
            )
            copies[-1].start()
    for copy in copies:
        copy.wait()


def called(kernel, out_shape, scalars, *operands, scratch=(), mib=16, earlier=()):
    smem = pl.BlockSpec(memory_space=pltpu.SMEM)
    vmem = pl.BlockSpec(memory_space=pltpu.VMEM)
    anywhere = pl.BlockSpec(memory_space=pl.ANY)
    many = isinstance(out_shape, (list, tuple))
    inputs, waits = len(scalars) + len(operands), len(earlier)

    def body(*refs):
        kernel(*refs[:inputs], *refs[inputs + waits :])

    return pl.pallas_call(
        body,
        out_shape=out_shape,
        in_specs=[smem] * len(scalars) + [vmem] * len(operands) + [anywhere] * waits,
        out_specs=[vmem] * len(out_shape) if many else vmem,
        scratch_shapes=scratch,
        compiler_params=pltpu.CompilerParams(vmem_limit_bytes=mib * MIB),
    )(*scalars, *operands, *earlier)


def shaped(*shape, dtype=f32):
    return jax.ShapeDtypeStruct(shape, dtype)


def pass_kernel(*refs):
    del refs


def after(value, earlier):
    return pl.pallas_call(
        pass_kernel,
        out_shape=shaped(*value.shape, dtype=value.dtype),
        in_specs=[pl.BlockSpec(memory_space=pl.ANY)] * 2,
        out_specs=pl.BlockSpec(memory_space=pl.ANY),
        input_output_aliases={0: 0},
        compiler_params=pltpu.CompilerParams(vmem_limit_bytes=MIB),
    )(value, earlier)


def quad_body(
    tokens,
    embed_table,
    norm_gain,
    input_proj,
    short_filter,
    pole_rate,
    residue,
    skip_gain,
    output_proj,
):
    genomes, rows = tokens.shape
    depth, branches, channels = input_proj.shape
    vocab, features = embed_table.shape
    members = lax.axis_size("ctx") // 2
    ctx, core, group = (lax.axis_index(name) for name in ("ctx", "chan", "groups"))
    quad, half = ctx % members, ctx // members
    place = jnp.stack([quad, half, group, core]).astype(jnp.int32)
    block = channels // members

    weights = input_proj.transpose(1, 0, 2)
    anywhere = pl.BlockSpec(memory_space=pl.ANY)
    packed = pl.pallas_call(
        pack_kernel,
        out_shape=[shaped(branches * depth + SPARE, LANES, dtype=bf16)] * members,
        in_specs=[anywhere, anywhere],
        out_specs=[anywhere] * members,
        scratch_shapes=[
            pltpu.VMEM((members, branches * depth + SPARE, LANES), bf16),
            pltpu.VMEM((genomes, rows), jnp.int32),
            pltpu.SemaphoreType.DMA,
            pltpu.SemaphoreType.DMA((members, branches)),
            pltpu.SemaphoreType.DMA((members,)),
        ],
        compiler_params=pltpu.CompilerParams(vmem_limit_bytes=61 * MIB),
    )(tokens, weights)
    gathered = [packed[0]] + [swapped(packed[m], "ctx", m) for m in range(1, members)]
    length = 2 * members * rows

    half_rows = output_proj.shape[0] // 2
    width = output_proj.shape[1]
    offered = pl.pallas_call(
        offer_kernel,
        out_shape=[shaped(half_rows // 2, width, dtype=bf16)] * 2,
        grid_spec=pltpu.PrefetchScalarGridSpec(
            num_scalar_prefetch=1,
            grid=(1,),
            in_specs=[pl.BlockSpec((half_rows, width), lambda i, place: (place[2], 0)), anywhere],
            out_specs=[pl.BlockSpec((half_rows // 2, width), lambda i, place: (0, 0))] * 2,
        ),
        compiler_params=pltpu.CompilerParams(vmem_limit_bytes=4 * MIB),
    )(place, output_proj, packed[1])
    count = 2 * members
    inner = [(i, count - 2 - i + 2 * (i % 2)) for i in range(members // 2, members + members // 2)]
    outer = [
        (i, count - 2 - i + 2 * (i % 2))
        for i in range(count)
        if not members // 2 <= i < members + members // 2
    ]

    part = features // 2
    step = 128
    normed = pl.pallas_call(
        norm_kernel,
        out_shape=shaped(vocab, part, dtype=bf16),
        grid_spec=pltpu.PrefetchScalarGridSpec(
            num_scalar_prefetch=1,
            grid=(vocab // step,),
            in_specs=[
                pl.BlockSpec((step, features), lambda i, place: (i, 0)),
                pl.BlockSpec((1, part), lambda i, place: (0, place[1])),
                pl.BlockSpec((step, part), lambda i, place: (i, place[1])),
                anywhere,
                anywhere,
            ],
            out_specs=pl.BlockSpec((step, part), lambda i, place: (i, 0)),
        ),
        compiler_params=pltpu.CompilerParams(vmem_limit_bytes=16 * MIB),
    )(place, embed_table, norm_gain.reshape(1, features), embed_table, gathered[1], packed[1])

    inner_fetched = [lax.ppermute(rows_part, "ctx", inner) for rows_part in offered]
    def partials(begin, count, spare, earlier=()):
        table_rows = count * (vocab // 2)
        return called(
            functools.partial(partial_kernel, begin=begin, count=count),
            [shaped(table_rows, LANES), shaped(table_rows + spare, LANES, dtype=bf16)],
            (),
            normed,
            *gathered,
            earlier=earlier,
        )

    def finished(keep, arrived):
        own = (keep + arrived[: keep.shape[0]].astype(f32)).astype(bf16)
        return own.reshape(-1, vocab // 2, LANES)

    pair_keep, pair_send = partials(0, 2, SPARE, tuple(inner_fetched))
    query_keep, query_send = partials(2, 1, 0)
    pair_arrived = swapped(pair_send, "ctx", members)
    query_arrived = swapped(query_send, "ctx", members)
    amp = residue * jnp.sqrt(-jnp.expm1(-2.0 * pole_rate))
    across = (LANES // pole_rate.shape[1] + 1) * CHUNK
    matrices, lines = called(
        prepare_kernel,
        [
            shaped(CHUNK, 2 * across + 2 * CHUNK, dtype=bf16),
            shaped(LANES + 8 * (branches + 1), LANES),
        ],
        (),
        pole_rate.T,
        amp.T,
        short_filter.transpose(0, 2, 1),
        skip_gain.reshape(-1, LANES),
        earlier=(pair_send,),
    )

    pair_own = after(finished(pair_keep, pair_arrived), matrices)
    query_own = finished(query_keep, query_arrived)
    pair_other = swapped(pair_own, "groups", 1)
    query_other = swapped(query_own, "groups", 1)

    span = length // 2
    value, picked = called(
        functools.partial(conv_kernel, genomes=genomes, rows=rows),
        [shaped(genomes * length, LANES), shaped(genomes * length, vocab, dtype=bf16)],
        (),
        pair_send,
        pair_arrived,
        pair_own,
        pair_other,
        matrices,
        lines,
    )
    *pieces, picked = called(
        functools.partial(gate_kernel, genomes=genomes),
        [shaped(span, LANES, dtype=bf16)] * 4 + [shaped(span, vocab, dtype=bf16)],
        (),
        picked,
        query_own,
        query_other,
        lines,
        value,
        scratch=[pltpu.VMEM((genomes * length, LANES), bf16)],
    )
    core_piece = swapped(pieces[1], "chan", 1)
    piece = jnp.stack(
        [
            pieces[0],
            core_piece,
            swapped(pieces[2], "ctx", members),
            swapped_both(pieces[3], members),
        ]
    )
    gated = [piece] + [swapped(piece, "ctx", m) for m in range(1, members)]

    outer_fetched = [lax.ppermute(after(rows_part, pair_own), "ctx", outer) for rows_part in offered]
    fetched = jnp.where(
        (ctx >= members // 2) & (ctx < members + members // 2),
        jnp.concatenate(inner_fetched),
        jnp.concatenate(outer_fetched),
    )
    fetched = after(fetched, piece)
    shared = swapped(fetched, "groups", 1)
    for ready in gated[1:]:
        shared = after(shared, ready)
    near, joined = called(
        near_kernel,
        [shaped(span, width, dtype=bf16), shaped(4 * 2, span, 2 * LANES, dtype=bf16)],
        (),
        picked,
        embed_table,
        *gated,
        output_proj,
        swapped(output_proj, "chan", 1),
        mib=24,
    )
    results = called(
        far_kernel,
        shaped(2, span, width, dtype=bf16),
        (),
        picked,
        embed_table,
        near,
        joined,
        fetched,
        swapped(fetched, "chan", 1),
        shared,
        swapped(shared, "chan", 1),
        mib=24,
    )
    both = jnp.stack([results[0], swapped(results[1], "chan", 1)])

    def rows_of(member):
        return lax.dynamic_slice_in_dim(both, member * rows, rows, 1)

    arrived = [rows_of(quad)] + [swapped(rows_of(quad ^ m), "ctx", m) for m in range(1, members)]
    return pl.pallas_call(
        place_kernel,
        out_shape=shaped(genomes, rows, members * width, dtype=bf16),
        in_specs=[pl.BlockSpec(memory_space=pltpu.VMEM)] * members,
        out_specs=anywhere,
        scratch_shapes=[pltpu.SemaphoreType.DMA((members, 2))],
        compiler_params=pltpu.CompilerParams(vmem_limit_bytes=4 * MIB),
    )(*arrived)


def solution(mesh):
    sizes = tuple(mesh.shape[name] for name in ("groups", "ctx", "chan"))
    return jax.shard_map(
        quad_body if sizes == (2, 8, 2) else general_body,
        mesh=mesh,
        in_specs=(
            P("groups", "ctx"),
            P(),
            P(),
            P("ctx", None, "chan"),
            P(None, "chan", None),
            P("chan", None),
            P("chan", None),
            P("chan"),
            P("chan", "ctx"),
        ),
        out_specs=P("groups", "ctx", "chan"),
        check_vma=False,
    )
```

```python
import functools

import jax
import jax.numpy as jnp
from jax import lax
from jax.experimental import pallas as pl
from jax.experimental.pallas import tpu as pltpu
from jax.sharding import PartitionSpec as P

epsilon = 1e-06
highest = lax.Precision.HIGHEST
f32 = jnp.float32
bf16 = jnp.bfloat16
CHUNK = 128
LANES = 128
MIB = 1024 * 1024
SPARE = 16


def passed_along(shard, axis, by):
    count = lax.axis_size(axis)
    pairs = [(i, i + by) for i in range(count) if 0 <= i + by < count]
    return lax.ppermute(shard, axis, pairs)


def entering(shard, axis, combine, identity):
    count, mine = (lax.axis_size(axis), lax.axis_index(axis))
    everything = jax.tree.map(lambda part: lax.all_gather(part, axis), shard)
    start = jax.tree.map(
        lambda part, zero: jnp.broadcast_to(jnp.asarray(zero, part.dtype), part.shape),
        shard,
        identity,
    )

    def hop(k, before):
        reached = k < mine
        new = combine(before, jax.tree.map(lambda part: part[k], everything))
        return jax.tree.map(lambda a, b: jnp.where(reached, a, b), new, before)

    return lax.fori_loop(0, count, hop, start)


def local_block(operands):
    rising, falling, inputs = operands
    length = rising.shape[2]
    toeplitz = jnp.einsum("gnt,gns->gts", rising, falling, precision=highest)
    causal = jnp.arange(length)[:, None] >= jnp.arange(length)[None, :]
    toeplitz = jnp.where(causal[None], toeplitz, 0.0)
    return jnp.einsum("gms,gts->gmt", inputs, toeplitz, precision=highest)


def lookup_rows(token_block, embed_table):
    vocab_count = embed_table.shape[0]
    onehot = (token_block[:, None] == jnp.arange(vocab_count, dtype=jnp.int32)[None, :]).astype(
        jnp.bfloat16
    )
    return jnp.dot(onehot, embed_table, preferred_element_type=jnp.float32)


def general_body(
    tokens,
    embed_table,
    norm_gain,
    input_proj,
    short_filter,
    pole_rate,
    residue,
    skip_gain,
    output_proj,
):
    genome_count, row_count = tokens.shape
    part_rows, branch_count, channels = input_proj.shape
    groups = pole_rate.shape[0]
    group_size = channels // groups
    tap_count = short_filter.shape[2]
    flat_count = genome_count * row_count
    flat_tokens = tokens.reshape(flat_count)
    widened = lookup_rows(flat_tokens, embed_table)
    inv_rms = lax.rsqrt(jnp.mean(widened * widened, axis=-1, keepdims=True) + epsilon)
    normed = (widened * inv_rms * norm_gain).astype(jnp.bfloat16)
    proj_cols = branch_count * channels
    flat_weight = input_proj.reshape(part_rows, proj_cols)
    spread = lax.all_to_all(normed, "ctx", split_axis=1, concat_axis=0, tiled=True)
    summed = lax.psum_scatter(
        jnp.dot(spread, flat_weight, preferred_element_type=jnp.float32),
        "ctx",
        scatter_dimension=0,
        tiled=True,
    )
    projected = summed.astype(jnp.bfloat16).reshape(genome_count, row_count, branch_count, channels)
    rim = passed_along(projected[:, row_count - (tap_count - 1) :], "ctx", 1)
    extended = jnp.concatenate([rim, projected], axis=1).astype(jnp.float32)
    taps_full = jnp.broadcast_to(
        short_filter[:, :, None, :], (branch_count, groups, group_size, tap_count)
    ).reshape(branch_count, channels, tap_count)
    filtered = jnp.zeros((genome_count, row_count, branch_count, channels), jnp.float32)
    for lag in range(tap_count):
        first_row = tap_count - 1 - lag
        filtered = filtered + taps_full[:, :, lag] * extended[:, first_row : first_row + row_count]
    query_part = filtered[:, :, 0]
    product = filtered[:, :, 1] * filtered[:, :, 2]
    mixes = genome_count * group_size
    grouped = (
        product.reshape(genome_count, row_count, groups, group_size)
        .transpose(2, 0, 3, 1)
        .reshape(groups, mixes, row_count)
    )
    positions = jnp.arange(row_count, dtype=jnp.float32)
    middle = float(row_count // 2)
    powers = jnp.exp(-pole_rate[:, :, None] * positions)
    next_powers = jnp.exp(-pole_rate[:, :, None] * (positions + 1.0))
    pole_amp = residue * jnp.sqrt(-jnp.expm1(-2.0 * pole_rate))
    rising = pole_amp[:, :, None] * jnp.exp(-pole_rate[:, :, None] * (positions - middle))
    falling = jnp.exp(-pole_rate[:, :, None] * (middle - positions))
    block_size = 8
    blocks = groups // block_size
    poles = pole_rate.shape[1]
    local_part = lax.map(
        local_block,
        (
            rising.reshape(blocks, block_size, poles, row_count),
            falling.reshape(blocks, block_size, poles, row_count),
            grouped.reshape(blocks, block_size, mixes, row_count),
        ),
    )
    local_part = local_part.reshape(groups, mixes, row_count)
    end_state = jnp.einsum("gms,gns->gmn", grouped, powers[:, :, ::-1], precision=highest)
    block_decay = jnp.exp(-pole_rate * row_count)

    def combine(earlier, later):
        return (earlier[0] * later[0], later[0][:, None, :] * earlier[1] + later[1])

    identity = (jnp.ones_like(block_decay), jnp.zeros_like(end_state))
    incoming = entering((block_decay, end_state), "ctx", combine, identity)[1]
    weighted = incoming * pole_amp[:, None, :]
    correction = jnp.einsum("gmn,gnt->gmt", weighted, next_powers, precision=highest)
    long_conv = (
        (local_part + correction)
        .reshape(groups, genome_count, group_size, row_count)
        .transpose(1, 3, 0, 2)
        .reshape(genome_count, row_count, channels)
    )
    gated = (
        (query_part * (long_conv + skip_gain * product))
        .astype(jnp.bfloat16)
        .reshape(flat_count, channels)
    )
    partial_value = jnp.dot(
        gated,
        lax.all_gather(output_proj, "ctx", axis=1, tiled=True),
        preferred_element_type=jnp.float32,
    )
    own_share = lax.psum_scatter(partial_value, "chan", scatter_dimension=1, tiled=True)
    half_width = own_share.shape[1]
    residual_part = lax.dynamic_slice_in_dim(
        widened, lax.axis_index("chan") * half_width, half_width, 1
    )
    block_out = (residual_part + own_share).astype(jnp.bfloat16)
    return block_out.reshape(genome_count, row_count, half_width)


def swapped(value, axis, mask):
    count = lax.axis_size(axis)
    return lax.ppermute(value, axis, [(i, i ^ mask) for i in range(count)])


def swapped_both(value, ctx_mask):
    count, cores = lax.axis_size("ctx"), lax.axis_size("chan")
    pairs = [
        (i * cores + c, (i ^ ctx_mask) * cores + (c ^ 1)) for i in range(count) for c in range(cores)
    ]
    return lax.ppermute(value, ("ctx", "chan"), pairs)


def split(value):
    high = value.astype(bf16)
    return high, (value - high.astype(f32)).astype(bf16)


def dot3(a_high, a_low, b):
    b_high, b_low = split(b)
    total = jnp.dot(a_high, b_high, preferred_element_type=f32)
    total += jnp.dot(a_low, b_high, preferred_element_type=f32)
    return total + jnp.dot(a_high, b_low, preferred_element_type=f32)


def lane_half(shape):
    return lax.broadcasted_iota(jnp.int32, shape, len(shape) - 1) < LANES // 2


def half_turn(value):
    return pltpu.roll(value, LANES // 2, value.ndim - 1)


def norm_kernel(place_ref, table_ref, gain_ref, part_ref, pair_ref, query_ref, out_ref):
    del place_ref, pair_ref, query_ref
    widened = table_ref[...].astype(f32)
    mean = jnp.sum(widened * widened, axis=1, keepdims=True) / widened.shape[1]
    own = part_ref[...].astype(f32)
    out_ref[...] = (own * lax.rsqrt(mean + epsilon) * gain_ref[...]).astype(bf16)


def pack_kernel(tokens_ref, weight_ref, *refs):
    out_refs, (held_ref, token_ref, token_sem, in_sems, out_sems) = refs[:-5], refs[-5:]
    branches, depth, channels = weight_ref.shape
    members = len(out_refs)
    quad, group = lax.axis_index("ctx") % members, lax.axis_index("groups")
    block = channels // members
    order = (1, 2, 3, 0)
    fetch = pltpu.make_async_copy(tokens_ref, token_ref, token_sem)
    fetch.start()
    copies = {}
    for m in order:
        first = pl.multiple_of((quad ^ m) * block + group * LANES, LANES)
        for i, j in enumerate((1, 2, 0)):
            copies[m, i] = pltpu.make_async_copy(
                weight_ref.at[j, :, pl.ds(first, LANES)],
                held_ref.at[m, pl.ds(i * depth, depth), :],
                in_sems.at[m, i],
            )
            copies[m, i].start()
    rows = token_ref.shape[1]
    row = lax.broadcasted_iota(jnp.int32, (SPARE, rows), 0)
    fetch.wait()
    token = jnp.where(row % 4 < 2, token_ref[0:1, :], token_ref[1:2, :])
    token = jnp.where(row % 2 == 0, token >> 8, token & 255)
    token = jnp.where(row // 4 == quad, token, 0).astype(f32).astype(bf16)
    for m in order:
        held_ref[m, branches * depth :, :] = jnp.zeros((SPARE, LANES), bf16)
        held_ref[m, branches * depth :, :rows] = token
    results = []
    for m in order:
        for i in range(branches):
            copies[m, i].wait()
        results.append(pltpu.make_async_copy(held_ref.at[m], out_refs[m], out_sems.at[m]))
        results[-1].start()
    for result in results:
        result.wait()


def here():
    members = lax.axis_size("ctx") // 2
    ctx = lax.axis_index("ctx")
    return ctx % members, ctx // members, lax.axis_index("groups"), lax.axis_index("chan")


def pick(half, near_ref, far_ref, picked_ref, genomes, rows):
    vocab = picked_ref.shape[1]
    length = picked_ref.shape[0] // genomes
    first = near_ref.shape[0] - SPARE
    diagonal = lax.broadcasted_iota(jnp.int32, (rows, rows), 0) == lax.broadcasted_iota(
        jnp.int32, (rows, rows), 1
    )
    entries = lax.broadcasted_iota(jnp.int32, (rows, vocab), 1).astype(f32)
    for other, ref in enumerate((near_ref, far_ref)):
        parts = ref[first:, :rows].astype(f32)
        for member in range(length // (2 * rows)):
            for b in range(genomes):
                at = 4 * member + 2 * b
                line = parts[at : at + 1] * 256.0 + parts[at + 1 : at + 2]
                column = jnp.sum(jnp.where(diagonal, line, 0.0), axis=1, keepdims=True)
                place = b * length + (half ^ other) * (length // 2) + member * rows
                picked_ref[pl.ds(pl.multiple_of(place, rows), rows), :] = (
                    (column == entries).astype(f32).astype(bf16)
                )


def prepare_kernel(rate_ref, amp_ref, taps_ref, skip_ref, matrices_ref, rows_ref):
    quad, half, _, _ = here()

    group_count = rate_ref.shape[1]
    poles = rate_ref.shape[0]
    count = LANES // poles

    def group_at(lane):
        place = lane // poles
        return quad * (2 * count) + (place // (count // 2)) * count + half * (count // 2) + place % (count // 2)

    lane = lax.broadcasted_iota(jnp.int32, (group_count, LANES), 1)
    chosen = (lax.broadcasted_iota(jnp.int32, (group_count, LANES), 0) == group_at(lane)).astype(f32)
    turned_lane = lax.broadcasted_iota(jnp.int32, (LANES, group_count), 0)
    turned = (lax.broadcasted_iota(jnp.int32, (LANES, group_count), 1) == group_at(turned_lane)).astype(f32)

    def along_lanes(ref):
        spread = jnp.dot(ref[...], chosen, precision=highest, preferred_element_type=f32)
        keep = lax.broadcasted_iota(jnp.int32, spread.shape, 0) == lax.broadcasted_iota(
            jnp.int32, spread.shape, 1
        ) % poles
        return jnp.sum(jnp.where(keep, spread, 0.0), axis=0, keepdims=True)

    rate, amp = along_lanes(rate_ref), along_lanes(amp_ref)
    spread = lax.dot_general(
        turned, rate_ref[...], (((1,), (1,)), ((), ())), precision=highest, preferred_element_type=f32
    )
    keep = lax.broadcasted_iota(jnp.int32, spread.shape, 1) == lax.broadcasted_iota(
        jnp.int32, spread.shape, 0
    ) % poles
    rate_col = jnp.sum(jnp.where(keep, spread, 0.0), axis=1, keepdims=True)

    square = (CHUNK, LANES)
    row = lax.broadcasted_iota(jnp.int32, square, 0)
    col = lax.broadcasted_iota(jnp.int32, square, 1)
    at = row.astype(f32)
    middle = float(CHUNK // 2)
    rising = amp * jnp.exp(-rate * (at - middle))
    falling = jnp.exp(-rate * (middle - at))
    width = (count + 1) * CHUNK
    for g in range(count):
        own = jnp.where(col // poles == g, falling, 0.0)
        block = lax.dot_general(
            rising, own, (((1,), (1,)), ((), ())), precision=highest, preferred_element_type=f32
        )
        high, low = split(jnp.where(row >= col, block, 0.0))
        matrices_ref[:, g * CHUNK : (g + 1) * CHUNK] = high
        matrices_ref[:, width + g * CHUNK : width + (g + 1) * CHUNK] = low
    high, low = split(amp * jnp.exp(-rate * (at + 1.0)))
    matrices_ref[:, count * CHUNK : width] = high
    matrices_ref[:, width + count * CHUNK : 2 * width] = low
    high, low = split(jnp.exp(-rate_col * (float(CHUNK - 1) - col.astype(f32))))
    matrices_ref[:, 2 * width : 2 * width + CHUNK] = high
    matrices_ref[:, 2 * width + CHUNK :] = low

    rows_ref[:LANES] = jnp.exp(-rate_col * float(CHUNK)) + jnp.zeros(square, f32)
    branches = taps_ref.shape[0]
    for j in range(branches):
        taps = jnp.dot(taps_ref[j], chosen, precision=highest, preferred_element_type=f32)
        rows_ref[LANES + 8 * j : LANES + 8 * j + taps.shape[0]] = taps
    upper = skip_ref[pl.ds(2 * quad, 1), :]
    lower = skip_ref[pl.ds(2 * quad + 1, 1), :]
    upper = jnp.where(half == 0, upper, half_turn(upper))
    lower = jnp.where(half == 1, lower, half_turn(lower))
    end = LANES + 8 * branches
    rows_ref[end : end + 1] = jnp.where(lane_half(upper.shape), upper, lower)


def partial_kernel(normed_ref, *refs, begin, count):
    weight_refs, (keep_ref, send_ref) = refs[:-2], refs[-2:]
    quad, half, _, _ = here()
    rows, features = normed_ref.shape
    depth = features // len(weight_refs)
    total = jnp.zeros((rows, count * LANES), f32)
    tokens = jnp.zeros((SPARE, LANES), f32)
    for m, weight_ref in enumerate(weight_refs):
        first = pl.multiple_of((quad ^ m) * depth, depth)
        columns = jnp.concatenate(
            [weight_ref[j * depth : (j + 1) * depth, :] for j in range(begin, begin + count)], axis=1
        )
        total += jnp.dot(
            normed_ref[:, pl.ds(first, depth)], columns, preferred_element_type=f32
        )
        tokens += weight_ref[weight_ref.shape[0] - SPARE :, :].astype(f32)
    part = rows // 2
    for j in range(count):
        mine = total[:, j * LANES : (j + 1) * LANES]
        mine = jnp.where(half == 0, mine, half_turn(mine))
        top, bottom = mine[:part], mine[part:]
        left = lane_half(top.shape)
        keep_ref[j * part : (j + 1) * part, :] = jnp.where(left, top, half_turn(bottom))
        send_ref[j * part : (j + 1) * part, :] = jnp.where(left, half_turn(top), bottom).astype(bf16)
    if send_ref.shape[0] > count * part:
        send_ref[count * part :, :] = tokens.astype(bf16)


def filtered_branch(group, picked, row, mine, theirs, rows_ref, branch):
    mine, theirs = mine.astype(f32), theirs.astype(f32)
    first = jnp.where(group == 0, mine, theirs)
    second = jnp.where(group == 0, theirs, mine)
    left = lane_half(first.shape)
    top = jnp.where(left, first, half_turn(second))
    bottom = jnp.where(left, half_turn(first), second)
    table = jnp.concatenate([top, bottom], axis=0).astype(bf16)
    now = jnp.dot(picked, table, preferred_element_type=f32)
    first_tap = LANES + 8 * branch
    total = rows_ref[first_tap : first_tap + 1] * now
    for lag in range(1, 3):
        late = jnp.where(row >= lag, pltpu.roll(now, lag, 0), 0.0)
        total += rows_ref[first_tap + lag : first_tap + lag + 1] * late
    return total


def conv_kernel(
    near_ref, far_ref, own_ref, other_ref, matrices_ref, rows_ref, value_ref, picked_ref, *, genomes, rows
):
    _, half, group, _ = here()
    pick(half, near_ref, far_ref, picked_ref, genomes, rows)
    positions = picked_ref.shape[0]
    length = positions // genomes
    row = lax.broadcasted_iota(jnp.int32, (positions, LANES), 0) % length
    picked = picked_ref[...]
    key, value = (
        filtered_branch(group, picked, row, own_ref[j - 1], other_ref[j - 1], rows_ref, j)
        for j in (1, 2)
    )
    product = key * value
    size = 16
    count = LANES // size
    width = genomes * LANES
    lane = lax.broadcasted_iota(jnp.int32, (CHUNK, width), 1) % LANES
    pole_row = lax.broadcasted_iota(jnp.int32, (LANES, width), 0)
    same = pole_row // size == (lax.broadcasted_iota(jnp.int32, (LANES, width), 1) % LANES) // size
    fade = jnp.concatenate([rows_ref[:LANES]] * genomes, axis=1)
    skip = rows_ref[rows_ref.shape[0] - 8 : rows_ref.shape[0] - 7]
    across = (count + 1) * CHUNK
    high, low = matrices_ref[:, :across], matrices_ref[:, across : 2 * across]
    ends_high = matrices_ref[:, 2 * across : 2 * across + CHUNK]
    ends_low = matrices_ref[:, 2 * across + CHUNK :]
    state = jnp.zeros((LANES, width), f32)
    chunks = length // CHUNK
    for c in range(chunks):
        spans = [slice(b * length + c * CHUNK, b * length + (c + 1) * CHUNK) for b in range(genomes)]
        block = jnp.concatenate([product[span] for span in spans], axis=1)
        stacked = jnp.concatenate(
            [jnp.where(lane // size == g, block, 0.0) for g in range(count)] + [state], axis=0
        )
        conv = dot3(high, low, stacked)
        for b, span in enumerate(spans):
            value_ref[span, :] = conv[:, b * LANES : (b + 1) * LANES] + skip * product[span]
        if c < chunks - 1:
            ends = dot3(ends_high, ends_low, block)
            state = fade * state + jnp.where(same, ends, 0.0)


def gate_kernel(picked_ref, own_ref, other_ref, rows_ref, value_ref, *refs, genomes):
    piece_refs, (mine_ref, held_ref) = refs[:4], refs[4:]
    _, half, group, core = here()
    positions = picked_ref.shape[0]
    length = positions // genomes
    row = lax.broadcasted_iota(jnp.int32, (positions, LANES), 0) % length
    query = filtered_branch(group, picked_ref[...], row, own_ref[0], other_ref[0], rows_ref, 0)
    held_ref[...] = (query * value_ref[...]).astype(bf16)
    part = length // 2
    for r, piece_ref in enumerate(piece_refs):
        place = 2 * (core ^ (r % 2)) + (half ^ (r // 2))
        piece_ref[...] = held_ref[pl.ds(pl.multiple_of(place * part, part), part), :]
    mine_ref[...] = picked_ref[pl.ds(pl.multiple_of((2 * core + half) * part, part), part), :]


def offer_kernel(place_ref, rows_ref, packed_ref, first_ref, second_ref):
    del place_ref, packed_ref
    count = first_ref.shape[0]
    first_ref[...] = rows_ref[:count]
    second_ref[...] = rows_ref[count:]


def residual(picked_ref, table_ref, first, width):
    return jnp.dot(
        picked_ref[...],
        table_ref[:, pl.ds(pl.multiple_of(first, width), width)],
        preferred_element_type=f32,
    )


def near_kernel(picked_ref, table_ref, *refs):
    piece_refs, (own_ref, core_ref, out_ref, joined_ref) = refs[:4], refs[4:]
    quad, half, _, _ = here()
    block = 2 * LANES
    for m, piece_ref in enumerate(piece_refs):
        for other_core in (0, 1):
            near = piece_ref[other_core].astype(f32)
            far = piece_ref[2 + other_core].astype(f32)
            first = jnp.where(half == 0, near, far)
            second = jnp.where(half == 0, far, near)
            left = lane_half(first.shape)
            pair = [
                jnp.where(left, first, half_turn(second)),
                jnp.where(left, half_turn(first), second),
            ]
            joined_ref[2 * (quad ^ m) + other_core] = jnp.concatenate(pair, axis=1).astype(bf16)
    width = own_ref.shape[1]
    total = jnp.zeros(out_ref.shape, f32)
    for member in range(4):
        rows = slice(member * block, (member + 1) * block)
        for other_core, ref in enumerate((own_ref, core_ref)):
            total += jnp.dot(
                joined_ref[2 * member + other_core], ref[rows, :], preferred_element_type=f32
            )
    total += residual(picked_ref, table_ref, (4 * half + quad) * width, width)
    out_ref[...] = total.astype(bf16)


def far_kernel(picked_ref, table_ref, near_ref, joined_ref, *refs):
    far_refs, (kept_ref, sent_ref) = (refs[:2], refs[2:4]), refs[4:]
    quad, half, group, core = here()
    block = 2 * LANES
    width = near_ref.shape[1]
    total = jnp.zeros(near_ref.shape, f32)
    for member in range(4):
        rows = slice((member % 2) * block, (member % 2 + 1) * block)
        for other_core in (0, 1):
            source = 2 * (2 * (group ^ (member // 2)) + member % 2) + other_core
            total += jnp.dot(
                joined_ref[source],
                far_refs[member // 2][other_core][rows, :],
                preferred_element_type=f32,
            )
    total += residual(picked_ref, table_ref, (4 * (half ^ 1) + (quad ^ 2)) * width, width)
    near, far = near_ref[...], total.astype(bf16)
    kept_ref[...] = jnp.where(half == core, near, far)
    sent_ref[...] = jnp.where(half == core, far, near)


def place_kernel(*refs):
    part_refs, out_ref = refs[:8], refs[8]
    quad, half, _, core = here()
    width = part_refs[0].shape[1]
    for g in (0, 1):
        for m in range(4):
            first = pl.multiple_of((quad ^ m ^ (2 * (half ^ core))) * width, width)
            out_ref[core ^ g, :, pl.ds(first, width)] = part_refs[4 * g + m][...]


def called(kernel, out_shape, scalars, *operands, scratch=(), mib=16, earlier=()):
    smem = pl.BlockSpec(memory_space=pltpu.SMEM)
    vmem = pl.BlockSpec(memory_space=pltpu.VMEM)
    anywhere = pl.BlockSpec(memory_space=pl.ANY)
    many = isinstance(out_shape, (list, tuple))
    inputs, waits = len(scalars) + len(operands), len(earlier)

    def body(*refs):
        kernel(*refs[:inputs], *refs[inputs + waits :])

    return pl.pallas_call(
        body,
        out_shape=out_shape,
        in_specs=[smem] * len(scalars) + [vmem] * len(operands) + [anywhere] * waits,
        out_specs=[vmem] * len(out_shape) if many else vmem,
        scratch_shapes=scratch,
        compiler_params=pltpu.CompilerParams(vmem_limit_bytes=mib * MIB),
    )(*scalars, *operands, *earlier)


def shaped(*shape, dtype=f32):
    return jax.ShapeDtypeStruct(shape, dtype)


def pass_kernel(*refs):
    del refs


def after(value, earlier):
    return pl.pallas_call(
        pass_kernel,
        out_shape=shaped(*value.shape, dtype=value.dtype),
        in_specs=[pl.BlockSpec(memory_space=pl.ANY)] * 2,
        out_specs=pl.BlockSpec(memory_space=pl.ANY),
        input_output_aliases={0: 0},
        compiler_params=pltpu.CompilerParams(vmem_limit_bytes=MIB),
    )(value, earlier)


def quad_body(
    tokens,
    embed_table,
    norm_gain,
    input_proj,
    short_filter,
    pole_rate,
    residue,
    skip_gain,
    output_proj,
):
    genomes, rows = tokens.shape
    depth, branches, channels = input_proj.shape
    vocab, features = embed_table.shape
    members = lax.axis_size("ctx") // 2
    ctx, core, group = (lax.axis_index(name) for name in ("ctx", "chan", "groups"))
    quad, half = ctx % members, ctx // members
    place = jnp.stack([quad, half, group, core]).astype(jnp.int32)
    block = channels // members

    weights = input_proj.transpose(1, 0, 2)
    anywhere = pl.BlockSpec(memory_space=pl.ANY)
    packed = pl.pallas_call(
        pack_kernel,
        out_shape=[shaped(branches * depth + SPARE, LANES, dtype=bf16)] * members,
        in_specs=[anywhere, anywhere],
        out_specs=[anywhere] * members,
        scratch_shapes=[
            pltpu.VMEM((members, branches * depth + SPARE, LANES), bf16),
            pltpu.VMEM((genomes, rows), jnp.int32),
            pltpu.SemaphoreType.DMA,
            pltpu.SemaphoreType.DMA((members, branches)),
            pltpu.SemaphoreType.DMA((members,)),
        ],
        compiler_params=pltpu.CompilerParams(vmem_limit_bytes=61 * MIB),
    )(tokens, weights)
    gathered = [packed[0]] + [swapped(packed[m], "ctx", m) for m in range(1, members)]
    length = 2 * members * rows

    half_rows = output_proj.shape[0] // 2
    width = output_proj.shape[1]
    offered = pl.pallas_call(
        offer_kernel,
        out_shape=[shaped(half_rows // 2, width, dtype=bf16)] * 2,
        grid_spec=pltpu.PrefetchScalarGridSpec(
            num_scalar_prefetch=1,
            grid=(1,),
            in_specs=[pl.BlockSpec((half_rows, width), lambda i, place: (place[2], 0)), anywhere],
            out_specs=[pl.BlockSpec((half_rows // 2, width), lambda i, place: (0, 0))] * 2,
        ),
        compiler_params=pltpu.CompilerParams(vmem_limit_bytes=4 * MIB),
    )(place, output_proj, packed[1])
    count = 2 * members
    inner = [(i, count - 2 - i + 2 * (i % 2)) for i in range(members // 2, members + members // 2)]
    outer = [
        (i, count - 2 - i + 2 * (i % 2))
        for i in range(count)
        if not members // 2 <= i < members + members // 2
    ]

    part = features // 2
    step = 128
    normed = pl.pallas_call(
        norm_kernel,
        out_shape=shaped(vocab, part, dtype=bf16),
        grid_spec=pltpu.PrefetchScalarGridSpec(
            num_scalar_prefetch=1,
            grid=(vocab // step,),
            in_specs=[
                pl.BlockSpec((step, features), lambda i, place: (i, 0)),
                pl.BlockSpec((1, part), lambda i, place: (0, place[1])),
                pl.BlockSpec((step, part), lambda i, place: (i, place[1])),
                anywhere,
                anywhere,
            ],
            out_specs=pl.BlockSpec((step, part), lambda i, place: (i, 0)),
        ),
        compiler_params=pltpu.CompilerParams(vmem_limit_bytes=16 * MIB),
    )(place, embed_table, norm_gain.reshape(1, features), embed_table, gathered[2], packed[1])

    inner_fetched = [lax.ppermute(rows_part, "ctx", inner) for rows_part in offered]
    def partials(begin, count, spare, earlier=()):
        table_rows = count * (vocab // 2)
        return called(
            functools.partial(partial_kernel, begin=begin, count=count),
            [shaped(table_rows, LANES), shaped(table_rows + spare, LANES, dtype=bf16)],
            (),
            normed,
            *gathered,
            earlier=earlier,
        )

    def finished(keep, arrived):
        own = (keep + arrived[: keep.shape[0]].astype(f32)).astype(bf16)
        return own.reshape(-1, vocab // 2, LANES)

    pair_keep, pair_send = partials(0, 2, SPARE, tuple(inner_fetched))
    query_keep, query_send = partials(2, 1, 0)
    pair_arrived = swapped(pair_send, "ctx", members)
    query_arrived = swapped(query_send, "ctx", members)
    amp = residue * jnp.sqrt(-jnp.expm1(-2.0 * pole_rate))
    across = (LANES // pole_rate.shape[1] + 1) * CHUNK
    matrices, lines = called(
        prepare_kernel,
        [
            shaped(CHUNK, 2 * across + 2 * CHUNK, dtype=bf16),
            shaped(LANES + 8 * (branches + 1), LANES),
        ],
        (),
        pole_rate.T,
        amp.T,
        short_filter.transpose(0, 2, 1),
        skip_gain.reshape(-1, LANES),
        earlier=(pair_send,),
    )

    pair_own = after(finished(pair_keep, pair_arrived), matrices)
    query_own = finished(query_keep, query_arrived)
    pair_other = swapped(pair_own, "groups", 1)
    query_other = swapped(query_own, "groups", 1)

    span = length // 2
    value, picked = called(
        functools.partial(conv_kernel, genomes=genomes, rows=rows),
        [shaped(genomes * length, LANES), shaped(genomes * length, vocab, dtype=bf16)],
        (),
        pair_send,
        pair_arrived,
        pair_own,
        pair_other,
        matrices,
        lines,
    )
    *pieces, picked = called(
        functools.partial(gate_kernel, genomes=genomes),
        [shaped(span, LANES, dtype=bf16)] * 4 + [shaped(span, vocab, dtype=bf16)],
        (),
        picked,
        query_own,
        query_other,
        lines,
        value,
        scratch=[pltpu.VMEM((genomes * length, LANES), bf16)],
    )
    core_piece = swapped(pieces[1], "chan", 1)
    piece = jnp.stack(
        [
            pieces[0],
            core_piece,
            swapped(pieces[2], "ctx", members),
            swapped_both(pieces[3], members),
        ]
    )
    gated = [piece] + [swapped(piece, "ctx", m) for m in range(1, members)]

    outer_fetched = [lax.ppermute(after(rows_part, pair_own), "ctx", outer) for rows_part in offered]
    fetched = jnp.where(
        (ctx >= members // 2) & (ctx < members + members // 2),
        jnp.concatenate(inner_fetched),
        jnp.concatenate(outer_fetched),
    )
    fetched = after(fetched, piece)
    shared = swapped(fetched, "groups", 1)
    for ready in gated[1:]:
        shared = after(shared, ready)
    near, joined = called(
        near_kernel,
        [shaped(span, width, dtype=bf16), shaped(4 * 2, span, 2 * LANES, dtype=bf16)],
        (),
        picked,
        embed_table,
        *gated,
        output_proj,
        swapped(output_proj, "chan", 1),
        mib=24,
    )
    results = called(
        far_kernel,
        [shaped(span, width, dtype=bf16)] * 2,
        (),
        picked,
        embed_table,
        near,
        joined,
        fetched,
        swapped(fetched, "chan", 1),
        shared,
        swapped(shared, "chan", 1),
        mib=24,
    )
    kept, sent = results
    received = swapped(sent, "chan", 1)

    def rows_of(array, member):
        return lax.dynamic_slice_in_dim(array, member * rows, rows, 0)

    kept_parts = [rows_of(kept, quad)] + [
        swapped(rows_of(kept, quad ^ m), "ctx", m) for m in range(1, members)
    ]
    received_parts = [rows_of(received, quad)] + [
        swapped(rows_of(received, quad ^ m), "ctx", m) for m in range(1, members)
    ]
    return called(
        place_kernel,
        shaped(genomes, rows, members * width, dtype=bf16),
        (),
        *kept_parts,
        *received_parts,
    )


def solution(mesh):
    sizes = tuple(mesh.shape[name] for name in ("groups", "ctx", "chan"))
    return jax.shard_map(
        quad_body if sizes == (2, 8, 2) else general_body,
        mesh=mesh,
        in_specs=(
            P("groups", "ctx"),
            P(),
            P(),
            P("ctx", None, "chan"),
            P(None, "chan", None),
            P("chan", None),
            P("chan", None),
            P("chan"),
            P("chan", "ctx"),
        ),
        out_specs=P("groups", "ctx", "chan"),
        check_vma=False,
    )
```

```python
import functools

import jax
import jax.numpy as jnp
from jax import lax
from jax.experimental import pallas as pl
from jax.experimental.pallas import tpu as pltpu
from jax.sharding import PartitionSpec as P

epsilon = 1e-06
highest = lax.Precision.HIGHEST
f32 = jnp.float32
bf16 = jnp.bfloat16
CHUNK = 128
LANES = 128
MIB = 1024 * 1024
SPARE = 16


def passed_along(shard, axis, by):
    count = lax.axis_size(axis)
    pairs = [(i, i + by) for i in range(count) if 0 <= i + by < count]
    return lax.ppermute(shard, axis, pairs)


def entering(shard, axis, combine, identity):
    count, mine = (lax.axis_size(axis), lax.axis_index(axis))
    everything = jax.tree.map(lambda part: lax.all_gather(part, axis), shard)
    start = jax.tree.map(
        lambda part, zero: jnp.broadcast_to(jnp.asarray(zero, part.dtype), part.shape),
        shard,
        identity,
    )

    def hop(k, before):
        reached = k < mine
        new = combine(before, jax.tree.map(lambda part: part[k], everything))
        return jax.tree.map(lambda a, b: jnp.where(reached, a, b), new, before)

    return lax.fori_loop(0, count, hop, start)


def local_block(operands):
    rising, falling, inputs = operands
    length = rising.shape[2]
    toeplitz = jnp.einsum("gnt,gns->gts", rising, falling, precision=highest)
    causal = jnp.arange(length)[:, None] >= jnp.arange(length)[None, :]
    toeplitz = jnp.where(causal[None], toeplitz, 0.0)
    return jnp.einsum("gms,gts->gmt", inputs, toeplitz, precision=highest)


def lookup_rows(token_block, embed_table):
    vocab_count = embed_table.shape[0]
    onehot = (token_block[:, None] == jnp.arange(vocab_count, dtype=jnp.int32)[None, :]).astype(
        jnp.bfloat16
    )
    return jnp.dot(onehot, embed_table, preferred_element_type=jnp.float32)


def general_body(
    tokens,
    embed_table,
    norm_gain,
    input_proj,
    short_filter,
    pole_rate,
    residue,
    skip_gain,
    output_proj,
):
    genome_count, row_count = tokens.shape
    part_rows, branch_count, channels = input_proj.shape
    groups = pole_rate.shape[0]
    group_size = channels // groups
    tap_count = short_filter.shape[2]
    flat_count = genome_count * row_count
    flat_tokens = tokens.reshape(flat_count)
    widened = lookup_rows(flat_tokens, embed_table)
    inv_rms = lax.rsqrt(jnp.mean(widened * widened, axis=-1, keepdims=True) + epsilon)
    normed = (widened * inv_rms * norm_gain).astype(jnp.bfloat16)
    proj_cols = branch_count * channels
    flat_weight = input_proj.reshape(part_rows, proj_cols)
    spread = lax.all_to_all(normed, "ctx", split_axis=1, concat_axis=0, tiled=True)
    summed = lax.psum_scatter(
        jnp.dot(spread, flat_weight, preferred_element_type=jnp.float32),
        "ctx",
        scatter_dimension=0,
        tiled=True,
    )
    projected = summed.astype(jnp.bfloat16).reshape(genome_count, row_count, branch_count, channels)
    rim = passed_along(projected[:, row_count - (tap_count - 1) :], "ctx", 1)
    extended = jnp.concatenate([rim, projected], axis=1).astype(jnp.float32)
    taps_full = jnp.broadcast_to(
        short_filter[:, :, None, :], (branch_count, groups, group_size, tap_count)
    ).reshape(branch_count, channels, tap_count)
    filtered = jnp.zeros((genome_count, row_count, branch_count, channels), jnp.float32)
    for lag in range(tap_count):
        first_row = tap_count - 1 - lag
        filtered = filtered + taps_full[:, :, lag] * extended[:, first_row : first_row + row_count]
    query_part = filtered[:, :, 0]
    product = filtered[:, :, 1] * filtered[:, :, 2]
    mixes = genome_count * group_size
    grouped = (
        product.reshape(genome_count, row_count, groups, group_size)
        .transpose(2, 0, 3, 1)
        .reshape(groups, mixes, row_count)
    )
    positions = jnp.arange(row_count, dtype=jnp.float32)
    middle = float(row_count // 2)
    powers = jnp.exp(-pole_rate[:, :, None] * positions)
    next_powers = jnp.exp(-pole_rate[:, :, None] * (positions + 1.0))
    pole_amp = residue * jnp.sqrt(-jnp.expm1(-2.0 * pole_rate))
    rising = pole_amp[:, :, None] * jnp.exp(-pole_rate[:, :, None] * (positions - middle))
    falling = jnp.exp(-pole_rate[:, :, None] * (middle - positions))
    block_size = 8
    blocks = groups // block_size
    poles = pole_rate.shape[1]
    local_part = lax.map(
        local_block,
        (
            rising.reshape(blocks, block_size, poles, row_count),
            falling.reshape(blocks, block_size, poles, row_count),
            grouped.reshape(blocks, block_size, mixes, row_count),
        ),
    )
    local_part = local_part.reshape(groups, mixes, row_count)
    end_state = jnp.einsum("gms,gns->gmn", grouped, powers[:, :, ::-1], precision=highest)
    block_decay = jnp.exp(-pole_rate * row_count)

    def combine(earlier, later):
        return (earlier[0] * later[0], later[0][:, None, :] * earlier[1] + later[1])

    identity = (jnp.ones_like(block_decay), jnp.zeros_like(end_state))
    incoming = entering((block_decay, end_state), "ctx", combine, identity)[1]
    weighted = incoming * pole_amp[:, None, :]
    correction = jnp.einsum("gmn,gnt->gmt", weighted, next_powers, precision=highest)
    long_conv = (
        (local_part + correction)
        .reshape(groups, genome_count, group_size, row_count)
        .transpose(1, 3, 0, 2)
        .reshape(genome_count, row_count, channels)
    )
    gated = (
        (query_part * (long_conv + skip_gain * product))
        .astype(jnp.bfloat16)
        .reshape(flat_count, channels)
    )
    partial_value = jnp.dot(
        gated,
        lax.all_gather(output_proj, "ctx", axis=1, tiled=True),
        preferred_element_type=jnp.float32,
    )
    own_share = lax.psum_scatter(partial_value, "chan", scatter_dimension=1, tiled=True)
    half_width = own_share.shape[1]
    residual_part = lax.dynamic_slice_in_dim(
        widened, lax.axis_index("chan") * half_width, half_width, 1
    )
    block_out = (residual_part + own_share).astype(jnp.bfloat16)
    return block_out.reshape(genome_count, row_count, half_width)


def swapped(value, axis, mask):
    count = lax.axis_size(axis)
    return lax.ppermute(value, axis, [(i, i ^ mask) for i in range(count)])


def swapped_both(value, ctx_mask):
    count, cores = lax.axis_size("ctx"), lax.axis_size("chan")
    pairs = [
        (i * cores + c, (i ^ ctx_mask) * cores + (c ^ 1)) for i in range(count) for c in range(cores)
    ]
    return lax.ppermute(value, ("ctx", "chan"), pairs)


def split(value):
    high = value.astype(bf16)
    return high, (value - high.astype(f32)).astype(bf16)


def dot3(a_high, a_low, b):
    b_high, b_low = split(b)
    total = jnp.dot(a_high, b_high, preferred_element_type=f32)
    total += jnp.dot(a_low, b_high, preferred_element_type=f32)
    return total + jnp.dot(a_high, b_low, preferred_element_type=f32)


def lane_half(shape):
    return lax.broadcasted_iota(jnp.int32, shape, len(shape) - 1) < LANES // 2


def half_turn(value):
    return pltpu.roll(value, LANES // 2, value.ndim - 1)


def norm_kernel(place_ref, table_ref, gain_ref, part_ref, pair_ref, query_ref, out_ref):
    del place_ref, pair_ref, query_ref
    widened = table_ref[...].astype(f32)
    mean = jnp.sum(widened * widened, axis=1, keepdims=True) / widened.shape[1]
    own = part_ref[...].astype(f32)
    out_ref[...] = (own * lax.rsqrt(mean + epsilon) * gain_ref[...]).astype(bf16)


def pack_kernel(tokens_ref, weight_ref, *refs):
    out_refs, (held_ref, token_ref, token_sem, in_sems, out_sems) = refs[:-5], refs[-5:]
    branches, depth, channels = weight_ref.shape
    members = len(out_refs)
    quad, group = lax.axis_index("ctx") % members, lax.axis_index("groups")
    block = channels // members
    order = (1, 2, 3, 0)
    fetch = pltpu.make_async_copy(tokens_ref, token_ref, token_sem)
    fetch.start()
    copies = {}
    for m in order:
        first = pl.multiple_of((quad ^ m) * block + group * LANES, LANES)
        for i, j in enumerate((1, 2, 0)):
            copies[m, i] = pltpu.make_async_copy(
                weight_ref.at[j, :, pl.ds(first, LANES)],
                held_ref.at[m, pl.ds(i * depth, depth), :],
                in_sems.at[m, i],
            )
            copies[m, i].start()
    rows = token_ref.shape[1]
    row = lax.broadcasted_iota(jnp.int32, (SPARE, rows), 0)
    fetch.wait()
    token = jnp.where(row % 4 < 2, token_ref[0:1, :], token_ref[1:2, :])
    token = jnp.where(row % 2 == 0, token >> 8, token & 255)
    token = jnp.where(row // 4 == quad, token, 0).astype(f32).astype(bf16)
    for m in order:
        held_ref[m, branches * depth :, :] = jnp.zeros((SPARE, LANES), bf16)
        held_ref[m, branches * depth :, :rows] = token
    results = []
    for m in order:
        for i in range(branches):
            copies[m, i].wait()
        results.append(pltpu.make_async_copy(held_ref.at[m], out_refs[m], out_sems.at[m]))
        results[-1].start()
    for result in results:
        result.wait()


def here():
    members = lax.axis_size("ctx") // 2
    ctx = lax.axis_index("ctx")
    return ctx % members, ctx // members, lax.axis_index("groups"), lax.axis_index("chan")


def pick(half, near_ref, far_ref, picked_ref, genomes, rows):
    vocab = picked_ref.shape[1]
    length = picked_ref.shape[0] // genomes
    first = near_ref.shape[0] - SPARE
    diagonal = lax.broadcasted_iota(jnp.int32, (rows, rows), 0) == lax.broadcasted_iota(
        jnp.int32, (rows, rows), 1
    )
    entries = lax.broadcasted_iota(jnp.int32, (rows, vocab), 1).astype(f32)
    for other, ref in enumerate((near_ref, far_ref)):
        parts = ref[first:, :rows].astype(f32)
        for member in range(length // (2 * rows)):
            for b in range(genomes):
                at = 4 * member + 2 * b
                line = parts[at : at + 1] * 256.0 + parts[at + 1 : at + 2]
                column = jnp.sum(jnp.where(diagonal, line, 0.0), axis=1, keepdims=True)
                place = b * length + (half ^ other) * (length // 2) + member * rows
                picked_ref[pl.ds(pl.multiple_of(place, rows), rows), :] = (
                    (column == entries).astype(f32).astype(bf16)
                )


def prepare_kernel(rate_ref, amp_ref, taps_ref, skip_ref, matrices_ref, rows_ref):
    quad, half, _, _ = here()

    group_count = rate_ref.shape[1]
    poles = rate_ref.shape[0]
    count = LANES // poles

    def group_at(lane):
        place = lane // poles
        return quad * (2 * count) + (place // (count // 2)) * count + half * (count // 2) + place % (count // 2)

    lane = lax.broadcasted_iota(jnp.int32, (group_count, LANES), 1)
    chosen = (lax.broadcasted_iota(jnp.int32, (group_count, LANES), 0) == group_at(lane)).astype(f32)
    turned_lane = lax.broadcasted_iota(jnp.int32, (LANES, group_count), 0)
    turned = (lax.broadcasted_iota(jnp.int32, (LANES, group_count), 1) == group_at(turned_lane)).astype(f32)

    def along_lanes(ref):
        spread = jnp.dot(ref[...], chosen, precision=highest, preferred_element_type=f32)
        keep = lax.broadcasted_iota(jnp.int32, spread.shape, 0) == lax.broadcasted_iota(
            jnp.int32, spread.shape, 1
        ) % poles
        return jnp.sum(jnp.where(keep, spread, 0.0), axis=0, keepdims=True)

    rate, amp = along_lanes(rate_ref), along_lanes(amp_ref)
    spread = lax.dot_general(
        turned, rate_ref[...], (((1,), (1,)), ((), ())), precision=highest, preferred_element_type=f32
    )
    keep = lax.broadcasted_iota(jnp.int32, spread.shape, 1) == lax.broadcasted_iota(
        jnp.int32, spread.shape, 0
    ) % poles
    rate_col = jnp.sum(jnp.where(keep, spread, 0.0), axis=1, keepdims=True)

    square = (CHUNK, LANES)
    row = lax.broadcasted_iota(jnp.int32, square, 0)
    col = lax.broadcasted_iota(jnp.int32, square, 1)
    at = row.astype(f32)
    middle = float(CHUNK // 2)
    rising = amp * jnp.exp(-rate * (at - middle))
    falling = jnp.exp(-rate * (middle - at))
    width = (count + 1) * CHUNK
    for g in range(count):
        own = jnp.where(col // poles == g, falling, 0.0)
        block = lax.dot_general(
            rising, own, (((1,), (1,)), ((), ())), precision=highest, preferred_element_type=f32
        )
        high, low = split(jnp.where(row >= col, block, 0.0))
        matrices_ref[:, g * CHUNK : (g + 1) * CHUNK] = high
        matrices_ref[:, width + g * CHUNK : width + (g + 1) * CHUNK] = low
    high, low = split(amp * jnp.exp(-rate * (at + 1.0)))
    matrices_ref[:, count * CHUNK : width] = high
    matrices_ref[:, width + count * CHUNK : 2 * width] = low
    high, low = split(jnp.exp(-rate_col * (float(CHUNK - 1) - col.astype(f32))))
    matrices_ref[:, 2 * width : 2 * width + CHUNK] = high
    matrices_ref[:, 2 * width + CHUNK :] = low

    rows_ref[:LANES] = jnp.exp(-rate_col * float(CHUNK)) + jnp.zeros(square, f32)
    branches = taps_ref.shape[0]
    for j in range(branches):
        taps = jnp.dot(taps_ref[j], chosen, precision=highest, preferred_element_type=f32)
        rows_ref[LANES + 8 * j : LANES + 8 * j + taps.shape[0]] = taps
    upper = skip_ref[pl.ds(2 * quad, 1), :]
    lower = skip_ref[pl.ds(2 * quad + 1, 1), :]
    upper = jnp.where(half == 0, upper, half_turn(upper))
    lower = jnp.where(half == 1, lower, half_turn(lower))
    end = LANES + 8 * branches
    rows_ref[end : end + 1] = jnp.where(lane_half(upper.shape), upper, lower)


def partial_kernel(normed_ref, *refs, begin, count):
    weight_refs, (keep_ref, send_ref) = refs[:-2], refs[-2:]
    quad, half, _, _ = here()
    rows, features = normed_ref.shape
    depth = features // len(weight_refs)
    total = jnp.zeros((rows, count * LANES), f32)
    tokens = jnp.zeros((SPARE, LANES), f32)
    for m, weight_ref in enumerate(weight_refs):
        first = pl.multiple_of((quad ^ m) * depth, depth)
        columns = jnp.concatenate(
            [weight_ref[j * depth : (j + 1) * depth, :] for j in range(begin, begin + count)], axis=1
        )
        total += jnp.dot(
            normed_ref[:, pl.ds(first, depth)], columns, preferred_element_type=f32
        )
        tokens += weight_ref[weight_ref.shape[0] - SPARE :, :].astype(f32)
    part = rows // 2
    for j in range(count):
        mine = total[:, j * LANES : (j + 1) * LANES]
        mine = jnp.where(half == 0, mine, half_turn(mine))
        top, bottom = mine[:part], mine[part:]
        left = lane_half(top.shape)
        keep_ref[j * part : (j + 1) * part, :] = jnp.where(left, top, half_turn(bottom))
        send_ref[j * part : (j + 1) * part, :] = jnp.where(left, half_turn(top), bottom).astype(bf16)
    if send_ref.shape[0] > count * part:
        send_ref[count * part :, :] = tokens.astype(bf16)


def filtered_branch(group, picked, row, mine, theirs, rows_ref, branch):
    mine, theirs = mine.astype(f32), theirs.astype(f32)
    first = jnp.where(group == 0, mine, theirs)
    second = jnp.where(group == 0, theirs, mine)
    left = lane_half(first.shape)
    top = jnp.where(left, first, half_turn(second))
    bottom = jnp.where(left, half_turn(first), second)
    table = jnp.concatenate([top, bottom], axis=0).astype(bf16)
    now = jnp.dot(picked, table, preferred_element_type=f32)
    first_tap = LANES + 8 * branch
    total = rows_ref[first_tap : first_tap + 1] * now
    for lag in range(1, 3):
        late = jnp.where(row >= lag, pltpu.roll(now, lag, 0), 0.0)
        total += rows_ref[first_tap + lag : first_tap + lag + 1] * late
    return total


def conv_kernel(
    near_ref, far_ref, own_ref, other_ref, matrices_ref, rows_ref, value_ref, picked_ref, *, genomes, rows
):
    _, half, group, _ = here()
    pick(half, near_ref, far_ref, picked_ref, genomes, rows)
    positions = picked_ref.shape[0]
    length = positions // genomes
    row = lax.broadcasted_iota(jnp.int32, (positions, LANES), 0) % length
    picked = picked_ref[...]
    key, value = (
        filtered_branch(group, picked, row, own_ref[j - 1], other_ref[j - 1], rows_ref, j)
        for j in (1, 2)
    )
    product = key * value
    size = 16
    count = LANES // size
    width = genomes * LANES
    lane = lax.broadcasted_iota(jnp.int32, (CHUNK, width), 1) % LANES
    pole_row = lax.broadcasted_iota(jnp.int32, (LANES, width), 0)
    same = pole_row // size == (lax.broadcasted_iota(jnp.int32, (LANES, width), 1) % LANES) // size
    fade = jnp.concatenate([rows_ref[:LANES]] * genomes, axis=1)
    skip = rows_ref[rows_ref.shape[0] - 8 : rows_ref.shape[0] - 7]
    across = (count + 1) * CHUNK
    high, low = matrices_ref[:, :across], matrices_ref[:, across : 2 * across]
    ends_high = matrices_ref[:, 2 * across : 2 * across + CHUNK]
    ends_low = matrices_ref[:, 2 * across + CHUNK :]
    state = jnp.zeros((LANES, width), f32)
    chunks = length // CHUNK
    for c in range(chunks):
        spans = [slice(b * length + c * CHUNK, b * length + (c + 1) * CHUNK) for b in range(genomes)]
        block = jnp.concatenate([product[span] for span in spans], axis=1)
        stacked = jnp.concatenate(
            [jnp.where(lane // size == g, block, 0.0) for g in range(count)] + [state], axis=0
        )
        conv = dot3(high, low, stacked)
        for b, span in enumerate(spans):
            value_ref[span, :] = conv[:, b * LANES : (b + 1) * LANES] + skip * product[span]
        if c < chunks - 1:
            ends = dot3(ends_high, ends_low, block)
            state = fade * state + jnp.where(same, ends, 0.0)


def gate_kernel(picked_ref, own_ref, other_ref, rows_ref, value_ref, *refs, genomes):
    piece_refs, (mine_ref, held_ref) = refs[:4], refs[4:]
    _, half, group, core = here()
    positions = picked_ref.shape[0]
    length = positions // genomes
    row = lax.broadcasted_iota(jnp.int32, (positions, LANES), 0) % length
    query = filtered_branch(group, picked_ref[...], row, own_ref[0], other_ref[0], rows_ref, 0)
    held_ref[...] = (query * value_ref[...]).astype(bf16)
    part = length // 2
    for r, piece_ref in enumerate(piece_refs):
        place = 2 * (core ^ (r % 2)) + (half ^ (r // 2))
        piece_ref[...] = held_ref[pl.ds(pl.multiple_of(place * part, part), part), :]
    mine_ref[...] = picked_ref[pl.ds(pl.multiple_of((2 * core + half) * part, part), part), :]


def offer_kernel(place_ref, rows_ref, packed_ref, first_ref, second_ref):
    del place_ref, packed_ref
    count = first_ref.shape[0]
    first_ref[...] = rows_ref[:count]
    second_ref[...] = rows_ref[count:]


def residual(picked_ref, table_ref, first, width):
    return jnp.dot(
        picked_ref[...],
        table_ref[:, pl.ds(pl.multiple_of(first, width), width)],
        preferred_element_type=f32,
    )


def near_kernel(picked_ref, table_ref, *refs):
    piece_refs, refs = refs[:4], refs[4:]
    own_ref, core_ref, fetched_ref, core_fetched_ref, out_ref, part_ref, joined_ref = refs
    quad, half, group, _ = here()
    block = 2 * LANES
    for m, piece_ref in enumerate(piece_refs):
        for other_core in (0, 1):
            near = piece_ref[other_core].astype(f32)
            far = piece_ref[2 + other_core].astype(f32)
            first = jnp.where(half == 0, near, far)
            second = jnp.where(half == 0, far, near)
            left = lane_half(first.shape)
            pair = [
                jnp.where(left, first, half_turn(second)),
                jnp.where(left, half_turn(first), second),
            ]
            joined_ref[2 * (quad ^ m) + other_core] = jnp.concatenate(pair, axis=1).astype(bf16)
    width = own_ref.shape[1]
    total = jnp.zeros(out_ref.shape, f32)
    for member in range(4):
        rows = slice(member * block, (member + 1) * block)
        for other_core, ref in enumerate((own_ref, core_ref)):
            total += jnp.dot(
                joined_ref[2 * member + other_core], ref[rows, :], preferred_element_type=f32
            )
    total += residual(picked_ref, table_ref, (4 * half + quad) * width, width)
    out_ref[...] = total.astype(bf16)
    part = residual(picked_ref, table_ref, (4 * (half ^ 1) + (quad ^ 2)) * width, width)
    for i in (0, 1):
        rows = slice(i * block, (i + 1) * block)
        for other_core, ref in enumerate((fetched_ref, core_fetched_ref)):
            part += jnp.dot(
                joined_ref[2 * (2 * group + i) + other_core],
                ref[rows, :],
                preferred_element_type=f32,
            )
    part_ref[...] = part


def far_kernel(near_ref, part_ref, joined_ref, shared_ref, core_shared_ref, kept_ref, sent_ref):
    _, half, group, core = here()
    block = 2 * LANES
    total = part_ref[...]
    for i in (0, 1):
        rows = slice(i * block, (i + 1) * block)
        for other_core, ref in enumerate((shared_ref, core_shared_ref)):
            total += jnp.dot(
                joined_ref[2 * (2 * (group ^ 1) + i) + other_core],
                ref[rows, :],
                preferred_element_type=f32,
            )
    near, far = near_ref[...], total.astype(bf16)
    kept_ref[...] = jnp.where(half == core, near, far)
    sent_ref[...] = jnp.where(half == core, far, near)


def place_kernel(*refs):
    part_refs, out_ref = refs[:8], refs[8]
    quad, half, _, core = here()
    width = part_refs[0].shape[1]
    for g in (0, 1):
        for m in range(4):
            first = pl.multiple_of((quad ^ m ^ (2 * (half ^ core))) * width, width)
            out_ref[core ^ g, :, pl.ds(first, width)] = part_refs[4 * g + m][...]


def called(kernel, out_shape, scalars, *operands, scratch=(), mib=16, earlier=()):
    smem = pl.BlockSpec(memory_space=pltpu.SMEM)
    vmem = pl.BlockSpec(memory_space=pltpu.VMEM)
    anywhere = pl.BlockSpec(memory_space=pl.ANY)
    many = isinstance(out_shape, (list, tuple))
    inputs, waits = len(scalars) + len(operands), len(earlier)

    def body(*refs):
        kernel(*refs[:inputs], *refs[inputs + waits :])

    return pl.pallas_call(
        body,
        out_shape=out_shape,
        in_specs=[smem] * len(scalars) + [vmem] * len(operands) + [anywhere] * waits,
        out_specs=[vmem] * len(out_shape) if many else vmem,
        scratch_shapes=scratch,
        compiler_params=pltpu.CompilerParams(vmem_limit_bytes=mib * MIB),
    )(*scalars, *operands, *earlier)


def shaped(*shape, dtype=f32):
    return jax.ShapeDtypeStruct(shape, dtype)


def pass_kernel(*refs):
    del refs


def after(value, earlier):
    return pl.pallas_call(
        pass_kernel,
        out_shape=shaped(*value.shape, dtype=value.dtype),
        in_specs=[pl.BlockSpec(memory_space=pl.ANY)] * 2,
        out_specs=pl.BlockSpec(memory_space=pl.ANY),
        input_output_aliases={0: 0},
        compiler_params=pltpu.CompilerParams(vmem_limit_bytes=MIB),
    )(value, earlier)


def quad_body(
    tokens,
    embed_table,
    norm_gain,
    input_proj,
    short_filter,
    pole_rate,
    residue,
    skip_gain,
    output_proj,
):
    genomes, rows = tokens.shape
    depth, branches, channels = input_proj.shape
    vocab, features = embed_table.shape
    members = lax.axis_size("ctx") // 2
    ctx, core, group = (lax.axis_index(name) for name in ("ctx", "chan", "groups"))
    quad, half = ctx % members, ctx // members
    place = jnp.stack([quad, half, group, core]).astype(jnp.int32)
    block = channels // members

    weights = input_proj.transpose(1, 0, 2)
    anywhere = pl.BlockSpec(memory_space=pl.ANY)
    packed = pl.pallas_call(
        pack_kernel,
        out_shape=[shaped(branches * depth + SPARE, LANES, dtype=bf16)] * members,
        in_specs=[anywhere, anywhere],
        out_specs=[anywhere] * members,
        scratch_shapes=[
            pltpu.VMEM((members, branches * depth + SPARE, LANES), bf16),
            pltpu.VMEM((genomes, rows), jnp.int32),
            pltpu.SemaphoreType.DMA,
            pltpu.SemaphoreType.DMA((members, branches)),
            pltpu.SemaphoreType.DMA((members,)),
        ],
        compiler_params=pltpu.CompilerParams(vmem_limit_bytes=61 * MIB),
    )(tokens, weights)
    gathered = [packed[0]] + [swapped(packed[m], "ctx", m) for m in range(1, members)]
    length = 2 * members * rows

    half_rows = output_proj.shape[0] // 2
    width = output_proj.shape[1]
    offered = pl.pallas_call(
        offer_kernel,
        out_shape=[shaped(half_rows // 2, width, dtype=bf16)] * 2,
        grid_spec=pltpu.PrefetchScalarGridSpec(
            num_scalar_prefetch=1,
            grid=(1,),
            in_specs=[pl.BlockSpec((half_rows, width), lambda i, place: (place[2], 0)), anywhere],
            out_specs=[pl.BlockSpec((half_rows // 2, width), lambda i, place: (0, 0))] * 2,
        ),
        compiler_params=pltpu.CompilerParams(vmem_limit_bytes=4 * MIB),
    )(place, output_proj, packed[1])
    count = 2 * members
    inner = [(i, count - 2 - i + 2 * (i % 2)) for i in range(members // 2, members + members // 2)]
    outer = [
        (i, count - 2 - i + 2 * (i % 2))
        for i in range(count)
        if not members // 2 <= i < members + members // 2
    ]

    part = features // 2
    step = 128
    normed = pl.pallas_call(
        norm_kernel,
        out_shape=shaped(vocab, part, dtype=bf16),
        grid_spec=pltpu.PrefetchScalarGridSpec(
            num_scalar_prefetch=1,
            grid=(vocab // step,),
            in_specs=[
                pl.BlockSpec((step, features), lambda i, place: (i, 0)),
                pl.BlockSpec((1, part), lambda i, place: (0, place[1])),
                pl.BlockSpec((step, part), lambda i, place: (i, place[1])),
                anywhere,
                anywhere,
            ],
            out_specs=pl.BlockSpec((step, part), lambda i, place: (i, 0)),
        ),
        compiler_params=pltpu.CompilerParams(vmem_limit_bytes=16 * MIB),
    )(place, embed_table, norm_gain.reshape(1, features), embed_table, gathered[2], packed[1])

    inner_fetched = [lax.ppermute(rows_part, "ctx", inner) for rows_part in offered]
    def partials(begin, count, spare, earlier=()):
        table_rows = count * (vocab // 2)
        return called(
            functools.partial(partial_kernel, begin=begin, count=count),
            [shaped(table_rows, LANES), shaped(table_rows + spare, LANES, dtype=bf16)],
            (),
            normed,
            *gathered,
            earlier=earlier,
        )

    def finished(keep, arrived):
        own = (keep + arrived[: keep.shape[0]].astype(f32)).astype(bf16)
        return own.reshape(-1, vocab // 2, LANES)

    pair_keep, pair_send = partials(0, 2, SPARE, tuple(inner_fetched))
    query_keep, query_send = partials(2, 1, 0)
    pair_arrived = swapped(pair_send, "ctx", members)
    query_arrived = swapped(query_send, "ctx", members)
    amp = residue * jnp.sqrt(-jnp.expm1(-2.0 * pole_rate))
    across = (LANES // pole_rate.shape[1] + 1) * CHUNK
    matrices, lines = called(
        prepare_kernel,
        [
            shaped(CHUNK, 2 * across + 2 * CHUNK, dtype=bf16),
            shaped(LANES + 8 * (branches + 1), LANES),
        ],
        (),
        pole_rate.T,
        amp.T,
        short_filter.transpose(0, 2, 1),
        skip_gain.reshape(-1, LANES),
        earlier=(pair_send,),
    )

    pair_own = after(finished(pair_keep, pair_arrived), matrices)
    query_own = finished(query_keep, query_arrived)
    pair_other = swapped(pair_own, "groups", 1)
    query_other = swapped(query_own, "groups", 1)

    span = length // 2
    value, picked = called(
        functools.partial(conv_kernel, genomes=genomes, rows=rows),
        [shaped(genomes * length, LANES), shaped(genomes * length, vocab, dtype=bf16)],
        (),
        pair_send,
        pair_arrived,
        pair_own,
        pair_other,
        matrices,
        lines,
    )
    *pieces, picked = called(
        functools.partial(gate_kernel, genomes=genomes),
        [shaped(span, LANES, dtype=bf16)] * 4 + [shaped(span, vocab, dtype=bf16)],
        (),
        picked,
        query_own,
        query_other,
        lines,
        value,
        scratch=[pltpu.VMEM((genomes * length, LANES), bf16)],
    )
    core_piece = swapped(pieces[1], "chan", 1)
    piece = jnp.stack(
        [
            pieces[0],
            core_piece,
            swapped(pieces[2], "ctx", members),
            swapped_both(pieces[3], members),
        ]
    )
    gated = [piece] + [swapped(piece, "ctx", m) for m in range(1, members)]

    outer_fetched = [lax.ppermute(after(rows_part, pair_own), "ctx", outer) for rows_part in offered]
    fetched = jnp.where(
        (ctx >= members // 2) & (ctx < members + members // 2),
        jnp.concatenate(inner_fetched),
        jnp.concatenate(outer_fetched),
    )
    fetched = after(fetched, piece)
    shared = swapped(fetched, "groups", 1)
    for ready in gated[1:]:
        shared = after(shared, ready)
    near, part_far, joined = called(
        near_kernel,
        [
            shaped(span, width, dtype=bf16),
            shaped(span, width),
            shaped(4 * 2, span, 2 * LANES, dtype=bf16),
        ],
        (),
        picked,
        embed_table,
        *gated,
        output_proj,
        swapped(output_proj, "chan", 1),
        fetched,
        swapped(fetched, "chan", 1),
        mib=24,
    )
    results = called(
        far_kernel,
        [shaped(span, width, dtype=bf16)] * 2,
        (),
        near,
        part_far,
        joined,
        shared,
        swapped(shared, "chan", 1),
        mib=24,
    )
    kept, sent = results
    received = swapped(sent, "chan", 1)

    def rows_of(array, member):
        return lax.dynamic_slice_in_dim(array, member * rows, rows, 0)

    kept_parts = [rows_of(kept, quad)] + [
        swapped(rows_of(kept, quad ^ m), "ctx", m) for m in range(1, members)
    ]
    received_parts = [rows_of(received, quad)] + [
        swapped(rows_of(received, quad ^ m), "ctx", m) for m in range(1, members)
    ]
    return called(
        place_kernel,
        shaped(genomes, rows, members * width, dtype=bf16),
        (),
        *kept_parts,
        *received_parts,
    )


def solution(mesh):
    sizes = tuple(mesh.shape[name] for name in ("groups", "ctx", "chan"))
    return jax.shard_map(
        quad_body if sizes == (2, 8, 2) else general_body,
        mesh=mesh,
        in_specs=(
            P("groups", "ctx"),
            P(),
            P(),
            P("ctx", None, "chan"),
            P(None, "chan", None),
            P("chan", None),
            P("chan", None),
            P("chan"),
            P("chan", "ctx"),
        ),
        out_specs=P("groups", "ctx", "chan"),
        check_vma=False,
    )
```

```python
import functools

import jax
import jax.numpy as jnp
from jax import lax
from jax.experimental import pallas as pl
from jax.experimental.pallas import tpu as pltpu
from jax.sharding import PartitionSpec as P

epsilon = 1e-06
highest = lax.Precision.HIGHEST
f32 = jnp.float32
bf16 = jnp.bfloat16
CHUNK = 128
LANES = 128
MIB = 1024 * 1024
SPARE = 16


def passed_along(shard, axis, by):
    count = lax.axis_size(axis)
    pairs = [(i, i + by) for i in range(count) if 0 <= i + by < count]
    return lax.ppermute(shard, axis, pairs)


def entering(shard, axis, combine, identity):
    count, mine = (lax.axis_size(axis), lax.axis_index(axis))
    everything = jax.tree.map(lambda part: lax.all_gather(part, axis), shard)
    start = jax.tree.map(
        lambda part, zero: jnp.broadcast_to(jnp.asarray(zero, part.dtype), part.shape),
        shard,
        identity,
    )

    def hop(k, before):
        reached = k < mine
        new = combine(before, jax.tree.map(lambda part: part[k], everything))
        return jax.tree.map(lambda a, b: jnp.where(reached, a, b), new, before)

    return lax.fori_loop(0, count, hop, start)


def local_block(operands):
    rising, falling, inputs = operands
    length = rising.shape[2]
    toeplitz = jnp.einsum("gnt,gns->gts", rising, falling, precision=highest)
    causal = jnp.arange(length)[:, None] >= jnp.arange(length)[None, :]
    toeplitz = jnp.where(causal[None], toeplitz, 0.0)
    return jnp.einsum("gms,gts->gmt", inputs, toeplitz, precision=highest)


def lookup_rows(token_block, embed_table):
    vocab_count = embed_table.shape[0]
    onehot = (token_block[:, None] == jnp.arange(vocab_count, dtype=jnp.int32)[None, :]).astype(
        jnp.bfloat16
    )
    return jnp.dot(onehot, embed_table, preferred_element_type=jnp.float32)


def general_body(
    tokens,
    embed_table,
    norm_gain,
    input_proj,
    short_filter,
    pole_rate,
    residue,
    skip_gain,
    output_proj,
):
    genome_count, row_count = tokens.shape
    part_rows, branch_count, channels = input_proj.shape
    groups = pole_rate.shape[0]
    group_size = channels // groups
    tap_count = short_filter.shape[2]
    flat_count = genome_count * row_count
    flat_tokens = tokens.reshape(flat_count)
    widened = lookup_rows(flat_tokens, embed_table)
    inv_rms = lax.rsqrt(jnp.mean(widened * widened, axis=-1, keepdims=True) + epsilon)
    normed = (widened * inv_rms * norm_gain).astype(jnp.bfloat16)
    proj_cols = branch_count * channels
    flat_weight = input_proj.reshape(part_rows, proj_cols)
    spread = lax.all_to_all(normed, "ctx", split_axis=1, concat_axis=0, tiled=True)
    summed = lax.psum_scatter(
        jnp.dot(spread, flat_weight, preferred_element_type=jnp.float32),
        "ctx",
        scatter_dimension=0,
        tiled=True,
    )
    projected = summed.astype(jnp.bfloat16).reshape(genome_count, row_count, branch_count, channels)
    rim = passed_along(projected[:, row_count - (tap_count - 1) :], "ctx", 1)
    extended = jnp.concatenate([rim, projected], axis=1).astype(jnp.float32)
    taps_full = jnp.broadcast_to(
        short_filter[:, :, None, :], (branch_count, groups, group_size, tap_count)
    ).reshape(branch_count, channels, tap_count)
    filtered = jnp.zeros((genome_count, row_count, branch_count, channels), jnp.float32)
    for lag in range(tap_count):
        first_row = tap_count - 1 - lag
        filtered = filtered + taps_full[:, :, lag] * extended[:, first_row : first_row + row_count]
    query_part = filtered[:, :, 0]
    product = filtered[:, :, 1] * filtered[:, :, 2]
    mixes = genome_count * group_size
    grouped = (
        product.reshape(genome_count, row_count, groups, group_size)
        .transpose(2, 0, 3, 1)
        .reshape(groups, mixes, row_count)
    )
    positions = jnp.arange(row_count, dtype=jnp.float32)
    middle = float(row_count // 2)
    powers = jnp.exp(-pole_rate[:, :, None] * positions)
    next_powers = jnp.exp(-pole_rate[:, :, None] * (positions + 1.0))
    pole_amp = residue * jnp.sqrt(-jnp.expm1(-2.0 * pole_rate))
    rising = pole_amp[:, :, None] * jnp.exp(-pole_rate[:, :, None] * (positions - middle))
    falling = jnp.exp(-pole_rate[:, :, None] * (middle - positions))
    block_size = 8
    blocks = groups // block_size
    poles = pole_rate.shape[1]
    local_part = lax.map(
        local_block,
        (
            rising.reshape(blocks, block_size, poles, row_count),
            falling.reshape(blocks, block_size, poles, row_count),
            grouped.reshape(blocks, block_size, mixes, row_count),
        ),
    )
    local_part = local_part.reshape(groups, mixes, row_count)
    end_state = jnp.einsum("gms,gns->gmn", grouped, powers[:, :, ::-1], precision=highest)
    block_decay = jnp.exp(-pole_rate * row_count)

    def combine(earlier, later):
        return (earlier[0] * later[0], later[0][:, None, :] * earlier[1] + later[1])

    identity = (jnp.ones_like(block_decay), jnp.zeros_like(end_state))
    incoming = entering((block_decay, end_state), "ctx", combine, identity)[1]
    weighted = incoming * pole_amp[:, None, :]
    correction = jnp.einsum("gmn,gnt->gmt", weighted, next_powers, precision=highest)
    long_conv = (
        (local_part + correction)
        .reshape(groups, genome_count, group_size, row_count)
        .transpose(1, 3, 0, 2)
        .reshape(genome_count, row_count, channels)
    )
    gated = (
        (query_part * (long_conv + skip_gain * product))
        .astype(jnp.bfloat16)
        .reshape(flat_count, channels)
    )
    partial_value = jnp.dot(
        gated,
        lax.all_gather(output_proj, "ctx", axis=1, tiled=True),
        preferred_element_type=jnp.float32,
    )
    own_share = lax.psum_scatter(partial_value, "chan", scatter_dimension=1, tiled=True)
    half_width = own_share.shape[1]
    residual_part = lax.dynamic_slice_in_dim(
        widened, lax.axis_index("chan") * half_width, half_width, 1
    )
    block_out = (residual_part + own_share).astype(jnp.bfloat16)
    return block_out.reshape(genome_count, row_count, half_width)


def swapped(value, axis, mask):
    count = lax.axis_size(axis)
    return lax.ppermute(value, axis, [(i, i ^ mask) for i in range(count)])


def swapped_both(value, ctx_mask):
    count, cores = lax.axis_size("ctx"), lax.axis_size("chan")
    pairs = [
        (i * cores + c, (i ^ ctx_mask) * cores + (c ^ 1)) for i in range(count) for c in range(cores)
    ]
    return lax.ppermute(value, ("ctx", "chan"), pairs)


def split(value):
    high = value.astype(bf16)
    return high, (value - high.astype(f32)).astype(bf16)


def dot3(a_high, a_low, b):
    b_high, b_low = split(b)
    total = jnp.dot(a_high, b_high, preferred_element_type=f32)
    total += jnp.dot(a_low, b_high, preferred_element_type=f32)
    return total + jnp.dot(a_high, b_low, preferred_element_type=f32)


def lane_half(shape):
    return lax.broadcasted_iota(jnp.int32, shape, len(shape) - 1) < LANES // 2


def half_turn(value):
    return pltpu.roll(value, LANES // 2, value.ndim - 1)


def norm_kernel(place_ref, table_ref, gain_ref, part_ref, pair_ref, query_ref, out_ref):
    del place_ref, pair_ref, query_ref
    widened = table_ref[...].astype(f32)
    mean = jnp.sum(widened * widened, axis=1, keepdims=True) / widened.shape[1]
    own = part_ref[...].astype(f32)
    out_ref[...] = (own * lax.rsqrt(mean + epsilon) * gain_ref[...]).astype(bf16)


def pack_kernel(tokens_ref, weight_ref, *refs):
    out_refs, (held_ref, token_ref, token_sem, in_sems, out_sems) = refs[:-5], refs[-5:]
    branches, depth, channels = weight_ref.shape
    members = len(out_refs)
    quad, group = lax.axis_index("ctx") % members, lax.axis_index("groups")
    block = channels // members
    order = (1, 2, 3, 0)
    fetch = pltpu.make_async_copy(tokens_ref, token_ref, token_sem)
    fetch.start()
    copies = {}
    for m in order:
        first = pl.multiple_of((quad ^ m) * block + group * LANES, LANES)
        for i, j in enumerate((1, 2, 0)):
            copies[m, i] = pltpu.make_async_copy(
                weight_ref.at[j, :, pl.ds(first, LANES)],
                held_ref.at[m, pl.ds(i * depth, depth), :],
                in_sems.at[m, i],
            )
            copies[m, i].start()
    rows = token_ref.shape[1]
    row = lax.broadcasted_iota(jnp.int32, (SPARE, rows), 0)
    fetch.wait()
    token = jnp.where(row % 4 < 2, token_ref[0:1, :], token_ref[1:2, :])
    token = jnp.where(row % 2 == 0, token >> 8, token & 255)
    token = jnp.where(row // 4 == quad, token, 0).astype(f32).astype(bf16)
    for m in order:
        held_ref[m, branches * depth :, :] = jnp.zeros((SPARE, LANES), bf16)
        held_ref[m, branches * depth :, :rows] = token
    results = []
    for m in order:
        for i in range(branches):
            copies[m, i].wait()
        results.append(pltpu.make_async_copy(held_ref.at[m], out_refs[m], out_sems.at[m]))
        results[-1].start()
    for result in results:
        result.wait()


def here():
    members = lax.axis_size("ctx") // 2
    ctx = lax.axis_index("ctx")
    return ctx % members, ctx // members, lax.axis_index("groups"), lax.axis_index("chan")


def pick(half, near_ref, far_ref, picked_ref, genomes, rows):
    vocab = picked_ref.shape[1]
    length = picked_ref.shape[0] // genomes
    first = near_ref.shape[0] - SPARE
    diagonal = lax.broadcasted_iota(jnp.int32, (rows, rows), 0) == lax.broadcasted_iota(
        jnp.int32, (rows, rows), 1
    )
    entries = lax.broadcasted_iota(jnp.int32, (rows, vocab), 1).astype(f32)
    for other, ref in enumerate((near_ref, far_ref)):
        parts = ref[first:, :rows].astype(f32)
        for member in range(length // (2 * rows)):
            for b in range(genomes):
                at = 4 * member + 2 * b
                line = parts[at : at + 1] * 256.0 + parts[at + 1 : at + 2]
                column = jnp.sum(jnp.where(diagonal, line, 0.0), axis=1, keepdims=True)
                place = b * length + (half ^ other) * (length // 2) + member * rows
                picked_ref[pl.ds(pl.multiple_of(place, rows), rows), :] = (
                    (column == entries).astype(f32).astype(bf16)
                )


def prepare_kernel(rate_ref, amp_ref, taps_ref, skip_ref, matrices_ref, rows_ref):
    quad, half, _, _ = here()

    group_count = rate_ref.shape[1]
    poles = rate_ref.shape[0]
    count = LANES // poles

    def group_at(lane):
        place = lane // poles
        return quad * (2 * count) + (place // (count // 2)) * count + half * (count // 2) + place % (count // 2)

    lane = lax.broadcasted_iota(jnp.int32, (group_count, LANES), 1)
    chosen = (lax.broadcasted_iota(jnp.int32, (group_count, LANES), 0) == group_at(lane)).astype(f32)
    turned_lane = lax.broadcasted_iota(jnp.int32, (LANES, group_count), 0)
    turned = (lax.broadcasted_iota(jnp.int32, (LANES, group_count), 1) == group_at(turned_lane)).astype(f32)

    def along_lanes(ref):
        spread = jnp.dot(ref[...], chosen, precision=highest, preferred_element_type=f32)
        keep = lax.broadcasted_iota(jnp.int32, spread.shape, 0) == lax.broadcasted_iota(
            jnp.int32, spread.shape, 1
        ) % poles
        return jnp.sum(jnp.where(keep, spread, 0.0), axis=0, keepdims=True)

    rate, amp = along_lanes(rate_ref), along_lanes(amp_ref)
    spread = lax.dot_general(
        turned, rate_ref[...], (((1,), (1,)), ((), ())), precision=highest, preferred_element_type=f32
    )
    keep = lax.broadcasted_iota(jnp.int32, spread.shape, 1) == lax.broadcasted_iota(
        jnp.int32, spread.shape, 0
    ) % poles
    rate_col = jnp.sum(jnp.where(keep, spread, 0.0), axis=1, keepdims=True)

    square = (CHUNK, LANES)
    row = lax.broadcasted_iota(jnp.int32, square, 0)
    col = lax.broadcasted_iota(jnp.int32, square, 1)
    at = row.astype(f32)
    middle = float(CHUNK // 2)
    rising = amp * jnp.exp(-rate * (at - middle))
    falling = jnp.exp(-rate * (middle - at))
    width = (count + 1) * CHUNK
    for g in range(count):
        own = jnp.where(col // poles == g, falling, 0.0)
        block = lax.dot_general(
            rising, own, (((1,), (1,)), ((), ())), precision=highest, preferred_element_type=f32
        )
        high, low = split(jnp.where(row >= col, block, 0.0))
        matrices_ref[:, g * CHUNK : (g + 1) * CHUNK] = high
        matrices_ref[:, width + g * CHUNK : width + (g + 1) * CHUNK] = low
    high, low = split(amp * jnp.exp(-rate * (at + 1.0)))
    matrices_ref[:, count * CHUNK : width] = high
    matrices_ref[:, width + count * CHUNK : 2 * width] = low
    high, low = split(jnp.exp(-rate_col * (float(CHUNK - 1) - col.astype(f32))))
    matrices_ref[:, 2 * width : 2 * width + CHUNK] = high
    matrices_ref[:, 2 * width + CHUNK :] = low

    rows_ref[:LANES] = jnp.exp(-rate_col * float(CHUNK)) + jnp.zeros(square, f32)
    branches = taps_ref.shape[0]
    for j in range(branches):
        taps = jnp.dot(taps_ref[j], chosen, precision=highest, preferred_element_type=f32)
        rows_ref[LANES + 8 * j : LANES + 8 * j + taps.shape[0]] = taps
    upper = skip_ref[pl.ds(2 * quad, 1), :]
    lower = skip_ref[pl.ds(2 * quad + 1, 1), :]
    upper = jnp.where(half == 0, upper, half_turn(upper))
    lower = jnp.where(half == 1, lower, half_turn(lower))
    end = LANES + 8 * branches
    rows_ref[end : end + 1] = jnp.where(lane_half(upper.shape), upper, lower)


def partial_kernel(normed_ref, *refs, begin, count):
    weight_refs, (keep_ref, send_ref) = refs[:-2], refs[-2:]
    quad, half, _, _ = here()
    rows, features = normed_ref.shape
    depth = features // len(weight_refs)
    total = jnp.zeros((rows, count * LANES), f32)
    tokens = jnp.zeros((SPARE, LANES), f32)
    for m, weight_ref in enumerate(weight_refs):
        first = pl.multiple_of((quad ^ m) * depth, depth)
        columns = jnp.concatenate(
            [weight_ref[j * depth : (j + 1) * depth, :] for j in range(begin, begin + count)], axis=1
        )
        total += jnp.dot(
            normed_ref[:, pl.ds(first, depth)], columns, preferred_element_type=f32
        )
        tokens += weight_ref[weight_ref.shape[0] - SPARE :, :].astype(f32)
    part = rows // 2
    for j in range(count):
        mine = total[:, j * LANES : (j + 1) * LANES]
        mine = jnp.where(half == 0, mine, half_turn(mine))
        top, bottom = mine[:part], mine[part:]
        left = lane_half(top.shape)
        keep_ref[j * part : (j + 1) * part, :] = jnp.where(left, top, half_turn(bottom))
        send_ref[j * part : (j + 1) * part, :] = jnp.where(left, half_turn(top), bottom).astype(bf16)
    if send_ref.shape[0] > count * part:
        send_ref[count * part :, :] = tokens.astype(bf16)


def filtered_branch(group, picked, row, mine, theirs, rows_ref, branch):
    mine, theirs = mine.astype(f32), theirs.astype(f32)
    first = jnp.where(group == 0, mine, theirs)
    second = jnp.where(group == 0, theirs, mine)
    left = lane_half(first.shape)
    top = jnp.where(left, first, half_turn(second))
    bottom = jnp.where(left, half_turn(first), second)
    table = jnp.concatenate([top, bottom], axis=0).astype(bf16)
    now = jnp.dot(picked, table, preferred_element_type=f32)
    first_tap = LANES + 8 * branch
    total = rows_ref[first_tap : first_tap + 1] * now
    for lag in range(1, 3):
        late = jnp.where(row >= lag, pltpu.roll(now, lag, 0), 0.0)
        total += rows_ref[first_tap + lag : first_tap + lag + 1] * late
    return total


def conv_kernel(
    near_ref, far_ref, own_ref, other_ref, matrices_ref, rows_ref, value_ref, picked_ref, *, genomes, rows
):
    _, half, group, _ = here()
    pick(half, near_ref, far_ref, picked_ref, genomes, rows)
    positions = picked_ref.shape[0]
    length = positions // genomes
    row = lax.broadcasted_iota(jnp.int32, (positions, LANES), 0) % length
    picked = picked_ref[...]
    key, value = (
        filtered_branch(group, picked, row, own_ref[j - 1], other_ref[j - 1], rows_ref, j)
        for j in (1, 2)
    )
    product = key * value
    size = 16
    count = LANES // size
    width = genomes * LANES
    lane = lax.broadcasted_iota(jnp.int32, (CHUNK, width), 1) % LANES
    pole_row = lax.broadcasted_iota(jnp.int32, (LANES, width), 0)
    same = pole_row // size == (lax.broadcasted_iota(jnp.int32, (LANES, width), 1) % LANES) // size
    fade = jnp.concatenate([rows_ref[:LANES]] * genomes, axis=1)
    skip = rows_ref[rows_ref.shape[0] - 8 : rows_ref.shape[0] - 7]
    across = (count + 1) * CHUNK
    high, low = matrices_ref[:, :across], matrices_ref[:, across : 2 * across]
    ends_high = matrices_ref[:, 2 * across : 2 * across + CHUNK]
    ends_low = matrices_ref[:, 2 * across + CHUNK :]
    state = jnp.zeros((LANES, width), f32)
    chunks = length // CHUNK
    for c in range(chunks):
        spans = [slice(b * length + c * CHUNK, b * length + (c + 1) * CHUNK) for b in range(genomes)]
        block = jnp.concatenate([product[span] for span in spans], axis=1)
        stacked = jnp.concatenate(
            [jnp.where(lane // size == g, block, 0.0) for g in range(count)] + [state], axis=0
        )
        conv = dot3(high, low, stacked)
        for b, span in enumerate(spans):
            value_ref[span, :] = conv[:, b * LANES : (b + 1) * LANES] + skip * product[span]
        if c < chunks - 1:
            ends = dot3(ends_high, ends_low, block)
            state = fade * state + jnp.where(same, ends, 0.0)


def gate_kernel(picked_ref, own_ref, other_ref, rows_ref, value_ref, *refs, genomes):
    piece_refs, (mine_ref, held_ref) = refs[:4], refs[4:]
    _, half, group, core = here()
    positions = picked_ref.shape[0]
    length = positions // genomes
    row = lax.broadcasted_iota(jnp.int32, (positions, LANES), 0) % length
    query = filtered_branch(group, picked_ref[...], row, own_ref[0], other_ref[0], rows_ref, 0)
    held_ref[...] = (query * value_ref[...]).astype(bf16)
    part = length // 2
    for r, piece_ref in enumerate(piece_refs):
        place = 2 * (core ^ (r % 2)) + (half ^ (r // 2))
        piece_ref[...] = held_ref[pl.ds(pl.multiple_of(place * part, part), part), :]
    mine_ref[...] = picked_ref[pl.ds(pl.multiple_of((2 * core + half) * part, part), part), :]


def offer_kernel(place_ref, rows_ref, packed_ref, first_ref, second_ref):
    del place_ref, packed_ref
    count = first_ref.shape[0]
    first_ref[...] = rows_ref[:count]
    second_ref[...] = rows_ref[count:]


def residual(picked_ref, table_ref, first, width):
    return jnp.dot(
        picked_ref[...],
        table_ref[:, pl.ds(pl.multiple_of(first, width), width)],
        preferred_element_type=f32,
    )


def near_kernel(picked_ref, table_ref, *refs):
    piece_refs, refs = refs[:4], refs[4:]
    own_ref, core_ref, fetched_ref, core_fetched_ref, out_ref, part_ref, joined_ref = refs
    quad, half, group, _ = here()
    block = 2 * LANES
    for m, piece_ref in enumerate(piece_refs):
        for other_core in (0, 1):
            near = piece_ref[other_core].astype(f32)
            far = piece_ref[2 + other_core].astype(f32)
            first = jnp.where(half == 0, near, far)
            second = jnp.where(half == 0, far, near)
            left = lane_half(first.shape)
            pair = [
                jnp.where(left, first, half_turn(second)),
                jnp.where(left, half_turn(first), second),
            ]
            joined_ref[2 * (quad ^ m) + other_core] = jnp.concatenate(pair, axis=1).astype(bf16)
    width = own_ref.shape[1]
    total = jnp.zeros(out_ref.shape, f32)
    for member in range(4):
        rows = slice(member * block, (member + 1) * block)
        for other_core, ref in enumerate((own_ref, core_ref)):
            total += jnp.dot(
                joined_ref[2 * member + other_core], ref[rows, :], preferred_element_type=f32
            )
    total += residual(picked_ref, table_ref, (4 * half + quad) * width, width)
    out_ref[...] = total.astype(bf16)
    part = residual(picked_ref, table_ref, (4 * (half ^ 1) + (quad ^ 2)) * width, width)
    for i in (0, 1):
        rows = slice(i * block, (i + 1) * block)
        for other_core, ref in enumerate((fetched_ref, core_fetched_ref)):
            part += jnp.dot(
                joined_ref[2 * (2 * group + i) + other_core],
                ref[rows, :],
                preferred_element_type=f32,
            )
    part_ref[...] = part


def far_kernel(near_ref, part_ref, joined_ref, shared_ref, core_shared_ref, kept_ref, sent_ref):
    _, half, group, core = here()
    block = 2 * LANES
    total = part_ref[...]
    for i in (0, 1):
        rows = slice(i * block, (i + 1) * block)
        for other_core, ref in enumerate((shared_ref, core_shared_ref)):
            total += jnp.dot(
                joined_ref[2 * (2 * (group ^ 1) + i) + other_core],
                ref[rows, :],
                preferred_element_type=f32,
            )
    near, far = near_ref[...], total.astype(bf16)
    kept_ref[...] = jnp.where(half == core, near, far)
    sent_ref[...] = jnp.where(half == core, far, near)


def place_kernel(*refs):
    part_refs, out_ref = refs[:8], refs[8]
    quad, half, _, core = here()
    width = part_refs[0].shape[1]
    for g in (0, 1):
        for m in range(4):
            first = pl.multiple_of((quad ^ m ^ (2 * (half ^ core))) * width, width)
            out_ref[core ^ g, :, pl.ds(first, width)] = part_refs[4 * g + m][...]


def called(kernel, out_shape, scalars, *operands, scratch=(), mib=16, earlier=()):
    smem = pl.BlockSpec(memory_space=pltpu.SMEM)
    vmem = pl.BlockSpec(memory_space=pltpu.VMEM)
    anywhere = pl.BlockSpec(memory_space=pl.ANY)
    many = isinstance(out_shape, (list, tuple))
    inputs, waits = len(scalars) + len(operands), len(earlier)

    def body(*refs):
        kernel(*refs[:inputs], *refs[inputs + waits :])

    return pl.pallas_call(
        body,
        out_shape=out_shape,
        in_specs=[smem] * len(scalars) + [vmem] * len(operands) + [anywhere] * waits,
        out_specs=[vmem] * len(out_shape) if many else vmem,
        scratch_shapes=scratch,
        compiler_params=pltpu.CompilerParams(vmem_limit_bytes=mib * MIB),
    )(*scalars, *operands, *earlier)


def shaped(*shape, dtype=f32):
    return jax.ShapeDtypeStruct(shape, dtype)


def pass_kernel(*refs):
    del refs


def after(value, earlier):
    return pl.pallas_call(
        pass_kernel,
        out_shape=shaped(*value.shape, dtype=value.dtype),
        in_specs=[pl.BlockSpec(memory_space=pl.ANY)] * 2,
        out_specs=pl.BlockSpec(memory_space=pl.ANY),
        input_output_aliases={0: 0},
        compiler_params=pltpu.CompilerParams(vmem_limit_bytes=MIB),
    )(value, earlier)


def quad_body(
    tokens,
    embed_table,
    norm_gain,
    input_proj,
    short_filter,
    pole_rate,
    residue,
    skip_gain,
    output_proj,
):
    genomes, rows = tokens.shape
    depth, branches, channels = input_proj.shape
    vocab, features = embed_table.shape
    members = lax.axis_size("ctx") // 2
    ctx, core, group = (lax.axis_index(name) for name in ("ctx", "chan", "groups"))
    quad, half = ctx % members, ctx // members
    place = jnp.stack([quad, half, group, core]).astype(jnp.int32)
    block = channels // members

    weights = input_proj.transpose(1, 0, 2)
    anywhere = pl.BlockSpec(memory_space=pl.ANY)
    packed = pl.pallas_call(
        pack_kernel,
        out_shape=[shaped(branches * depth + SPARE, LANES, dtype=bf16)] * members,
        in_specs=[anywhere, anywhere],
        out_specs=[anywhere] * members,
        scratch_shapes=[
            pltpu.VMEM((members, branches * depth + SPARE, LANES), bf16),
            pltpu.VMEM((genomes, rows), jnp.int32),
            pltpu.SemaphoreType.DMA,
            pltpu.SemaphoreType.DMA((members, branches)),
            pltpu.SemaphoreType.DMA((members,)),
        ],
        compiler_params=pltpu.CompilerParams(vmem_limit_bytes=61 * MIB),
    )(tokens, weights)
    gathered = [packed[0]] + [swapped(packed[m], "ctx", m) for m in range(1, members)]
    length = 2 * members * rows

    half_rows = output_proj.shape[0] // 2
    width = output_proj.shape[1]
    offered = pl.pallas_call(
        offer_kernel,
        out_shape=[shaped(half_rows // 2, width, dtype=bf16)] * 2,
        grid_spec=pltpu.PrefetchScalarGridSpec(
            num_scalar_prefetch=1,
            grid=(1,),
            in_specs=[pl.BlockSpec((half_rows, width), lambda i, place: (place[2], 0)), anywhere],
            out_specs=[pl.BlockSpec((half_rows // 2, width), lambda i, place: (0, 0))] * 2,
        ),
        compiler_params=pltpu.CompilerParams(vmem_limit_bytes=4 * MIB),
    )(place, output_proj, packed[1])
    count = 2 * members
    inner = [(i, count - 2 - i + 2 * (i % 2)) for i in range(members // 2, members + members // 2)]
    outer = [
        (i, count - 2 - i + 2 * (i % 2))
        for i in range(count)
        if not members // 2 <= i < members + members // 2
    ]

    part = features // 2
    step = 256
    normed = pl.pallas_call(
        norm_kernel,
        out_shape=shaped(vocab, part, dtype=bf16),
        grid_spec=pltpu.PrefetchScalarGridSpec(
            num_scalar_prefetch=1,
            grid=(vocab // step,),
            in_specs=[
                pl.BlockSpec((step, features), lambda i, place: (i, 0)),
                pl.BlockSpec((1, part), lambda i, place: (0, place[1])),
                pl.BlockSpec((step, part), lambda i, place: (i, place[1])),
                anywhere,
                anywhere,
            ],
            out_specs=pl.BlockSpec((step, part), lambda i, place: (i, 0)),
        ),
        compiler_params=pltpu.CompilerParams(vmem_limit_bytes=16 * MIB),
    )(place, embed_table, norm_gain.reshape(1, features), embed_table, gathered[2], packed[1])

    inner_fetched = [lax.ppermute(rows_part, "ctx", inner) for rows_part in offered]
    def partials(begin, count, spare, earlier=()):
        table_rows = count * (vocab // 2)
        return called(
            functools.partial(partial_kernel, begin=begin, count=count),
            [shaped(table_rows, LANES), shaped(table_rows + spare, LANES, dtype=bf16)],
            (),
            normed,
            *gathered,
            earlier=earlier,
        )

    def finished(keep, arrived):
        own = (keep + arrived[: keep.shape[0]].astype(f32)).astype(bf16)
        return own.reshape(-1, vocab // 2, LANES)

    pair_keep, pair_send = partials(0, 2, SPARE)
    query_keep, query_send = partials(2, 1, 0)
    pair_arrived = swapped(pair_send, "ctx", members)
    query_arrived = swapped(query_send, "ctx", members)
    amp = residue * jnp.sqrt(-jnp.expm1(-2.0 * pole_rate))
    across = (LANES // pole_rate.shape[1] + 1) * CHUNK
    matrices, lines = called(
        prepare_kernel,
        [
            shaped(CHUNK, 2 * across + 2 * CHUNK, dtype=bf16),
            shaped(LANES + 8 * (branches + 1), LANES),
        ],
        (),
        pole_rate.T,
        amp.T,
        short_filter.transpose(0, 2, 1),
        skip_gain.reshape(-1, LANES),
        earlier=(pair_send, *inner_fetched),
    )

    pair_own = after(finished(pair_keep, pair_arrived), matrices)
    query_own = finished(query_keep, query_arrived)
    pair_other = swapped(pair_own, "groups", 1)
    query_other = swapped(query_own, "groups", 1)

    span = length // 2
    value, picked = called(
        functools.partial(conv_kernel, genomes=genomes, rows=rows),
        [shaped(genomes * length, LANES), shaped(genomes * length, vocab, dtype=bf16)],
        (),
        pair_send,
        pair_arrived,
        pair_own,
        pair_other,
        matrices,
        lines,
    )
    *pieces, picked = called(
        functools.partial(gate_kernel, genomes=genomes),
        [shaped(span, LANES, dtype=bf16)] * 4 + [shaped(span, vocab, dtype=bf16)],
        (),
        picked,
        query_own,
        query_other,
        lines,
        value,
        scratch=[pltpu.VMEM((genomes * length, LANES), bf16)],
    )
    core_piece = swapped(pieces[1], "chan", 1)
    piece = jnp.stack(
        [
            pieces[0],
            core_piece,
            swapped(pieces[2], "ctx", members),
            swapped_both(pieces[3], members),
        ]
    )
    gated = [piece] + [swapped(piece, "ctx", m) for m in range(1, members)]

    outer_fetched = [lax.ppermute(after(rows_part, pair_own), "ctx", outer) for rows_part in offered]
    fetched = jnp.where(
        (ctx >= members // 2) & (ctx < members + members // 2),
        jnp.concatenate(inner_fetched),
        jnp.concatenate(outer_fetched),
    )
    fetched = after(fetched, piece)
    shared = swapped(fetched, "groups", 1)
    for ready in gated[1:]:
        shared = after(shared, ready)
    near, part_far, joined = called(
        near_kernel,
        [
            shaped(span, width, dtype=bf16),
            shaped(span, width),
            shaped(4 * 2, span, 2 * LANES, dtype=bf16),
        ],
        (),
        picked,
        embed_table,
        *gated,
        output_proj,
        swapped(output_proj, "chan", 1),
        fetched,
        swapped(fetched, "chan", 1),
        mib=24,
    )
    results = called(
        far_kernel,
        [shaped(span, width, dtype=bf16)] * 2,
        (),
        near,
        part_far,
        joined,
        shared,
        swapped(shared, "chan", 1),
        mib=24,
    )
    kept, sent = results
    received = swapped(sent, "chan", 1)

    def rows_of(array, member):
        return lax.dynamic_slice_in_dim(array, member * rows, rows, 0)

    kept_parts = [rows_of(kept, quad)] + [
        swapped(rows_of(kept, quad ^ m), "ctx", m) for m in range(1, members)
    ]
    received_parts = [rows_of(received, quad)] + [
        swapped(rows_of(received, quad ^ m), "ctx", m) for m in range(1, members)
    ]
    return called(
        place_kernel,
        shaped(genomes, rows, members * width, dtype=bf16),
        (),
        *kept_parts,
        *received_parts,
    )


def solution(mesh):
    sizes = tuple(mesh.shape[name] for name in ("groups", "ctx", "chan"))
    return jax.shard_map(
        quad_body if sizes == (2, 8, 2) else general_body,
        mesh=mesh,
        in_specs=(
            P("groups", "ctx"),
            P(),
            P(),
            P("ctx", None, "chan"),
            P(None, "chan", None),
            P("chan", None),
            P("chan", None),
            P("chan"),
            P("chan", "ctx"),
        ),
        out_specs=P("groups", "ctx", "chan"),
        check_vma=False,
    )
```
